32 devices in a mesh: col: 8 (over z, y), row: 4 (over x, core).
Axes of the slice: x: 2, y: 2, z: 4, core: 2. Of those that a mesh axis runs over, the one named last changes fastest.
Arguments:
- pivot_block: bfloat16 [512, 512], P(None, 'row'), may hold values from -0.5 to 5.5, as said below
- panel: bfloat16 [4, 256, 512], P('row', 'col'), may hold values from -1.1953125 to 1.1953125
- lead: int32 [4, 2], P('row'), may hold values from 0 to 3
- trailing: bfloat16 [1024, 1024], P('row', 'col'), may hold values from -1.796875 to 1.796875
Outputs:
- pivot_factor: float32 [512, 512], P(None, 'row')
- panel_factor: bfloat16 [4, 256, 512], P('row', 'col')
- schur: bfloat16 [1024, 1024], P('row', 'col')
The draws below stay inside these ranges and needn't reach their ends.
Inputs may be any that keep to these rules, and one draw needn't show every extreme that they name: `pivot_block`: symmetric positive definite.
All inputs are finite; a program needn't handle non-finite values.
Results may differ from the reference program's by a relative error of at most 0.0042.
Values may be sent and summed in bfloat16 or wider, within the bound.
No kernel may reach another device: no remote copies, remote signals or barrier semaphores. Data moves between devices by JAX's collectives and lax.ppermute only.
A program may use at most 64 MiB of HBM per device.

```python
import math
import jax
import jax.numpy as jnp
from jax import lax

PIVOT = 512
BLOCK = 128
KB = 4
GROUPS = 4
GROUP_ROWS = 256
GROUP_BLOCKS = 2
TRAIL = 1024


def draw_pivot_block(key, part):
    first_key, second_key, third_key = jax.random.split(jax.random.fold_in(key, 11), 3)
    position = jnp.arange(PIVOT).astype(jnp.float32)
    distance = jnp.abs(position[:, None] - position[None, :])
    length_scale = PIVOT / 16.0
    kernel = jnp.exp(-distance / length_scale)
    scales = jnp.exp(jax.random.uniform(first_key, (PIVOT,), jnp.float32, math.log(0.75), math.log(1.25)))
    jitter = jax.random.normal(second_key, (PIVOT, PIVOT), jnp.float32) * 0.02
    symmetric = jnp.clip((jitter + jitter.T) * 0.5, -0.06, 0.06)
    diagonal = jax.random.uniform(third_key, (PIVOT,), jnp.float32, 2.0, 3.0)
    correlated = 1.5 * kernel * scales[:, None] * scales[None, :]
    return (correlated + symmetric + jnp.eye(PIVOT, dtype=jnp.float32) * diagonal[None, :]).astype(jnp.bfloat16)


def draw_lead(key, part):
    first_key, second_key = jax.random.split(jax.random.fold_in(key, 23))
    earliest = jax.random.randint(first_key, (GROUPS, 1), 0, KB // 2)
    return jax.random.randint(second_key, (GROUPS, GROUP_BLOCKS), earliest, KB).astype(jnp.int32)


def steps_of(stream_key, dims, shards, least, high):
    def one(dim, shards_of):
        steps = jax.random.uniform(jax.random.fold_in(jax.random.fold_in(stream_key, 6), dim), (shards_of,), jnp.float32, least / len(shards), high / len(shards))
        return jnp.repeat(jnp.exp(steps), dims[dim] // shards_of).reshape((-1,) + (1,) * (len(dims) - dim - 1))

    gain = one(*shards[0])
    for cut in shards[1:]:
        gain = gain * one(*cut)
    return gain


def gaussian(stream_key, shape, width, reach, pieces=(), kind=jnp.bfloat16):
    entries = jax.random.normal(stream_key, shape, jnp.float32) * width
    if len(pieces) > 0:
        entries = steps_of(stream_key, shape, pieces, -0.22, 0.18) * entries
    return jnp.clip(entries, min=-reach, max=reach).astype(kind)


def setup_inputs(seed: int = 0) -> dict:
    seeds = jax.random.split(jax.random.key(seed), 5)
    pivot_block = draw_pivot_block(jax.random.fold_in(seeds[4], 71), 0)
    panel = gaussian(seeds[1], (GROUPS, GROUP_ROWS, PIVOT), 0.2, 1.1953125, ((0, 4), (1, 8)))
    lead = draw_lead(jax.random.fold_in(seeds[4], 71), 0)
    trailing = gaussian(seeds[3], (TRAIL, TRAIL), 0.3, 1.796875, ((0, 4), (1, 8)))
    return dict(pivot_block=pivot_block, panel=panel, lead=lead, trailing=trailing)


def reference(pivot_block, panel, lead, trailing):
    pivot_factor = jnp.linalg.cholesky(pivot_block.astype(jnp.float32))
    col_block = (jnp.arange(PIVOT) // BLOCK).astype(jnp.int32)
    row_lead = jnp.repeat(lead, BLOCK, axis=1)
    live_mask = col_block[None, None, :] >= row_lead[:, :, None]
    masked = jnp.where(live_mask, panel.astype(jnp.float32), jnp.float32(0.0)).reshape(TRAIL, PIVOT)
    solved = jax.scipy.linalg.solve_triangular(pivot_factor, masked.T, lower=True).T
    panel_factor = solved.astype(jnp.bfloat16)
    panel_wide = panel_factor.astype(jnp.float32)

    def one_group(group_index):
        first = (group_index * GROUP_ROWS).astype(jnp.int32)
        group_rows = lax.dynamic_slice_in_dim(panel_wide, first, GROUP_ROWS, 0)
        target_rows = lax.dynamic_slice_in_dim(trailing, first, GROUP_ROWS, 0)
        update = jnp.dot(group_rows, panel_wide.T, precision=lax.Precision.HIGHEST)
        return (target_rows.astype(jnp.float32) - update).astype(jnp.bfloat16)
    schur = lax.map(one_group, jnp.arange(GROUPS).astype(jnp.int32)).reshape(TRAIL, TRAIL)
    return (pivot_factor, panel_factor.reshape(GROUPS, GROUP_ROWS, PIVOT), schur)
```

```python
import functools

import jax
import jax.numpy as jnp
from jax import lax
from jax.experimental import pallas as pl
from jax.experimental.pallas import tpu as pltpu
from jax.sharding import PartitionSpec as P

BLOCK = 128
STRIP = 32
GROUP = 8
LANES = 128
DIRECT = 8


def split(value):
    high = value.astype(jnp.bfloat16)
    low = (value - high.astype(jnp.float32)).astype(jnp.bfloat16)
    return high, low


def row_of(value, row):
    return jnp.broadcast_to(value[row : row + 1, :], (GROUP, LANES))


def reciprocal(value):
    guess = pl.reciprocal(value, approx=True)
    return guess, 2.0 - value * guess


def eliminate_strip(diagonal, first, rest):
    groups = STRIP // GROUP
    sublane = lax.broadcasted_iota(jnp.int32, (GROUP, LANES), 0)
    lane = lax.broadcasted_iota(jnp.int32, (GROUP, LANES), 1)
    zero = jnp.zeros((GROUP, LANES), jnp.float32)
    diag = [diagonal[g * GROUP : (g + 1) * GROUP, :] for g in range(groups)]
    column = [
        [
            jnp.broadcast_to(diag[g][:, first + j : first + j + 1], (GROUP, LANES)) if g >= j // GROUP else None
            for g in range(groups)
        ]
        for j in range(STRIP)
    ]
    inside = (lane >= first) & (lane < first + STRIP)
    rows = [
        [jnp.where(inside, jnp.where(lane - first == sublane + g * GROUP, 1.0, 0.0), diag[g]) for g in range(groups)]
    ] + [[block[g * GROUP : (g + 1) * GROUP, :] for g in range(groups)] for block in rest]
    lower = [zero] * groups
    for k in range(0, STRIP, 2):
        home, sub = k // GROUP, k % GROUP
        u, v = column[k], column[k + 1]
        a = row_of(u[home], sub)
        b = row_of(u[home], sub + 1)
        c = row_of(v[home], sub + 1)
        det = a * c - b * b
        guess, correction = reciprocal(det)
        n1 = [None if g < home else c * u[g] - b * v[g] for g in range(groups)]
        n2 = [None if g < home else a * v[g] - b * u[g] for g in range(groups)]
        w1 = [None if g < home else (n1[g] * guess) * correction for g in range(groups)]
        w2 = [None if g < home else (n2[g] * guess) * correction for g in range(groups)]
        for j in range(k + 2, STRIP):
            at, row = j // GROUP, j % GROUP
            uj, vj = row_of(u[at], row), row_of(v[at], row)
            for g in range(at, groups):
                if j < k + 4:
                    step = ((n1[g] * uj + n2[g] * vj) * guess) * correction
                else:
                    step = w1[g] * uj + w2[g] * vj
                column[j][g] = column[j][g] - step
        root_a = lax.rsqrt(a)
        root_d = lax.rsqrt(a * det)
        for g in range(home, groups):
            lower[g] = jnp.where(lane == first + k, u[g] * root_a, lower[g])
            lower[g] = jnp.where(lane == first + k + 1, n2[g] * root_d, lower[g])
        below = sublane > sub + 1
        w1[home] = jnp.where(below, w1[home], 0.0)
        w2[home] = jnp.where(below, w2[home], 0.0)
        for block in rows:
            t0, t1 = row_of(block[home], sub), row_of(block[home], sub + 1)
            for g in range(home, groups):
                block[g] = block[g] - (w1[g] * t0 + w2[g] * t1)
            block[home] = jnp.where(sublane == sub, t0 * root_a, block[home])
            block[home] = jnp.where(sublane == sub + 1, (a * t1 - b * t0) * root_d, block[home])
    for g in range(groups):
        keep = (lane <= first + sublane + g * GROUP) & inside
        lower[g] = jnp.where(keep, lower[g], 0.0)
    return [jnp.concatenate(block, axis=0) for block in rows], jnp.concatenate(lower, axis=0)


def matmul(left, right):
    return jnp.dot(left, right, preferred_element_type=jnp.float32)


def factor_kernel(axis, *refs):
    count = lax.axis_size(axis)
    parts, (own_ref, high_ref, low_ref, work, lower) = refs[:count], refs[count:]
    me = lax.axis_index(axis)
    size = parts[0].shape[0]
    lane = lax.broadcasted_iota(jnp.int32, (LANES, LANES), 1)
    row = lax.broadcasted_iota(jnp.int32, (LANES, LANES), 0)
    for shift, part in enumerate(parts):
        work[lax.rem(me + shift, count)] = part[...].astype(jnp.float32)

    def block_step(q, carry):
        base = pl.multiple_of(q * LANES, LANES)
        places = [lax.rem(q + d, count) for d in range(count)]
        for first in range(0, LANES, STRIP):
            here = pl.ds(base + first, STRIP)
            strip = [work[place, here, :] for place in places]
            done, diagonal = eliminate_strip(strip[0], first, strip[1:])
            lower[q, pl.ds(first, STRIP), :] = diagonal
            for place, block in zip(places, done):
                work[place, here, :] = block
            left = LANES - first - STRIP
            if left == 0:
                break
            high, low = split(done[0])
            wide = jnp.concatenate([high, low, high, jnp.zeros_like(high)], axis=0).astype(jnp.float32)
            lhs = wide.T[first + STRIP :, :].astype(jnp.bfloat16)
            under = pl.ds(base + first + STRIP, left)
            for d, (place, block) in enumerate(zip(places, done)):
                high, low = split(block)
                rhs = jnp.concatenate([high, high, low, jnp.zeros_like(high)], axis=0)
                old = work[place, under, :]
                if d == 0:
                    at = lax.broadcasted_iota(jnp.int32, old.shape, 1)
                    old = jnp.where((at >= first) & (at < first + STRIP), 0.0, old)
                work[place, under, :] = old - matmul(lhs, rhs)

        here = pl.ds(base, LANES)

        def below(i, carry):
            high, low = split(work[i, here, :].T)
            lhs = jnp.concatenate([high, low], axis=1)
            under = pl.ds(pl.multiple_of(i * LANES, LANES), LANES)
            for d, place in enumerate(places):
                rhs = work[place, here, :]
                if d == 0:
                    rhs = jnp.where(lane // STRIP > row // STRIP, 0.0, rhs)
                rhs_high, rhs_low = split(rhs)
                product = matmul(lhs, jnp.concatenate([rhs_high, rhs_high], axis=0)) + matmul(high, rhs_low)
                if d == 0:
                    work[place, under, :] = -product
                else:
                    work[place, under, :] = work[place, under, :] - product
            return carry

        lax.fori_loop(q + 1, count, below, 0)
        return carry

    lax.fori_loop(0, count, block_step, 0)

    for i in range(count):
        here = pl.ds(pl.multiple_of(me * LANES, LANES), LANES)
        block = work[i, here, :]
        beyond = lane // STRIP > row // STRIP
        upper = jnp.where((i > me) | ((i == me) & beyond), block, 0.0)
        own_ref[i * LANES : (i + 1) * LANES, :] = upper.T + jnp.where(i == me, lower[i], 0.0)
        for c in range(count):
            block = work[c, i * LANES : (i + 1) * LANES, :]
            if c > i:
                block = jnp.zeros_like(block)
            elif c == i:
                block = jnp.where(lane <= row, block, 0.0)
            high, low = split(block)
            high_ref[i * LANES : (i + 1) * LANES, c * LANES : (c + 1) * LANES] = high
            low_ref[i * LANES : (i + 1) * LANES, c * LANES : (c + 1) * LANES] = low


def solve_kernel(row_axis, col_axis, pieces, sides, *refs):
    high_ref, low_ref = refs[:2]
    group_refs, side_refs = refs[2 : 2 + pieces], refs[2 + pieces : 2 + pieces + sides]
    trailing_ref, own_ref, schur_ref, group, side = refs[2 + pieces + sides :]
    my_row, my_col = lax.axis_index(row_axis), lax.axis_index(col_axis)
    size = high_ref.shape[0]
    half = size // 2
    share = own_ref.shape[1]
    for shift, ref in enumerate(group_refs):
        if pieces == 1:
            group[...] = ref[...]
        else:
            at = lax.rem(my_col + shift, pieces) * share
            group[pl.ds(pl.multiple_of(at, share), share), :] = ref[...]
    for shift, ref in enumerate(side_refs):
        at = lax.rem(my_row + sides - shift, sides) * share
        side[pl.ds(pl.multiple_of(at, share), share), :] = ref[...]
    contract = (((1,), (1,)), ((), ()))

    def product(left, right):
        return lax.dot_general(left, right, contract, preferred_element_type=jnp.float32)

    def solve(rows):
        first = product(rows[:, :half], high_ref[:half, :half]) + product(rows[:, :half], low_ref[:half, :half])
        second = product(rows, high_ref[half:, :]) + product(rows, low_ref[half:, :])
        return jnp.concatenate([first, second], axis=1).astype(jnp.bfloat16)

    side[...] = solve(side[...])
    rows = group.shape[0]
    chunk = min(rows, 256)

    def step(i, carry):
        here = pl.ds(pl.multiple_of(i * chunk, chunk), chunk)
        solved = solve(group[here, :])
        group[here, :] = solved
        update = product(solved, side[...])
        schur_ref[here, :] = (trailing_ref[here, :].astype(jnp.float32) - update).astype(jnp.bfloat16)
        return carry

    if rows == chunk:
        step(0, 0)
    else:
        lax.fori_loop(0, rows // chunk, step, 0)
    own_ref[0] = group[pl.ds(pl.multiple_of(my_col * share, share), share), :]


def body(pivot_block, panel, lead, trailing):
    pivot_size, local_width = pivot_block.shape
    rows, cols = lax.axis_size("row"), lax.axis_size("col")
    share = panel.shape[1]
    col_index = lax.axis_index("col")
    vmem = pl.BlockSpec(memory_space=pltpu.VMEM)

    pivots = [pivot_block] + [
        lax.ppermute(pivot_block, "row", [((d + s) % rows, d) for d in range(rows)]) for s in range(1, rows)
    ]

    block_of_row = (col_index * share + jnp.arange(share)) // BLOCK
    matches = block_of_row[:, None] == jnp.arange(lead.shape[1])[None, :]
    row_lead = jnp.sum(jnp.where(matches, lead, 0), axis=1)
    live = (jnp.arange(pivot_size) // BLOCK)[None, :] >= row_lead[:, None]
    masked = jnp.where(live, panel[0], jnp.zeros_like(panel[0]))

    if cols <= DIRECT:
        group = [masked] + [
            lax.ppermute(masked, "col", [((d + s) % cols, d) for d in range(cols)]) for s in range(1, cols)
        ]
    else:
        group = [lax.all_gather(masked, "col", axis=0, tiled=True)]
    ratio = cols // rows
    side = []
    for s in range(rows):
        pairs = []
        for r in range(rows):
            for c in range(cols):
                target = ((c % rows + s) % rows, r * ratio + c // rows)
                pairs.append((c * rows + r, target[1] * rows + target[0]))
        side.append(lax.ppermute(masked, ("col", "row"), pairs))

    own, high, low = pl.pallas_call(
        functools.partial(factor_kernel, "row"),
        out_shape=(
            jax.ShapeDtypeStruct((pivot_size, local_width), jnp.float32),
            jax.ShapeDtypeStruct((pivot_size, pivot_size), jnp.bfloat16),
            jax.ShapeDtypeStruct((pivot_size, pivot_size), jnp.bfloat16),
        ),
        in_specs=[vmem] * rows,
        out_specs=(vmem,) * 3,
        scratch_shapes=[
            pltpu.VMEM((rows, pivot_size, LANES), jnp.float32),
            pltpu.VMEM((rows, LANES, LANES), jnp.float32),
        ],
        compiler_params=pltpu.CompilerParams(vmem_limit_bytes=32 * 1024 * 1024),
        cost_estimate=pl.CostEstimate(flops=10**9, bytes_accessed=2 * 10**6, transcendentals=10**5),
        name="factor",
    )(*pivots)

    group_rows = share * cols
    panel_factor, schur = pl.pallas_call(
        functools.partial(solve_kernel, "row", "col", len(group), len(side)),
        out_shape=(
            jax.ShapeDtypeStruct(panel.shape, jnp.bfloat16),
            jax.ShapeDtypeStruct(trailing.shape, jnp.bfloat16),
        ),
        in_specs=[vmem] * (3 + len(group) + len(side)),
        out_specs=(vmem,) * 2,
        scratch_shapes=[
            pltpu.VMEM((group_rows, pivot_size), jnp.bfloat16),
            pltpu.VMEM((share * rows, pivot_size), jnp.bfloat16),
        ],
        compiler_params=pltpu.CompilerParams(vmem_limit_bytes=48 * 1024 * 1024),
        cost_estimate=pl.CostEstimate(flops=4 * 10**8, bytes_accessed=2 * 10**6, transcendentals=0),
        name="solve",
    )(high, low, *group, *side, trailing)
    return (own, panel_factor, schur)


def solution(mesh):
    return jax.shard_map(
        body,
        mesh=mesh,
        in_specs=(P(None, "row"), P("row", "col", None), P("row", None), P("row", "col")),
        out_specs=(P(None, "row"), P("row", "col", None), P("row", "col")),
        check_vma=False,
    )
```

```python
import functools

import jax
import jax.numpy as jnp
from jax import lax
from jax.experimental import pallas as pl
from jax.experimental.pallas import tpu as pltpu
from jax.sharding import PartitionSpec as P

BLOCK = 128
STRIP = 32
GROUP = 8
LANES = 128


def split(value):
    high = value.astype(jnp.bfloat16)
    low = (value - high.astype(jnp.float32)).astype(jnp.bfloat16)
    return high, low


def row_of(value, row):
    return jnp.broadcast_to(value[row : row + 1, :], (GROUP, LANES))


def reciprocal(value):
    guess = pl.reciprocal(value, approx=True)
    return guess, 2.0 - value * guess


def eliminate_strip(diagonal, first, rest):
    groups = STRIP // GROUP
    sublane = lax.broadcasted_iota(jnp.int32, (GROUP, LANES), 0)
    lane = lax.broadcasted_iota(jnp.int32, (GROUP, LANES), 1)
    zero = jnp.zeros((GROUP, LANES), jnp.float32)
    diag = [diagonal[g * GROUP : (g + 1) * GROUP, :] for g in range(groups)]
    column = [
        [
            jnp.broadcast_to(diag[g][:, first + j : first + j + 1], (GROUP, LANES)) if g >= j // GROUP else None
            for g in range(groups)
        ]
        for j in range(STRIP)
    ]
    inside = (lane >= first) & (lane < first + STRIP)
    rows = [
        [jnp.where(inside, jnp.where(lane - first == sublane + g * GROUP, 1.0, 0.0), diag[g]) for g in range(groups)]
    ] + [[block[g * GROUP : (g + 1) * GROUP, :] for g in range(groups)] for block in rest]
    lower = [zero] * groups
    for k in range(0, STRIP, 2):
        home, sub = k // GROUP, k % GROUP
        u, v = column[k], column[k + 1]
        a = row_of(u[home], sub)
        b = row_of(u[home], sub + 1)
        c = row_of(v[home], sub + 1)
        det = a * c - b * b
        guess, correction = reciprocal(det)
        n1 = [None if g < home else c * u[g] - b * v[g] for g in range(groups)]
        n2 = [None if g < home else a * v[g] - b * u[g] for g in range(groups)]
        w1 = [None if g < home else (n1[g] * guess) * correction for g in range(groups)]
        w2 = [None if g < home else (n2[g] * guess) * correction for g in range(groups)]
        for j in range(k + 2, STRIP):
            at, row = j // GROUP, j % GROUP
            uj, vj = row_of(u[at], row), row_of(v[at], row)
            for g in range(at, groups):
                if j < k + 4:
                    step = ((n1[g] * uj + n2[g] * vj) * guess) * correction
                else:
                    step = w1[g] * uj + w2[g] * vj
                column[j][g] = column[j][g] - step
        root_a = lax.rsqrt(a)
        root_d = lax.rsqrt(a * det)
        for g in range(home, groups):
            lower[g] = jnp.where(lane == first + k, u[g] * root_a, lower[g])
            lower[g] = jnp.where(lane == first + k + 1, n2[g] * root_d, lower[g])
        below = sublane > sub + 1
        w1[home] = jnp.where(below, w1[home], 0.0)
        w2[home] = jnp.where(below, w2[home], 0.0)
        for block in rows:
            t0, t1 = row_of(block[home], sub), row_of(block[home], sub + 1)
            for g in range(home, groups):
                block[g] = block[g] - (w1[g] * t0 + w2[g] * t1)
            block[home] = jnp.where(sublane == sub, t0 * root_a, block[home])
            block[home] = jnp.where(sublane == sub + 1, (a * t1 - b * t0) * root_d, block[home])
    for g in range(groups):
        keep = (lane <= first + sublane + g * GROUP) & inside
        lower[g] = jnp.where(keep, lower[g], 0.0)
    return [jnp.concatenate(block, axis=0) for block in rows], jnp.concatenate(lower, axis=0)


def matmul(left, right):
    return jnp.dot(left, right, preferred_element_type=jnp.float32)


def factor_kernel(axis, *refs):
    count = lax.axis_size(axis)
    parts, (own_ref, high_ref, low_ref, work, lower) = refs[:count], refs[count:]
    me = lax.axis_index(axis)
    size = parts[0].shape[0]
    lane = lax.broadcasted_iota(jnp.int32, (LANES, LANES), 1)
    row = lax.broadcasted_iota(jnp.int32, (LANES, LANES), 0)
    for shift, part in enumerate(parts):
        work[lax.rem(me + shift, count)] = part[...].astype(jnp.float32)

    def block_step(q, carry):
        base = pl.multiple_of(q * LANES, LANES)
        places = [lax.rem(q + d, count) for d in range(count)]
        for first in range(0, LANES, STRIP):
            here = pl.ds(base + first, STRIP)
            strip = [work[place, here, :] for place in places]
            done, diagonal = eliminate_strip(strip[0], first, strip[1:])
            lower[q, pl.ds(first, STRIP), :] = diagonal
            for place, block in zip(places, done):
                work[place, here, :] = block
            left = LANES - first - STRIP
            if left == 0:
                break
            high, low = split(done[0])
            wide = jnp.concatenate([high, low, high, jnp.zeros_like(high)], axis=0).astype(jnp.float32)
            lhs = wide.T[first + STRIP :, :].astype(jnp.bfloat16)
            under = pl.ds(base + first + STRIP, left)
            for d, (place, block) in enumerate(zip(places, done)):
                high, low = split(block)
                rhs = jnp.concatenate([high, high, low, jnp.zeros_like(high)], axis=0)
                old = work[place, under, :]
                if d == 0:
                    at = lax.broadcasted_iota(jnp.int32, old.shape, 1)
                    old = jnp.where((at >= first) & (at < first + STRIP), 0.0, old)
                work[place, under, :] = old - matmul(lhs, rhs)

        here = pl.ds(base, LANES)

        def below(i, carry):
            high, low = split(work[i, here, :].T)
            lhs = jnp.concatenate([high, low], axis=1)
            under = pl.ds(pl.multiple_of(i * LANES, LANES), LANES)
            for d, place in enumerate(places):
                rhs = work[place, here, :]
                if d == 0:
                    rhs = jnp.where(lane // STRIP > row // STRIP, 0.0, rhs)
                rhs_high, rhs_low = split(rhs)
                product = matmul(lhs, jnp.concatenate([rhs_high, rhs_high], axis=0)) + matmul(high, rhs_low)
                if d == 0:
                    work[place, under, :] = -product
                else:
                    work[place, under, :] = work[place, under, :] - product
            return carry

        lax.fori_loop(q + 1, count, below, 0)
        return carry

    lax.fori_loop(0, count, block_step, 0)

    for i in range(count):
        here = pl.ds(pl.multiple_of(me * LANES, LANES), LANES)
        block = work[i, here, :]
        beyond = lane // STRIP > row // STRIP
        upper = jnp.where((i > me) | ((i == me) & beyond), block, 0.0)
        own_ref[i * LANES : (i + 1) * LANES, :] = upper.T + jnp.where(i == me, lower[i], 0.0)
        for c in range(count):
            block = work[c, i * LANES : (i + 1) * LANES, :]
            if c > i:
                block = jnp.zeros_like(block)
            elif c == i:
                block = jnp.where(lane <= row, block, 0.0)
            high, low = split(block)
            high_ref[i * LANES : (i + 1) * LANES, c * LANES : (c + 1) * LANES] = high
            low_ref[i * LANES : (i + 1) * LANES, c * LANES : (c + 1) * LANES] = low


def solve_kernel(row_axis, col_axis, order, group_count, *refs):
    high_ref, low_ref = refs[:2]
    inputs = refs[2 : 3 + group_count]
    trailing_ref, own_ref, schur_ref, group, side = refs[3 + group_count :]
    size = high_ref.shape[0]
    half = size // 2
    share = own_ref.shape[1]
    count = side.shape[0] // share
    my_row, my_col = lax.axis_index(row_axis), lax.axis_index(col_axis)
    for i, ref in enumerate(inputs[:-1]):
        if order is None:
            group[...] = ref[...]
        else:
            for p in range(count):
                at = jnp.bitwise_xor(my_col, i * count + p) * share
                group[pl.ds(pl.multiple_of(at, share), share), :] = ref[p * share : (p + 1) * share, :]
    for p in range(count):
        place = jnp.bitwise_xor(my_row, p) if order else lax.rem(my_row + count - p, count)
        side[pl.ds(pl.multiple_of(place * share, share), share), :] = inputs[-1][p * share : (p + 1) * share, :]
    contract = (((1,), (1,)), ((), ()))

    def product(left, right):
        return lax.dot_general(left, right, contract, preferred_element_type=jnp.float32)

    def solve(rows):
        first = product(rows[:, :half], high_ref[:half, :half]) + product(rows[:, :half], low_ref[:half, :half])
        second = product(rows, high_ref[half:, :]) + product(rows, low_ref[half:, :])
        return jnp.concatenate([first, second], axis=1).astype(jnp.bfloat16)

    side[...] = solve(side[...])
    rows = group.shape[0]
    chunk = min(rows, 256)

    def step(i, carry):
        here = pl.ds(pl.multiple_of(i * chunk, chunk), chunk)
        solved = solve(group[here, :])
        group[here, :] = solved
        update = product(solved, side[...])
        schur_ref[here, :] = (trailing_ref[here, :].astype(jnp.float32) - update).astype(jnp.bfloat16)
        return carry

    if rows == chunk:
        step(0, 0)
    else:
        lax.fori_loop(0, rows // chunk, step, 0)
    own_ref[0] = group[pl.ds(pl.multiple_of(my_col * share, share), share), :]


def body(pivot_block, panel, lead, trailing):
    pivot_size, local_width = pivot_block.shape
    rows, cols = lax.axis_size("row"), lax.axis_size("col")
    share = panel.shape[1]
    col_index = lax.axis_index("col")
    vmem = pl.BlockSpec(memory_space=pltpu.VMEM)

    pivots = [pivot_block] + [
        lax.ppermute(pivot_block, "row", [((d + s) % rows, d) for d in range(rows)]) for s in range(1, rows)
    ]

    def live(shards, rows_of):
        block = jnp.concatenate([(shard * share + jnp.arange(share)) // BLOCK for shard in shards])
        matches = block[:, None] == jnp.arange(lead.shape[1])[None, :]
        row_lead = jnp.sum(jnp.where(matches, lead, 0), axis=1)
        keep = (jnp.arange(pivot_size) // BLOCK)[None, :] >= row_lead[:, None]
        return jnp.where(keep, rows_of, jnp.zeros_like(rows_of))

    ratio = cols // rows
    paired = cols == 2 * rows and rows & (rows - 1) == 0

    def to_side(array, shift):
        pairs = []
        for r in range(rows):
            for c in range(cols):
                to_row, to_col = (c % rows + shift) % rows, r * ratio + c // rows
                pairs.append((c * rows + r, to_col * rows + to_row))
        return lax.ppermute(array, ("col", "row"), pairs)

    if paired:
        quad = [panel[0]] + [lax.ppermute(panel[0], "col", [(d ^ p, d) for d in range(cols)]) for p in range(1, rows)]
        quad = live([col_index ^ p for p in range(rows)], jnp.concatenate(quad, axis=0))
        group = [quad, lax.ppermute(quad, "col", [(d ^ rows, d) for d in range(cols)])]
        side = to_side(quad, 0)
    else:
        masked = live([col_index], panel[0])
        group = [lax.all_gather(masked, "col", axis=0, tiled=True)]
        side = jnp.concatenate([to_side(masked, s) for s in range(rows)], axis=0)

    own, high, low = pl.pallas_call(
        functools.partial(factor_kernel, "row"),
        out_shape=(
            jax.ShapeDtypeStruct((pivot_size, local_width), jnp.float32),
            jax.ShapeDtypeStruct((pivot_size, pivot_size), jnp.bfloat16),
            jax.ShapeDtypeStruct((pivot_size, pivot_size), jnp.bfloat16),
        ),
        in_specs=[vmem] * rows,
        out_specs=(vmem,) * 3,
        scratch_shapes=[
            pltpu.VMEM((rows, pivot_size, LANES), jnp.float32),
            pltpu.VMEM((rows, LANES, LANES), jnp.float32),
        ],
        compiler_params=pltpu.CompilerParams(vmem_limit_bytes=32 * 1024 * 1024),
        cost_estimate=pl.CostEstimate(flops=10**9, bytes_accessed=2 * 10**6, transcendentals=10**5),
        name="factor",
    )(*pivots)

    group_rows = share * cols
    panel_factor, schur = pl.pallas_call(
        functools.partial(solve_kernel, "row", "col", True if paired else None, len(group)),
        out_shape=(
            jax.ShapeDtypeStruct(panel.shape, jnp.bfloat16),
            jax.ShapeDtypeStruct(trailing.shape, jnp.bfloat16),
        ),
        in_specs=[vmem] * (4 + len(group)),
        out_specs=(vmem,) * 2,
        scratch_shapes=[
            pltpu.VMEM((group_rows, pivot_size), jnp.bfloat16),
            pltpu.VMEM((share * rows, pivot_size), jnp.bfloat16),
        ],
        compiler_params=pltpu.CompilerParams(vmem_limit_bytes=48 * 1024 * 1024),
        cost_estimate=pl.CostEstimate(flops=4 * 10**8, bytes_accessed=2 * 10**6, transcendentals=0),
        name="solve",
    )(high, low, *group, side, trailing)
    return (own, panel_factor, schur)


def solution(mesh):
    return jax.shard_map(
        body,
        mesh=mesh,
        in_specs=(P(None, "row"), P("row", "col", None), P("row", None), P("row", "col")),
        out_specs=(P(None, "row"), P("row", "col", None), P("row", "col")),
        check_vma=False,
    )
```

```python
import functools

import jax
import jax.numpy as jnp
from jax import lax
from jax.experimental import pallas as pl
from jax.experimental.pallas import tpu as pltpu
from jax.sharding import PartitionSpec as P

BLOCK = 128
STRIP = 32
GROUP = 8
LANES = 128


def split(value):
    high = value.astype(jnp.bfloat16)
    low = (value - high.astype(jnp.float32)).astype(jnp.bfloat16)
    return high, low


def row_of(value, row):
    return jnp.broadcast_to(value[row : row + 1, :], (GROUP, LANES))


def reciprocal(value):
    guess = pl.reciprocal(value, approx=True)
    return guess, 2.0 - value * guess


def eliminate_strip(strip, first):
    groups = STRIP // GROUP
    sublane = lax.broadcasted_iota(jnp.int32, (GROUP, LANES), 0)
    lane = lax.broadcasted_iota(jnp.int32, (GROUP, LANES), 1)
    zero = jnp.zeros((GROUP, LANES), jnp.float32)
    diag = [strip[g * GROUP : (g + 1) * GROUP, :] for g in range(groups)]
    column = [
        [
            jnp.broadcast_to(diag[g][:, first + j : first + j + 1], (GROUP, LANES)) if g >= j // GROUP else None
            for g in range(groups)
        ]
        for j in range(STRIP)
    ]
    inside = (lane >= first) & (lane < first + STRIP)
    block = [jnp.where(inside, jnp.where(lane - first == sublane + g * GROUP, 1.0, 0.0), diag[g]) for g in range(groups)]
    lower = [zero] * groups
    for k in range(0, STRIP, 2):
        home, sub = k // GROUP, k % GROUP
        u, v = column[k], column[k + 1]
        a = row_of(u[home], sub)
        b = row_of(u[home], sub + 1)
        c = row_of(v[home], sub + 1)
        det = a * c - b * b
        guess, correction = reciprocal(det)
        n1 = [None if g < home else c * u[g] - b * v[g] for g in range(groups)]
        n2 = [None if g < home else a * v[g] - b * u[g] for g in range(groups)]
        w1 = [None if g < home else (n1[g] * guess) * correction for g in range(groups)]
        w2 = [None if g < home else (n2[g] * guess) * correction for g in range(groups)]
        for j in range(k + 2, STRIP):
            at, row = j // GROUP, j % GROUP
            uj, vj = row_of(u[at], row), row_of(v[at], row)
            for g in range(at, groups):
                if j < k + 4:
                    step = ((n1[g] * uj + n2[g] * vj) * guess) * correction
                else:
                    step = w1[g] * uj + w2[g] * vj
                column[j][g] = column[j][g] - step
        root_a = lax.rsqrt(a)
        root_d = lax.rsqrt(a * det)
        for g in range(home, groups):
            lower[g] = jnp.where(lane == first + k, u[g] * root_a, lower[g])
            lower[g] = jnp.where(lane == first + k + 1, n2[g] * root_d, lower[g])
        below = sublane > sub + 1
        w1[home] = jnp.where(below, w1[home], 0.0)
        w2[home] = jnp.where(below, w2[home], 0.0)
        t0, t1 = row_of(block[home], sub), row_of(block[home], sub + 1)
        for g in range(home, groups):
            block[g] = block[g] - (w1[g] * t0 + w2[g] * t1)
        block[home] = jnp.where(sublane == sub, t0 * root_a, block[home])
        block[home] = jnp.where(sublane == sub + 1, (a * t1 - b * t0) * root_d, block[home])
    for g in range(groups):
        keep = (lane <= first + sublane + g * GROUP) & inside
        lower[g] = jnp.where(keep, lower[g], 0.0)
    return jnp.concatenate(block, axis=0), jnp.concatenate(lower, axis=0)


def matmul(left, right):
    return jnp.dot(left, right, preferred_element_type=jnp.float32)


def stacked(value):
    high, low = split(value)
    return jnp.concatenate([high, high, low, jnp.zeros_like(high)], axis=0)


def factor_kernel(axis, *refs):
    count = lax.axis_size(axis)
    parts, (own_ref, high_ref, low_ref, work, lower) = refs[:count], refs[count:]
    me = lax.axis_index(axis)
    lane = lax.broadcasted_iota(jnp.int32, (LANES, LANES), 1)
    row = lax.broadcasted_iota(jnp.int32, (LANES, LANES), 0)
    beyond = lane // STRIP > row // STRIP
    for shift, part in enumerate(parts):
        work[lax.rem(me + shift, count), : count * LANES, :] = part[...].astype(jnp.float32)

    def rows_at(block):
        return pl.ds(pl.multiple_of(block * LANES, LANES), LANES)

    def update(target, left, rights, places, on):
        high, low = split(jnp.where(on, left.T, 0.0))
        both = jnp.concatenate([high, low], axis=1)
        for d, (place, (right_high, right_low)) in enumerate(zip(places, rights)):
            product = matmul(both, jnp.concatenate([right_high, right_high], axis=0)) + matmul(high, right_low)
            old = work[place, rows_at(target), :]
            if d == 0:
                old = jnp.where(on, 0.0, old)
            work[place, rows_at(target), :] = old - product

    def block_step(q, carry):
        places = [lax.rem(q + d, count) for d in range(count)]
        rows = [work[place, rows_at(q), :] for place in places]

        before = jnp.maximum(q - 1, 0)
        old_places = [lax.rem(before + d, count) for d in range(count)]
        rights = [work[place, rows_at(before), :] for place in old_places]
        rights[0] = jnp.where(beyond, 0.0, rights[0])
        rights = [split(right) for right in rights]
        for target in (q + 1, q + 2):
            update(target, work[target, rows_at(before), :], rights, old_places, q > 0)

        done = [[] for _ in places]
        for first in range(0, LANES, STRIP):
            last = first + STRIP
            solved, diagonal = eliminate_strip(rows[0][:STRIP], first)
            lower[q, first:last, :] = diagonal
            in_strip = (lane[:STRIP] >= first) & (lane[:STRIP] < last)
            high, low = split(jnp.where(in_strip, solved, 0.0))
            high, low = high.astype(jnp.float32), low.astype(jnp.float32)
            inverse = high if first == 0 else pltpu.roll(high, LANES - first, 1)
            inverse += pltpu.roll(low, (LANES + STRIP - first) % LANES, 1) if first != STRIP else low
            inverse += pltpu.roll(high, (LANES + 2 * STRIP - first) % LANES, 1) if first != 2 * STRIP else high
            inverse = inverse.astype(jnp.bfloat16)
            strips = [solved] + [matmul(inverse, stacked(part[:STRIP])) for part in rows[1:]]
            for part, strip in zip(done, strips):
                part.append(strip)
            if last == LANES:
                break
            high, low = split(solved)
            wide = jnp.concatenate([high, low, high, jnp.zeros_like(high)], axis=0).astype(jnp.float32)
            left = wide.T[last:, :].astype(jnp.bfloat16)
            under = [part[STRIP:] for part in rows]
            inside = (lane[last:] >= first) & (lane[last:] < last)
            under[0] = jnp.where(inside, 0.0, under[0])
            rows = [part - matmul(left, stacked(strip)) for part, strip in zip(under, strips)]

        done = [jnp.concatenate(part, axis=0) for part in done]
        for place, part in zip(places, done):
            work[place, rows_at(q), :] = part
        rights = [split(part) for part in [jnp.where(beyond, 0.0, done[0])] + done[1:]]
        update(q + 1, done[1], rights, places, True)
        return carry

    lax.fori_loop(0, count, block_step, 0)

    for i in range(count):
        block = work[i, rows_at(me), :]
        upper = jnp.where((i > me) | ((i == me) & beyond), block, 0.0)
        own_ref[i * LANES : (i + 1) * LANES, :] = upper.T + jnp.where(i == me, lower[i], 0.0)
        for c in range(count):
            block = work[c, i * LANES : (i + 1) * LANES, :]
            if c > i:
                block = jnp.zeros_like(block)
            elif c == i:
                block = jnp.where(lane <= row, block, 0.0)
            high, low = split(block)
            high_ref[i * LANES : (i + 1) * LANES, c * LANES : (c + 1) * LANES] = high
            low_ref[i * LANES : (i + 1) * LANES, c * LANES : (c + 1) * LANES] = low


def solve_kernel(row_axis, col_axis, order, group_count, *refs):
    high_ref, low_ref = refs[:2]
    inputs = refs[2 : 3 + group_count]
    trailing_ref, own_ref, schur_ref, group, side = refs[3 + group_count :]
    size = high_ref.shape[0]
    half = size // 2
    share = own_ref.shape[1]
    count = side.shape[0] // share
    my_row, my_col = lax.axis_index(row_axis), lax.axis_index(col_axis)
    for i, ref in enumerate(inputs[:-1]):
        if order is None:
            group[...] = ref[...]
        else:
            for p in range(count):
                at = jnp.bitwise_xor(my_col, i * count + p) * share
                group[pl.ds(pl.multiple_of(at, share), share), :] = ref[p * share : (p + 1) * share, :]
    for p in range(count):
        place = jnp.bitwise_xor(my_row, p) if order else lax.rem(my_row + count - p, count)
        side[pl.ds(pl.multiple_of(place * share, share), share), :] = inputs[-1][p * share : (p + 1) * share, :]
    contract = (((1,), (1,)), ((), ()))

    def product(left, right):
        return lax.dot_general(left, right, contract, preferred_element_type=jnp.float32)

    def solve(rows):
        first = product(rows[:, :half], high_ref[:half, :half]) + product(rows[:, :half], low_ref[:half, :half])
        second = product(rows, high_ref[half:, :]) + product(rows, low_ref[half:, :])
        return jnp.concatenate([first, second], axis=1).astype(jnp.bfloat16)

    side[...] = solve(side[...])
    rows = group.shape[0]
    chunk = min(rows, 256)

    def step(i, carry):
        here = pl.ds(pl.multiple_of(i * chunk, chunk), chunk)
        solved = solve(group[here, :])
        group[here, :] = solved
        update = product(solved, side[...])
        schur_ref[here, :] = (trailing_ref[here, :].astype(jnp.float32) - update).astype(jnp.bfloat16)
        return carry

    if rows == chunk:
        step(0, 0)
    else:
        lax.fori_loop(0, rows // chunk, step, 0)
    own_ref[0] = group[pl.ds(pl.multiple_of(my_col * share, share), share), :]


def body(pivot_block, panel, lead, trailing):
    pivot_size, local_width = pivot_block.shape
    rows, cols = lax.axis_size("row"), lax.axis_size("col")
    share = panel.shape[1]
    col_index = lax.axis_index("col")
    vmem = pl.BlockSpec(memory_space=pltpu.VMEM)

    pivots = [pivot_block] + [
        lax.ppermute(pivot_block, "row", [((d + s) % rows, d) for d in range(rows)]) for s in range(1, rows)
    ]

    def live(shards, rows_of):
        block = jnp.concatenate([(shard * share + jnp.arange(share)) // BLOCK for shard in shards])
        matches = block[:, None] == jnp.arange(lead.shape[1])[None, :]
        row_lead = jnp.sum(jnp.where(matches, lead, 0), axis=1)
        keep = (jnp.arange(pivot_size) // BLOCK)[None, :] >= row_lead[:, None]
        return jnp.where(keep, rows_of, jnp.zeros_like(rows_of))

    ratio = cols // rows
    paired = cols == 2 * rows and rows & (rows - 1) == 0

    def to_side(array, shift):
        pairs = []
        for r in range(rows):
            for c in range(cols):
                to_row, to_col = (c % rows + shift) % rows, r * ratio + c // rows
                pairs.append((c * rows + r, to_col * rows + to_row))
        return lax.ppermute(array, ("col", "row"), pairs)

    if paired:
        quad = [panel[0]] + [lax.ppermute(panel[0], "col", [(d ^ p, d) for d in range(cols)]) for p in range(1, rows)]
        quad = live([col_index ^ p for p in range(rows)], jnp.concatenate(quad, axis=0))
        group = [quad, lax.ppermute(quad, "col", [(d ^ rows, d) for d in range(cols)])]
        side = to_side(quad, 0)
    else:
        masked = live([col_index], panel[0])
        group = [lax.all_gather(masked, "col", axis=0, tiled=True)]
        side = jnp.concatenate([to_side(masked, s) for s in range(rows)], axis=0)

    own, high, low = pl.pallas_call(
        functools.partial(factor_kernel, "row"),
        out_shape=(
            jax.ShapeDtypeStruct((pivot_size, local_width), jnp.float32),
            jax.ShapeDtypeStruct((pivot_size, pivot_size), jnp.bfloat16),
            jax.ShapeDtypeStruct((pivot_size, pivot_size), jnp.bfloat16),
        ),
        in_specs=[vmem] * rows,
        out_specs=(vmem,) * 3,
        scratch_shapes=[
            pltpu.VMEM((rows + 2, pivot_size + 2 * LANES, LANES), jnp.float32),
            pltpu.VMEM((rows, LANES, LANES), jnp.float32),
        ],
        compiler_params=pltpu.CompilerParams(vmem_limit_bytes=32 * 1024 * 1024),
        cost_estimate=pl.CostEstimate(flops=10**9, bytes_accessed=2 * 10**6, transcendentals=10**5),
        name="factor",
    )(*pivots)

    group_rows = share * cols
    panel_factor, schur = pl.pallas_call(
        functools.partial(solve_kernel, "row", "col", True if paired else None, len(group)),
        out_shape=(
            jax.ShapeDtypeStruct(panel.shape, jnp.bfloat16),
            jax.ShapeDtypeStruct(trailing.shape, jnp.bfloat16),
        ),
        in_specs=[vmem] * (4 + len(group)),
        out_specs=(vmem,) * 2,
        scratch_shapes=[
            pltpu.VMEM((group_rows, pivot_size), jnp.bfloat16),
            pltpu.VMEM((share * rows, pivot_size), jnp.bfloat16),
        ],
        compiler_params=pltpu.CompilerParams(vmem_limit_bytes=48 * 1024 * 1024),
        cost_estimate=pl.CostEstimate(flops=4 * 10**8, bytes_accessed=2 * 10**6, transcendentals=0),
        name="solve",
    )(high, low, *group, side, trailing)
    return (own, panel_factor, schur)


def solution(mesh):
    return jax.shard_map(
        body,
        mesh=mesh,
        in_specs=(P(None, "row"), P("row", "col", None), P("row", None), P("row", "col")),
        out_specs=(P(None, "row"), P("row", "col", None), P("row", "col")),
        check_vma=False,
    )
```

```python
import functools

import jax
import jax.numpy as jnp
from jax import lax
from jax.experimental import pallas as pl
from jax.experimental.pallas import tpu as pltpu
from jax.sharding import PartitionSpec as P

BLOCK = 128
STRIP = 32
GROUP = 8
LANES = 128


def split(value):
    high = value.astype(jnp.bfloat16)
    low = (value - high.astype(jnp.float32)).astype(jnp.bfloat16)
    return high, low


def row_of(value, row):
    return jnp.broadcast_to(value[row : row + 1, :], (GROUP, LANES))


def reciprocal(value):
    guess = pl.reciprocal(value, approx=True)
    return guess, 2.0 - value * guess


def eliminate_strip(strip, first):
    groups = STRIP // GROUP
    sublane = lax.broadcasted_iota(jnp.int32, (GROUP, LANES), 0)
    lane = lax.broadcasted_iota(jnp.int32, (GROUP, LANES), 1)
    zero = jnp.zeros((GROUP, LANES), jnp.float32)
    diag = [strip[g * GROUP : (g + 1) * GROUP, :] for g in range(groups)]
    column = [
        [
            jnp.broadcast_to(diag[g][:, first + j : first + j + 1], (GROUP, LANES)) if g >= j // GROUP else None
            for g in range(groups)
        ]
        for j in range(STRIP)
    ]
    inside = (lane >= first) & (lane < first + STRIP)
    block = [jnp.where(inside, jnp.where(lane - first == sublane + g * GROUP, 1.0, 0.0), diag[g]) for g in range(groups)]
    lower = [zero] * groups
    for k in range(0, STRIP, 2):
        home, sub = k // GROUP, k % GROUP
        u, v = column[k], column[k + 1]
        a = row_of(u[home], sub)
        b = row_of(u[home], sub + 1)
        c = row_of(v[home], sub + 1)
        det = a * c - b * b
        guess, correction = reciprocal(det)
        n1 = [None if g < home else c * u[g] - b * v[g] for g in range(groups)]
        n2 = [None if g < home else a * v[g] - b * u[g] for g in range(groups)]
        w1 = [None if g < home else (n1[g] * guess) * correction for g in range(groups)]
        w2 = [None if g < home else (n2[g] * guess) * correction for g in range(groups)]
        for j in range(k + 2, STRIP):
            at, row = j // GROUP, j % GROUP
            uj, vj = row_of(u[at], row), row_of(v[at], row)
            for g in range(at, groups):
                if j < k + 4:
                    step = ((n1[g] * uj + n2[g] * vj) * guess) * correction
                else:
                    step = w1[g] * uj + w2[g] * vj
                column[j][g] = column[j][g] - step
        root_a = lax.rsqrt(a)
        root_d = lax.rsqrt(a * det)
        for g in range(home, groups):
            lower[g] = jnp.where(lane == first + k, u[g] * root_a, lower[g])
            lower[g] = jnp.where(lane == first + k + 1, n2[g] * root_d, lower[g])
        below = sublane > sub + 1
        w1[home] = jnp.where(below, w1[home], 0.0)
        w2[home] = jnp.where(below, w2[home], 0.0)
        t0, t1 = row_of(block[home], sub), row_of(block[home], sub + 1)
        for g in range(home, groups):
            block[g] = block[g] - (w1[g] * t0 + w2[g] * t1)
        block[home] = jnp.where(sublane == sub, t0 * root_a, block[home])
        block[home] = jnp.where(sublane == sub + 1, (a * t1 - b * t0) * root_d, block[home])
    for g in range(groups):
        keep = (lane <= first + sublane + g * GROUP) & inside
        lower[g] = jnp.where(keep, lower[g], 0.0)
    return jnp.concatenate(block, axis=0), jnp.concatenate(lower, axis=0)


def matmul(left, right):
    return jnp.dot(left, right, preferred_element_type=jnp.float32)


def stacked(value):
    high, low = split(value)
    return jnp.concatenate([high, high, low, jnp.zeros_like(high)], axis=0)


def rows_at(block):
    return pl.ds(pl.multiple_of(block * LANES, LANES), LANES)


def square_iota(axis):
    return lax.broadcasted_iota(jnp.int32, (LANES, LANES), axis)


def beyond_strip():
    return square_iota(1) // STRIP > square_iota(0) // STRIP


def eliminate_block(rows, lower_ref):
    lane = square_iota(1)
    done = [[] for _ in rows]
    for first in range(0, LANES, STRIP):
        last = first + STRIP
        solved, diagonal = eliminate_strip(rows[0][:STRIP], first)
        lower_ref[first:last, :] = diagonal
        in_strip = (lane[:STRIP] >= first) & (lane[:STRIP] < last)
        high, low = split(jnp.where(in_strip, solved, 0.0))
        high, low = high.astype(jnp.float32), low.astype(jnp.float32)
        inverse = high if first == 0 else pltpu.roll(high, LANES - first, 1)
        inverse += pltpu.roll(low, (LANES + STRIP - first) % LANES, 1) if first != STRIP else low
        inverse += pltpu.roll(high, (LANES + 2 * STRIP - first) % LANES, 1) if first != 2 * STRIP else high
        inverse = inverse.astype(jnp.bfloat16)
        strips = [solved] + [matmul(inverse, stacked(part[:STRIP])) for part in rows[1:]]
        for part, strip in zip(done, strips):
            part.append(strip)
        if last == LANES:
            break
        high, low = split(solved)
        wide = jnp.concatenate([high, low, high, jnp.zeros_like(high)], axis=0).astype(jnp.float32)
        left = wide.T[last:, :].astype(jnp.bfloat16)
        under = [part[STRIP:] for part in rows]
        inside = (lane[last:] >= first) & (lane[last:] < last)
        under[0] = jnp.where(inside, 0.0, under[0])
        rows = [part - matmul(left, stacked(strip)) for part, strip in zip(under, strips)]
    return [jnp.concatenate(part, axis=0) for part in done]


def first_kernel(axis, *refs):
    count = lax.axis_size(axis)
    parts, (done_ref, lower_ref, work) = refs[:count], refs[count:]
    me = lax.axis_index(axis)
    for shift, part in enumerate(parts):
        work[lax.rem(me + shift, count)] = part[:LANES, :].astype(jnp.float32)
    done = eliminate_block([work[d] for d in range(count)], lower_ref)
    for d in range(count):
        done_ref[d] = done[d]


def rest_kernel(axis, *refs):
    count = lax.axis_size(axis)
    parts, (done_ref, first_lower, own_ref, high_ref, low_ref, work, lower) = refs[:count], refs[count:]
    me = lax.axis_index(axis)
    lane, row = square_iota(1), square_iota(0)
    beyond = beyond_strip()
    for shift, part in enumerate(parts):
        work[lax.rem(me + shift, count), LANES : count * LANES, :] = part[LANES:, :].astype(jnp.float32)
    work[:count, :LANES, :] = done_ref[...]
    lower[0] = first_lower[...]

    def block_step(q, carry):
        before = q - 1
        places = [lax.rem(before + d, count) for d in range(count)]
        rights = [work[place, rows_at(before), :] for place in places]
        rights[0] = jnp.where(beyond, 0.0, rights[0])
        rights = [split(right) for right in rights]

        def update(target):
            high, low = split(work[target, rows_at(before), :].T)
            both = jnp.concatenate([high, low], axis=1)
            new = []
            for d, (place, (right_high, right_low)) in enumerate(zip(places, rights)):
                product = matmul(both, jnp.concatenate([right_high, right_high], axis=0)) + matmul(high, right_low)
                new.append(-product if d == 0 else work[place, rows_at(target), :] - product)
            return new

        rows = update(q)
        for target in (q + 1, q + 2):
            for place, new in zip(places, update(target)):
                work[place, rows_at(target), :] = new
        done = eliminate_block(rows[1:] + rows[:1], lower.at[q])
        for place, part in zip(places[1:] + places[:1], done):
            work[place, rows_at(q), :] = part
        return carry

    lax.fori_loop(1, count, block_step, 0)

    for i in range(count):
        block = work[i, rows_at(me), :]
        upper = jnp.where((i > me) | ((i == me) & beyond), block, 0.0)
        own_ref[i * LANES : (i + 1) * LANES, :] = upper.T + jnp.where(i == me, lower[i], 0.0)
        for c in range(count):
            block = work[c, i * LANES : (i + 1) * LANES, :]
            if c > i:
                block = jnp.zeros_like(block)
            elif c == i:
                block = jnp.where(lane <= row, block, 0.0)
            high, low = split(block)
            high_ref[i * LANES : (i + 1) * LANES, c * LANES : (c + 1) * LANES] = high
            low_ref[i * LANES : (i + 1) * LANES, c * LANES : (c + 1) * LANES] = low


def solve_kernel(row_axis, col_axis, order, group_count, *refs):
    high_ref, low_ref = refs[:2]
    inputs = refs[2 : 3 + group_count]
    trailing_ref, own_ref, schur_ref, group, side = refs[3 + group_count :]
    size = high_ref.shape[0]
    half = size // 2
    share = own_ref.shape[1]
    count = side.shape[0] // share
    my_row, my_col = lax.axis_index(row_axis), lax.axis_index(col_axis)
    for i, ref in enumerate(inputs[:-1]):
        if order is None:
            group[...] = ref[...]
        else:
            for p in range(count):
                at = jnp.bitwise_xor(my_col, i * count + p) * share
                group[pl.ds(pl.multiple_of(at, share), share), :] = ref[p * share : (p + 1) * share, :]
    for p in range(count):
        place = jnp.bitwise_xor(my_row, p) if order else lax.rem(my_row + count - p, count)
        side[pl.ds(pl.multiple_of(place * share, share), share), :] = inputs[-1][p * share : (p + 1) * share, :]
    contract = (((1,), (1,)), ((), ()))

    def product(left, right):
        return lax.dot_general(left, right, contract, preferred_element_type=jnp.float32)

    def solve(rows):
        first = product(rows[:, :half], high_ref[:half, :half]) + product(rows[:, :half], low_ref[:half, :half])
        second = product(rows, high_ref[half:, :]) + product(rows, low_ref[half:, :])
        return jnp.concatenate([first, second], axis=1).astype(jnp.bfloat16)

    side[...] = solve(side[...])
    rows = group.shape[0]
    chunk = min(rows, 256)

    def step(i, carry):
        here = pl.ds(pl.multiple_of(i * chunk, chunk), chunk)
        solved = solve(group[here, :])
        group[here, :] = solved
        update = product(solved, side[...])
        schur_ref[here, :] = (trailing_ref[here, :].astype(jnp.float32) - update).astype(jnp.bfloat16)
        return carry

    if rows == chunk:
        step(0, 0)
    else:
        lax.fori_loop(0, rows // chunk, step, 0)
    own_ref[0] = group[pl.ds(pl.multiple_of(my_col * share, share), share), :]


def body(pivot_block, panel, lead, trailing):
    pivot_size, local_width = pivot_block.shape
    rows, cols = lax.axis_size("row"), lax.axis_size("col")
    share = panel.shape[1]
    col_index = lax.axis_index("col")
    vmem = pl.BlockSpec(memory_space=pltpu.VMEM)

    pivots = [pivot_block] + [
        lax.ppermute(pivot_block, "row", [((d + s) % rows, d) for d in range(rows)]) for s in range(1, rows)
    ]

    done, first_lower = pl.pallas_call(
        functools.partial(first_kernel, "row"),
        out_shape=(
            jax.ShapeDtypeStruct((rows, LANES, LANES), jnp.float32),
            jax.ShapeDtypeStruct((LANES, LANES), jnp.float32),
        ),
        in_specs=[vmem] * rows,
        out_specs=(vmem,) * 2,
        scratch_shapes=[pltpu.VMEM((rows, LANES, LANES), jnp.float32)],
        compiler_params=pltpu.CompilerParams(vmem_limit_bytes=32 * 1024 * 1024),
        cost_estimate=pl.CostEstimate(flops=3 * 10**8, bytes_accessed=10**6, transcendentals=10**5),
        name="first",
    )(*pivots)

    def live(shards, rows_of):
        block = jnp.concatenate([(shard * share + jnp.arange(share)) // BLOCK for shard in shards])
        matches = block[:, None] == jnp.arange(lead.shape[1])[None, :]
        row_lead = jnp.sum(jnp.where(matches, lead, 0), axis=1)
        keep = (jnp.arange(pivot_size) // BLOCK)[None, :] >= row_lead[:, None]
        return jnp.where(keep, rows_of, jnp.zeros_like(rows_of))

    ratio = cols // rows
    paired = cols == 2 * rows and rows & (rows - 1) == 0

    def to_side(array, shift):
        pairs = []
        for r in range(rows):
            for c in range(cols):
                to_row, to_col = (c % rows + shift) % rows, r * ratio + c // rows
                pairs.append((c * rows + r, to_col * rows + to_row))
        return lax.ppermute(array, ("col", "row"), pairs)

    if paired:
        own_rows, quad = panel[0], [panel[0]]
        for p in range(1, rows):
            if p == rows - 1:
                own_rows, _ = lax.optimization_barrier((own_rows, pivots))
            quad.append(lax.ppermute(own_rows, "col", [(d ^ p, d) for d in range(cols)]))
        quad, _ = lax.optimization_barrier((quad, first_lower))
        quad = live([col_index ^ p for p in range(rows)], jnp.concatenate(quad, axis=0))
        group = [quad, lax.ppermute(quad, "col", [(d ^ rows, d) for d in range(cols)])]
        side = to_side(quad, 0)
    else:
        masked = live([col_index], panel[0])
        group = [lax.all_gather(masked, "col", axis=0, tiled=True)]
        side = jnp.concatenate([to_side(masked, s) for s in range(rows)], axis=0)

    own, high, low = pl.pallas_call(
        functools.partial(rest_kernel, "row"),
        out_shape=(
            jax.ShapeDtypeStruct((pivot_size, local_width), jnp.float32),
            jax.ShapeDtypeStruct((pivot_size, pivot_size), jnp.bfloat16),
            jax.ShapeDtypeStruct((pivot_size, pivot_size), jnp.bfloat16),
        ),
        in_specs=[vmem] * (rows + 2),
        out_specs=(vmem,) * 3,
        scratch_shapes=[
            pltpu.VMEM((rows + 2, pivot_size + 2 * LANES, LANES), jnp.float32),
            pltpu.VMEM((rows, LANES, LANES), jnp.float32),
        ],
        compiler_params=pltpu.CompilerParams(vmem_limit_bytes=32 * 1024 * 1024),
        cost_estimate=pl.CostEstimate(flops=10**9, bytes_accessed=2 * 10**6, transcendentals=10**5),
        name="rest",
    )(*pivots, done, first_lower)

    group_rows = share * cols
    panel_factor, schur = pl.pallas_call(
        functools.partial(solve_kernel, "row", "col", True if paired else None, len(group)),
        out_shape=(
            jax.ShapeDtypeStruct(panel.shape, jnp.bfloat16),
            jax.ShapeDtypeStruct(trailing.shape, jnp.bfloat16),
        ),
        in_specs=[vmem] * (4 + len(group)),
        out_specs=(vmem,) * 2,
        scratch_shapes=[
            pltpu.VMEM((group_rows, pivot_size), jnp.bfloat16),
            pltpu.VMEM((share * rows, pivot_size), jnp.bfloat16),
        ],
        compiler_params=pltpu.CompilerParams(vmem_limit_bytes=48 * 1024 * 1024),
        cost_estimate=pl.CostEstimate(flops=4 * 10**8, bytes_accessed=2 * 10**6, transcendentals=0),
        name="solve",
    )(high, low, *group, side, trailing)
    return (own, panel_factor, schur)


def solution(mesh):
    return jax.shard_map(
        body,
        mesh=mesh,
        in_specs=(P(None, "row"), P("row", "col", None), P("row", None), P("row", "col")),
        out_specs=(P(None, "row"), P("row", "col", None), P("row", "col")),
        check_vma=False,
    )
```

```python
import functools

import jax
import jax.numpy as jnp
from jax import lax
from jax.experimental import pallas as pl
from jax.experimental.pallas import tpu as pltpu
from jax.sharding import PartitionSpec as P

BLOCK = 128
STRIP = 32
GROUP = 8
LANES = 128


def split(value):
    high = value.astype(jnp.bfloat16)
    low = (value - high.astype(jnp.float32)).astype(jnp.bfloat16)
    return high, low


def row_of(value, row):
    return jnp.broadcast_to(value[row : row + 1, :], (GROUP, LANES))


def reciprocal(value):
    guess = pl.reciprocal(value, approx=True)
    return guess, 2.0 - value * guess


def eliminate_strip(strip, first):
    groups = STRIP // GROUP
    sublane = lax.broadcasted_iota(jnp.int32, (GROUP, LANES), 0)
    lane = lax.broadcasted_iota(jnp.int32, (GROUP, LANES), 1)
    zero = jnp.zeros((GROUP, LANES), jnp.float32)
    diag = [strip[g * GROUP : (g + 1) * GROUP, :] for g in range(groups)]
    column = [
        [
            jnp.broadcast_to(diag[g][:, first + j : first + j + 1], (GROUP, LANES)) if g >= j // GROUP else None
            for g in range(groups)
        ]
        for j in range(STRIP)
    ]
    inside = (lane >= first) & (lane < first + STRIP)
    block = [jnp.where(inside, jnp.where(lane - first == sublane + g * GROUP, 1.0, 0.0), diag[g]) for g in range(groups)]
    lower = [zero] * groups
    for k in range(0, STRIP, 2):
        home, sub = k // GROUP, k % GROUP
        u, v = column[k], column[k + 1]
        a = row_of(u[home], sub)
        b = row_of(u[home], sub + 1)
        c = row_of(v[home], sub + 1)
        det = a * c - b * b
        guess, correction = reciprocal(det)
        n1 = [None if g < home else c * u[g] - b * v[g] for g in range(groups)]
        n2 = [None if g < home else a * v[g] - b * u[g] for g in range(groups)]
        w1 = [None if g < home else (n1[g] * guess) * correction for g in range(groups)]
        w2 = [None if g < home else (n2[g] * guess) * correction for g in range(groups)]
        for j in range(k + 2, STRIP):
            at, row = j // GROUP, j % GROUP
            uj, vj = row_of(u[at], row), row_of(v[at], row)
            for g in range(at, groups):
                if j < k + 4:
                    step = ((n1[g] * uj + n2[g] * vj) * guess) * correction
                else:
                    step = w1[g] * uj + w2[g] * vj
                column[j][g] = column[j][g] - step
        root_a = lax.rsqrt(a)
        root_d = lax.rsqrt(a * det)
        for g in range(home, groups):
            lower[g] = jnp.where(lane == first + k, u[g] * root_a, lower[g])
            lower[g] = jnp.where(lane == first + k + 1, n2[g] * root_d, lower[g])
        below = sublane > sub + 1
        w1[home] = jnp.where(below, w1[home], 0.0)
        w2[home] = jnp.where(below, w2[home], 0.0)
        t0, t1 = row_of(block[home], sub), row_of(block[home], sub + 1)
        for g in range(home, groups):
            block[g] = block[g] - (w1[g] * t0 + w2[g] * t1)
        block[home] = jnp.where(sublane == sub, t0 * root_a, block[home])
        block[home] = jnp.where(sublane == sub + 1, (a * t1 - b * t0) * root_d, block[home])
    for g in range(groups):
        keep = (lane <= first + sublane + g * GROUP) & inside
        lower[g] = jnp.where(keep, lower[g], 0.0)
    return jnp.concatenate(block, axis=0), jnp.concatenate(lower, axis=0)


def matmul(left, right):
    return jnp.dot(left, right, preferred_element_type=jnp.float32)


def stacked(value):
    high, low = split(value)
    return jnp.concatenate([high, high, low, jnp.zeros_like(high)], axis=0)


def rows_at(block):
    return pl.ds(pl.multiple_of(block * LANES, LANES), LANES)


def square_iota(axis):
    return lax.broadcasted_iota(jnp.int32, (LANES, LANES), axis)


def beyond_strip():
    return square_iota(1) // STRIP > square_iota(0) // STRIP


def eliminate_block(rows, lower_ref):
    lane = square_iota(1)
    done = [[] for _ in rows]
    for first in range(0, LANES, STRIP):
        last = first + STRIP
        solved, diagonal = eliminate_strip(rows[0][:STRIP], first)
        lower_ref[first:last, :] = diagonal
        in_strip = (lane[:STRIP] >= first) & (lane[:STRIP] < last)
        high, low = split(jnp.where(in_strip, solved, 0.0))
        high, low = high.astype(jnp.float32), low.astype(jnp.float32)
        inverse = high if first == 0 else pltpu.roll(high, LANES - first, 1)
        inverse += pltpu.roll(low, (LANES + STRIP - first) % LANES, 1) if first != STRIP else low
        inverse += pltpu.roll(high, (LANES + 2 * STRIP - first) % LANES, 1) if first != 2 * STRIP else high
        inverse = inverse.astype(jnp.bfloat16)
        strips = [solved] + [matmul(inverse, stacked(part[:STRIP])) for part in rows[1:]]
        for part, strip in zip(done, strips):
            part.append(strip)
        if last == LANES:
            break
        high, low = split(solved)
        wide = jnp.concatenate([high, low, high, jnp.zeros_like(high)], axis=0).astype(jnp.float32)
        left = wide.T[last:, :].astype(jnp.bfloat16)
        under = [part[STRIP:] for part in rows]
        inside = (lane[last:] >= first) & (lane[last:] < last)
        under[0] = jnp.where(inside, 0.0, under[0])
        rows = [part - matmul(left, stacked(strip)) for part, strip in zip(under, strips)]
    return [jnp.concatenate(part, axis=0) for part in done]


def assemble(me, own, mate, far, far_mate, work):
    size = own.shape[0]
    half = size // 2
    near = ((own, me), (mate, jnp.bitwise_xor(me, 1)))
    other = ((far, jnp.bitwise_xor(me, 2)), (far_mate, jnp.bitwise_xor(me, 3)))

    @pl.when(me < 2)
    def _():
        for part, column in near:
            work[column, :half, :] = part[:half, :].astype(jnp.float32)
            for block in range(half // LANES, size // LANES):
                flipped = part[block * LANES : (block + 1) * LANES, :].astype(jnp.float32).T
                work[block, rows_at(column), :] = flipped
        for part, column in other:
            work[column, half:size, :] = part[...].astype(jnp.float32)

    @pl.when(me >= 2)
    def _():
        for part, column in near:
            work[column, :size, :] = part[...].astype(jnp.float32)
        for part, column in other:
            work[column, :half, :] = part[...].astype(jnp.float32)


def first_kernel(axis, own, mate, far, far_mate, done_ref, lower_ref, work):
    count = lax.axis_size(axis)
    assemble(lax.axis_index(axis), own, mate, far, far_mate, work)
    done = eliminate_block([work[d, :LANES, :] for d in range(count)], lower_ref)
    for d in range(count):
        done_ref[d] = done[d]


def rest_kernel(
    axis, own, mate, far, far_mate, done_ref, first_lower, own_ref, high_ref, low_ref, work, lower
):
    count = lax.axis_size(axis)
    me = lax.axis_index(axis)
    lane, row = square_iota(1), square_iota(0)
    beyond = beyond_strip()
    assemble(me, own, mate, far, far_mate, work)
    work[:count, :LANES, :] = done_ref[...]
    lower[0] = first_lower[...]

    def block_step(q, carry):
        before = q - 1
        places = [lax.rem(before + d, count) for d in range(count)]
        rights = [work[place, rows_at(before), :] for place in places]
        rights[0] = jnp.where(beyond, 0.0, rights[0])
        rights = [split(right) for right in rights]

        def update(target):
            high, low = split(work[target, rows_at(before), :].T)
            both = jnp.concatenate([high, low], axis=1)
            new = []
            for d, (place, (right_high, right_low)) in enumerate(zip(places, rights)):
                product = matmul(both, jnp.concatenate([right_high, right_high], axis=0)) + matmul(high, right_low)
                new.append(-product if d == 0 else work[place, rows_at(target), :] - product)
            return new

        rows = update(q)
        for target in (q + 1, q + 2):
            for place, new in zip(places, update(target)):
                work[place, rows_at(target), :] = new
        done = eliminate_block(rows[1:] + rows[:1], lower.at[q])
        for place, part in zip(places[1:] + places[:1], done):
            work[place, rows_at(q), :] = part
        return carry

    lax.fori_loop(1, count, block_step, 0)

    for i in range(count):
        block = work[i, rows_at(me), :]
        upper = jnp.where((i > me) | ((i == me) & beyond), block, 0.0)
        own_ref[i * LANES : (i + 1) * LANES, :] = upper.T + jnp.where(i == me, lower[i], 0.0)
        for c in range(count):
            block = work[c, i * LANES : (i + 1) * LANES, :]
            if c > i:
                block = jnp.zeros_like(block)
            elif c == i:
                block = jnp.where(lane <= row, block, 0.0)
            high, low = split(block)
            high_ref[i * LANES : (i + 1) * LANES, c * LANES : (c + 1) * LANES] = high
            low_ref[i * LANES : (i + 1) * LANES, c * LANES : (c + 1) * LANES] = low


def solve_kernel(row_axis, col_axis, order, group_count, *refs):
    high_ref, low_ref = refs[:2]
    inputs = refs[2 : 3 + group_count]
    trailing_ref, own_ref, schur_ref, group, side = refs[3 + group_count :]
    size = high_ref.shape[0]
    half = size // 2
    share = own_ref.shape[1]
    count = side.shape[0] // share
    my_row, my_col = lax.axis_index(row_axis), lax.axis_index(col_axis)
    for i, ref in enumerate(inputs[:-1]):
        if order is None:
            group[...] = ref[...]
        else:
            for p in range(count):
                at = jnp.bitwise_xor(my_col, i * count + p) * share
                group[pl.ds(pl.multiple_of(at, share), share), :] = ref[p * share : (p + 1) * share, :]
    for p in range(count):
        place = jnp.bitwise_xor(my_row, p) if order else lax.rem(my_row + count - p, count)
        side[pl.ds(pl.multiple_of(place * share, share), share), :] = inputs[-1][p * share : (p + 1) * share, :]
    contract = (((1,), (1,)), ((), ()))

    def product(left, right):
        return lax.dot_general(left, right, contract, preferred_element_type=jnp.float32)

    def solve(rows):
        first = product(rows[:, :half], high_ref[:half, :half]) + product(rows[:, :half], low_ref[:half, :half])
        second = product(rows, high_ref[half:, :]) + product(rows, low_ref[half:, :])
        return jnp.concatenate([first, second], axis=1).astype(jnp.bfloat16)

    side[...] = solve(side[...])
    rows = group.shape[0]
    chunk = min(rows, 256)

    def step(i, carry):
        here = pl.ds(pl.multiple_of(i * chunk, chunk), chunk)
        solved = solve(group[here, :])
        group[here, :] = solved
        update = product(solved, side[...])
        schur_ref[here, :] = (trailing_ref[here, :].astype(jnp.float32) - update).astype(jnp.bfloat16)
        return carry

    if rows == chunk:
        step(0, 0)
    else:
        lax.fori_loop(0, rows // chunk, step, 0)
    own_ref[0] = group[pl.ds(pl.multiple_of(my_col * share, share), share), :]


def body(pivot_block, panel, lead, trailing):
    pivot_size, local_width = pivot_block.shape
    rows, cols = lax.axis_size("row"), lax.axis_size("col")
    share = panel.shape[1]
    col_index = lax.axis_index("col")
    vmem = pl.BlockSpec(memory_space=pltpu.VMEM)

    half = pivot_size // 2
    row_index = lax.axis_index("row")
    wide = pivot_block.astype(jnp.float32)
    mate = lax.ppermute(pivot_block, "row", [(d ^ 1, d) for d in range(rows)])
    diagonal_half = lax.dynamic_slice_in_dim(pivot_block, row_index // 2 * half, half, 0)
    far = lax.ppermute(diagonal_half, "row", [(d ^ 2, d) for d in range(rows)])
    far_mate = lax.ppermute(far, "row", [(d ^ 1, d) for d in range(rows)])
    pivots = [wide, mate, far, far_mate]

    done, first_lower = pl.pallas_call(
        functools.partial(first_kernel, "row"),
        out_shape=(
            jax.ShapeDtypeStruct((rows, LANES, LANES), jnp.float32),
            jax.ShapeDtypeStruct((LANES, LANES), jnp.float32),
        ),
        in_specs=[vmem] * len(pivots),
        out_specs=(vmem,) * 2,
        scratch_shapes=[pltpu.VMEM((rows, pivot_size, LANES), jnp.float32)],
        compiler_params=pltpu.CompilerParams(vmem_limit_bytes=32 * 1024 * 1024),
        cost_estimate=pl.CostEstimate(flops=3 * 10**8, bytes_accessed=10**6, transcendentals=10**5),
        name="first",
    )(*pivots)

    def live(shards, rows_of):
        block = jnp.concatenate([(shard * share + jnp.arange(share)) // BLOCK for shard in shards])
        matches = block[:, None] == jnp.arange(lead.shape[1])[None, :]
        row_lead = jnp.sum(jnp.where(matches, lead, 0), axis=1)
        keep = (jnp.arange(pivot_size) // BLOCK)[None, :] >= row_lead[:, None]
        return jnp.where(keep, rows_of, jnp.zeros_like(rows_of))

    ratio = cols // rows
    paired = cols == 2 * rows and rows & (rows - 1) == 0

    def to_side(array, shift):
        pairs = []
        for r in range(rows):
            for c in range(cols):
                to_row, to_col = (c % rows + shift) % rows, r * ratio + c // rows
                pairs.append((c * rows + r, to_col * rows + to_row))
        return lax.ppermute(array, ("col", "row"), pairs)

    if paired:
        own_rows, quad = panel[0], [panel[0]]
        for p in range(1, rows):
            if p == rows - 1:
                own_rows, _ = lax.optimization_barrier((own_rows, far))
            quad.append(lax.ppermute(own_rows, "col", [(d ^ p, d) for d in range(cols)]))
        quad, _ = lax.optimization_barrier((quad, first_lower))
        quad = live([col_index ^ p for p in range(rows)], jnp.concatenate(quad, axis=0))
        group = [quad, lax.ppermute(quad, "col", [(d ^ rows, d) for d in range(cols)])]
        side = to_side(quad, 0)
    else:
        masked = live([col_index], panel[0])
        group = [lax.all_gather(masked, "col", axis=0, tiled=True)]
        side = jnp.concatenate([to_side(masked, s) for s in range(rows)], axis=0)

    own, high, low = pl.pallas_call(
        functools.partial(rest_kernel, "row"),
        out_shape=(
            jax.ShapeDtypeStruct((pivot_size, local_width), jnp.float32),
            jax.ShapeDtypeStruct((pivot_size, pivot_size), jnp.bfloat16),
            jax.ShapeDtypeStruct((pivot_size, pivot_size), jnp.bfloat16),
        ),
        in_specs=[vmem] * (len(pivots) + 2),
        out_specs=(vmem,) * 3,
        scratch_shapes=[
            pltpu.VMEM((rows + 2, pivot_size + 2 * LANES, LANES), jnp.float32),
            pltpu.VMEM((rows, LANES, LANES), jnp.float32),
        ],
        compiler_params=pltpu.CompilerParams(vmem_limit_bytes=32 * 1024 * 1024),
        cost_estimate=pl.CostEstimate(flops=10**9, bytes_accessed=2 * 10**6, transcendentals=10**5),
        name="rest",
    )(*pivots, done, first_lower)

    group_rows = share * cols
    panel_factor, schur = pl.pallas_call(
        functools.partial(solve_kernel, "row", "col", True if paired else None, len(group)),
        out_shape=(
            jax.ShapeDtypeStruct(panel.shape, jnp.bfloat16),
            jax.ShapeDtypeStruct(trailing.shape, jnp.bfloat16),
        ),
        in_specs=[vmem] * (4 + len(group)),
        out_specs=(vmem,) * 2,
        scratch_shapes=[
            pltpu.VMEM((group_rows, pivot_size), jnp.bfloat16),
            pltpu.VMEM((share * rows, pivot_size), jnp.bfloat16),
        ],
        compiler_params=pltpu.CompilerParams(vmem_limit_bytes=48 * 1024 * 1024),
        cost_estimate=pl.CostEstimate(flops=4 * 10**8, bytes_accessed=2 * 10**6, transcendentals=0),
        name="solve",
    )(high, low, *group, side, trailing)
    return (own, panel_factor, schur)


def solution(mesh):
    return jax.shard_map(
        body,
        mesh=mesh,
        in_specs=(P(None, "row"), P("row", "col", None), P("row", None), P("row", "col")),
        out_specs=(P(None, "row"), P("row", "col", None), P("row", "col")),
        check_vma=False,
    )
```

```python
import functools

import jax
import jax.numpy as jnp
from jax import lax
from jax.experimental import pallas as pl
from jax.experimental.pallas import tpu as pltpu
from jax.sharding import PartitionSpec as P

BLOCK = 128
STRIP = 32
GROUP = 8
LANES = 128


def split(value):
    high = value.astype(jnp.bfloat16)
    low = (value - high.astype(jnp.float32)).astype(jnp.bfloat16)
    return high, low


def row_of(value, row):
    return jnp.broadcast_to(value[row : row + 1, :], (GROUP, LANES))


def reciprocal(value):
    guess = pl.reciprocal(value, approx=True)
    return guess, 2.0 - value * guess


def eliminate_strip(strip, first):
    groups = STRIP // GROUP
    sublane = lax.broadcasted_iota(jnp.int32, (GROUP, LANES), 0)
    lane = lax.broadcasted_iota(jnp.int32, (GROUP, LANES), 1)
    zero = jnp.zeros((GROUP, LANES), jnp.float32)
    diag = [strip[g * GROUP : (g + 1) * GROUP, :] for g in range(groups)]
    column = [
        [
            jnp.broadcast_to(diag[g][:, first + j : first + j + 1], (GROUP, LANES)) if g >= j // GROUP else None
            for g in range(groups)
        ]
        for j in range(STRIP)
    ]
    inside = (lane >= first) & (lane < first + STRIP)
    block = [jnp.where(inside, jnp.where(lane - first == sublane + g * GROUP, 1.0, 0.0), diag[g]) for g in range(groups)]
    lower = [zero] * groups
    for k in range(0, STRIP, 4):
        home, sub = k // GROUP, k % GROUP
        live = range(home, groups)
        u0, u1, u2, u3 = column[k : k + 4]

        def entry(i, j):
            return row_of(column[k + j][home], sub + i)

        a, b, c = entry(0, 0), entry(1, 0), entry(1, 1)
        p20, p21, p30, p31 = entry(2, 0), entry(2, 1), entry(3, 0), entry(3, 1)
        p22, p32, p33 = entry(2, 2), entry(3, 2), entry(3, 3)
        det1 = a * c - b * b
        m20, m21 = c * p20 - b * p21, a * p21 - b * p20
        m30, m31 = c * p30 - b * p31, a * p31 - b * p30
        s22 = det1 * p22 - (m20 * p20 + m21 * p21)
        s32 = det1 * p32 - (m30 * p20 + m31 * p21)
        s33 = det1 * p33 - (m30 * p30 + m31 * p31)
        det2 = s22 * s33 - s32 * s32
        guess1, correction1 = reciprocal(det1)
        guess2, correction2 = reciprocal(det2)
        r1 = guess1 * correction1
        n0 = {g: c * u0[g] - b * u1[g] for g in live}
        n1 = {g: a * u1[g] - b * u0[g] for g in live}
        v2 = {g: det1 * u2[g] - (n0[g] * p20 + n1[g] * p21) for g in live}
        v3 = {g: det1 * u3[g] - (n0[g] * p30 + n1[g] * p31) for g in live}
        n2 = {g: s33 * v2[g] - s32 * v3[g] for g in live}
        n3 = {g: s22 * v3[g] - s32 * v2[g] for g in live}
        w0 = {g: n0[g] * r1 for g in live}
        w1 = {g: n1[g] * r1 for g in live}
        y2 = {g: n2[g] * r1 for g in live}
        y3 = {g: n3[g] * r1 for g in live}
        w2 = {g: (y2[g] * guess2) * correction2 for g in live}
        w3 = {g: (y3[g] * guess2) * correction2 for g in live}
        for j in range(k + 4, STRIP):
            at, row = j // GROUP, j % GROUP
            e0, e1, e2, e3 = (row_of(vector[at], row) for vector in (u0, u1, v2, v3))
            for g in range(at, groups):
                early = column[j][g] - (w0[g] * e0 + w1[g] * e1)
                if j < k + 8:
                    column[j][g] = early - ((y2[g] * e2 + y3[g] * e3) * guess2) * correction2
                else:
                    column[j][g] = early - (w2[g] * e2 + w3[g] * e3)
        schur, det_schur = s22 * r1, (det2 * r1) * r1
        root0, root1 = lax.rsqrt(a), lax.rsqrt(a * det1)
        root2, root3 = lax.rsqrt(schur) * r1, (lax.rsqrt(schur * det_schur) * r1) * r1
        for g in live:
            for i, value in enumerate((u0[g] * root0, n1[g] * root1, v2[g] * root2, n3[g] * root3)):
                lower[g] = jnp.where(lane == first + k + i, value, lower[g])
        t0, t1, t2, t3 = (row_of(block[home], sub + i) for i in range(4))
        t2 = det1 * t2 - (m20 * t0 + m21 * t1)
        t3 = det1 * t3 - (m30 * t0 + m31 * t1)
        for g in live:
            step = (w0[g] * t0 + w1[g] * t1) + (w2[g] * t2 + w3[g] * t3)
            if g == home:
                step = jnp.where(sublane > sub + 3, step, 0.0)
            block[g] = block[g] - step
        finals = (t0 * root0, (a * t1 - b * t0) * root1, t2 * root2, (s22 * t3 - s32 * t2) * root3)
        for i, value in enumerate(finals):
            block[home] = jnp.where(sublane == sub + i, value, block[home])
    for g in range(groups):
        keep = (lane <= first + sublane + g * GROUP) & inside
        lower[g] = jnp.where(keep, lower[g], 0.0)
    return jnp.concatenate(block, axis=0), jnp.concatenate(lower, axis=0)


def matmul(left, right):
    return jnp.dot(left, right, preferred_element_type=jnp.float32)


def stacked(value):
    high, low = split(value)
    return jnp.concatenate([high, high, low, jnp.zeros_like(high)], axis=0)


def rows_at(block):
    return pl.ds(pl.multiple_of(block * LANES, LANES), LANES)


def square_iota(axis):
    return lax.broadcasted_iota(jnp.int32, (LANES, LANES), axis)


def beyond_strip():
    return square_iota(1) // STRIP > square_iota(0) // STRIP


def eliminate_block(rows, lower_ref):
    lane = square_iota(1)
    done = [[] for _ in rows]
    for first in range(0, LANES, STRIP):
        last = first + STRIP
        solved, diagonal = eliminate_strip(rows[0][:STRIP], first)
        lower_ref[first:last, :] = diagonal
        in_strip = (lane[:STRIP] >= first) & (lane[:STRIP] < last)
        high, low = split(jnp.where(in_strip, solved, 0.0))
        high, low = high.astype(jnp.float32), low.astype(jnp.float32)
        inverse = high if first == 0 else pltpu.roll(high, LANES - first, 1)
        inverse += pltpu.roll(low, (LANES + STRIP - first) % LANES, 1) if first != STRIP else low
        inverse += pltpu.roll(high, (LANES + 2 * STRIP - first) % LANES, 1) if first != 2 * STRIP else high
        inverse = inverse.astype(jnp.bfloat16)
        strips = [solved] + [matmul(inverse, stacked(part[:STRIP])) for part in rows[1:]]
        for part, strip in zip(done, strips):
            part.append(strip)
        if last == LANES:
            break
        high, low = split(solved)
        wide = jnp.concatenate([high, low, high, jnp.zeros_like(high)], axis=0).astype(jnp.float32)
        left = wide.T[last:, :].astype(jnp.bfloat16)
        under = [part[STRIP:] for part in rows]
        inside = (lane[last:] >= first) & (lane[last:] < last)
        under[0] = jnp.where(inside, 0.0, under[0])
        rows = [part - matmul(left, stacked(strip)) for part, strip in zip(under, strips)]
    return [jnp.concatenate(part, axis=0) for part in done]


def assemble(me, own, mate, far, far_mate, work):
    size = own.shape[0]
    half = size // 2
    near = ((own, me), (mate, jnp.bitwise_xor(me, 1)))
    other = ((far, jnp.bitwise_xor(me, 2)), (far_mate, jnp.bitwise_xor(me, 3)))

    @pl.when(me < 2)
    def _():
        for part, column in near:
            work[column, :half, :] = part[:half, :].astype(jnp.float32)
            for block in range(half // LANES, size // LANES):
                flipped = part[block * LANES : (block + 1) * LANES, :].astype(jnp.float32).T
                work[block, rows_at(column), :] = flipped
        for part, column in other:
            work[column, half:size, :] = part[...].astype(jnp.float32)

    @pl.when(me >= 2)
    def _():
        for part, column in near:
            work[column, :size, :] = part[...].astype(jnp.float32)
        for part, column in other:
            work[column, :half, :] = part[...].astype(jnp.float32)


def first_kernel(axis, own, mate, far, far_mate, done_ref, lower_ref, work):
    count = lax.axis_size(axis)
    assemble(lax.axis_index(axis), own, mate, far, far_mate, work)
    done = eliminate_block([work[d, :LANES, :] for d in range(count)], lower_ref)
    for d in range(count):
        done_ref[d] = done[d]


def rest_kernel(
    axis, own, mate, far, far_mate, done_ref, first_lower, own_ref, high_ref, low_ref, work, lower
):
    count = lax.axis_size(axis)
    me = lax.axis_index(axis)
    lane, row = square_iota(1), square_iota(0)
    beyond = beyond_strip()
    assemble(me, own, mate, far, far_mate, work)
    work[:count, :LANES, :] = done_ref[...]
    lower[0] = first_lower[...]

    def block_step(q, carry):
        before = q - 1
        places = [lax.rem(before + d, count) for d in range(count)]
        rights = [work[place, rows_at(before), :] for place in places]
        rights[0] = jnp.where(beyond, 0.0, rights[0])
        rights = [split(right) for right in rights]

        def update(target):
            high, low = split(work[target, rows_at(before), :].T)
            both = jnp.concatenate([high, low], axis=1)
            new = []
            for d, (place, (right_high, right_low)) in enumerate(zip(places, rights)):
                product = matmul(both, jnp.concatenate([right_high, right_high], axis=0)) + matmul(high, right_low)
                new.append(-product if d == 0 else work[place, rows_at(target), :] - product)
            return new

        rows = update(q)
        for target in (q + 1, q + 2):
            for place, new in zip(places, update(target)):
                work[place, rows_at(target), :] = new
        done = eliminate_block(rows[1:] + rows[:1], lower.at[q])
        for place, part in zip(places[1:] + places[:1], done):
            work[place, rows_at(q), :] = part
        return carry

    lax.fori_loop(1, count, block_step, 0)

    for i in range(count):
        block = work[i, rows_at(me), :]
        upper = jnp.where((i > me) | ((i == me) & beyond), block, 0.0)
        own_ref[i * LANES : (i + 1) * LANES, :] = upper.T + jnp.where(i == me, lower[i], 0.0)
        for c in range(count):
            block = work[c, i * LANES : (i + 1) * LANES, :]
            if c > i:
                block = jnp.zeros_like(block)
            elif c == i:
                block = jnp.where(lane <= row, block, 0.0)
            high, low = split(block)
            high_ref[i * LANES : (i + 1) * LANES, c * LANES : (c + 1) * LANES] = high
            low_ref[i * LANES : (i + 1) * LANES, c * LANES : (c + 1) * LANES] = low


def solve_kernel(row_axis, col_axis, order, group_count, *refs):
    high_ref, low_ref = refs[:2]
    inputs = refs[2 : 3 + group_count]
    trailing_ref, own_ref, schur_ref, group, side = refs[3 + group_count :]
    size = high_ref.shape[0]
    half = size // 2
    share = own_ref.shape[1]
    count = side.shape[0] // share
    my_row, my_col = lax.axis_index(row_axis), lax.axis_index(col_axis)
    for i, ref in enumerate(inputs[:-1]):
        if order is None:
            group[...] = ref[...]
        else:
            for p in range(count):
                at = jnp.bitwise_xor(my_col, i * count + p) * share
                group[pl.ds(pl.multiple_of(at, share), share), :] = ref[p * share : (p + 1) * share, :]
    for p in range(count):
        place = jnp.bitwise_xor(my_row, p) if order else lax.rem(my_row + count - p, count)
        side[pl.ds(pl.multiple_of(place * share, share), share), :] = inputs[-1][p * share : (p + 1) * share, :]
    contract = (((1,), (1,)), ((), ()))

    def product(left, right):
        return lax.dot_general(left, right, contract, preferred_element_type=jnp.float32)

    def solve(rows):
        first = product(rows[:, :half], high_ref[:half, :half]) + product(rows[:, :half], low_ref[:half, :half])
        second = product(rows, high_ref[half:, :]) + product(rows, low_ref[half:, :])
        return jnp.concatenate([first, second], axis=1).astype(jnp.bfloat16)

    side[...] = solve(side[...])
    rows = group.shape[0]
    chunk = min(rows, 256)

    def step(i, carry):
        here = pl.ds(pl.multiple_of(i * chunk, chunk), chunk)
        solved = solve(group[here, :])
        group[here, :] = solved
        update = product(solved, side[...])
        schur_ref[here, :] = (trailing_ref[here, :].astype(jnp.float32) - update).astype(jnp.bfloat16)
        return carry

    if rows == chunk:
        step(0, 0)
    else:
        lax.fori_loop(0, rows // chunk, step, 0)
    own_ref[0] = group[pl.ds(pl.multiple_of(my_col * share, share), share), :]


def body(pivot_block, panel, lead, trailing):
    pivot_size, local_width = pivot_block.shape
    rows, cols = lax.axis_size("row"), lax.axis_size("col")
    share = panel.shape[1]
    col_index = lax.axis_index("col")
    vmem = pl.BlockSpec(memory_space=pltpu.VMEM)

    half = pivot_size // 2
    row_index = lax.axis_index("row")
    wide = pivot_block.astype(jnp.float32)
    diagonal_half = lax.dynamic_slice_in_dim(pivot_block, row_index // 2 * half, half, 0)
    far = lax.ppermute(diagonal_half, "row", [(d ^ 2, d) for d in range(rows)])
    far_mate = lax.ppermute(diagonal_half, "row", [(d ^ 3, d) for d in range(rows)])
    mate = lax.ppermute(pivot_block, "row", [(d ^ 1, d) for d in range(rows)])
    pivots = [wide, mate, far, far_mate]

    done, first_lower = pl.pallas_call(
        functools.partial(first_kernel, "row"),
        out_shape=(
            jax.ShapeDtypeStruct((rows, LANES, LANES), jnp.float32),
            jax.ShapeDtypeStruct((LANES, LANES), jnp.float32),
        ),
        in_specs=[vmem] * len(pivots),
        out_specs=(vmem,) * 2,
        scratch_shapes=[pltpu.VMEM((rows, pivot_size, LANES), jnp.float32)],
        compiler_params=pltpu.CompilerParams(vmem_limit_bytes=32 * 1024 * 1024),
        cost_estimate=pl.CostEstimate(flops=3 * 10**8, bytes_accessed=10**6, transcendentals=10**5),
        name="first",
    )(*pivots)

    def live(shards, rows_of):
        block = jnp.concatenate([(shard * share + jnp.arange(share)) // BLOCK for shard in shards])
        matches = block[:, None] == jnp.arange(lead.shape[1])[None, :]
        row_lead = jnp.sum(jnp.where(matches, lead, 0), axis=1)
        keep = (jnp.arange(pivot_size) // BLOCK)[None, :] >= row_lead[:, None]
        return jnp.where(keep, rows_of, jnp.zeros_like(rows_of))

    ratio = cols // rows
    paired = cols == 2 * rows and rows & (rows - 1) == 0

    def to_side(array, shift):
        pairs = []
        for r in range(rows):
            for c in range(cols):
                to_row, to_col = (c % rows + shift) % rows, r * ratio + c // rows
                pairs.append((c * rows + r, to_col * rows + to_row))
        return lax.ppermute(array, ("col", "row"), pairs)

    if paired:
        own_rows, _ = lax.optimization_barrier((panel[0], diagonal_half))
        quad = [panel[0]]
        for p in range(1, rows):
            if p == rows - 1:
                own_rows, _ = lax.optimization_barrier((own_rows, mate))
            quad.append(lax.ppermute(own_rows, "col", [(d ^ p, d) for d in range(cols)]))
        quad, _ = lax.optimization_barrier((quad, first_lower))
        quad = live([col_index ^ p for p in range(rows)], jnp.concatenate(quad, axis=0))
        group = [quad, lax.ppermute(quad, "col", [(d ^ rows, d) for d in range(cols)])]
        side = to_side(quad, 0)
    else:
        masked = live([col_index], panel[0])
        group = [lax.all_gather(masked, "col", axis=0, tiled=True)]
        side = jnp.concatenate([to_side(masked, s) for s in range(rows)], axis=0)

    own, high, low = pl.pallas_call(
        functools.partial(rest_kernel, "row"),
        out_shape=(
            jax.ShapeDtypeStruct((pivot_size, local_width), jnp.float32),
            jax.ShapeDtypeStruct((pivot_size, pivot_size), jnp.bfloat16),
            jax.ShapeDtypeStruct((pivot_size, pivot_size), jnp.bfloat16),
        ),
        in_specs=[vmem] * (len(pivots) + 2),
        out_specs=(vmem,) * 3,
        scratch_shapes=[
            pltpu.VMEM((rows + 2, pivot_size + 2 * LANES, LANES), jnp.float32),
            pltpu.VMEM((rows, LANES, LANES), jnp.float32),
        ],
        compiler_params=pltpu.CompilerParams(vmem_limit_bytes=32 * 1024 * 1024),
        cost_estimate=pl.CostEstimate(flops=10**9, bytes_accessed=2 * 10**6, transcendentals=10**5),
        name="rest",
    )(*pivots, done, first_lower)

    group_rows = share * cols
    panel_factor, schur = pl.pallas_call(
        functools.partial(solve_kernel, "row", "col", True if paired else None, len(group)),
        out_shape=(
            jax.ShapeDtypeStruct(panel.shape, jnp.bfloat16),
            jax.ShapeDtypeStruct(trailing.shape, jnp.bfloat16),
        ),
        in_specs=[vmem] * (4 + len(group)),
        out_specs=(vmem,) * 2,
        scratch_shapes=[
            pltpu.VMEM((group_rows, pivot_size), jnp.bfloat16),
            pltpu.VMEM((share * rows, pivot_size), jnp.bfloat16),
        ],
        compiler_params=pltpu.CompilerParams(vmem_limit_bytes=48 * 1024 * 1024),
        cost_estimate=pl.CostEstimate(flops=4 * 10**8, bytes_accessed=2 * 10**6, transcendentals=0),
        name="solve",
    )(high, low, *group, side, trailing)
    return (own, panel_factor, schur)


def solution(mesh):
    return jax.shard_map(
        body,
        mesh=mesh,
        in_specs=(P(None, "row"), P("row", "col", None), P("row", None), P("row", "col")),
        out_specs=(P(None, "row"), P("row", "col", None), P("row", "col")),
        check_vma=False,
    )
```

```python
import functools

import jax
import jax.numpy as jnp
from jax import lax
from jax.experimental import pallas as pl
from jax.experimental.pallas import tpu as pltpu
from jax.sharding import PartitionSpec as P

BLOCK = 128
STRIP = 32
SUB = 16
GROUP = 8
LANES = 128


def split(value):
    high = value.astype(jnp.bfloat16)
    low = (value - high.astype(jnp.float32)).astype(jnp.bfloat16)
    return high, low


def row_of(value, row):
    return jnp.broadcast_to(value[row : row + 1, :], (GROUP, LANES))


def reciprocal(value):
    guess = pl.reciprocal(value, approx=True)
    return guess, 2.0 - value * guess


def eliminate_strip(strip, first):
    groups = STRIP // GROUP
    sublane = lax.broadcasted_iota(jnp.int32, (GROUP, LANES), 0)
    lane = lax.broadcasted_iota(jnp.int32, (GROUP, LANES), 1)
    zero = jnp.zeros((GROUP, LANES), jnp.float32)
    block = [strip[g * GROUP : (g + 1) * GROUP, :] for g in range(groups)]
    inside = (lane >= first) & (lane < first + STRIP)
    lower = [zero] * groups
    column = [None] * STRIP
    for k in range(0, STRIP, 4):
        if k % SUB == 0:
            for j in range(k, k + SUB):
                column[j] = [
                    jnp.broadcast_to(block[g][:, first + j : first + j + 1], (GROUP, LANES)) if g >= j // GROUP else None
                    for g in range(groups)
                ]
            taken = (lane >= first + k) & (lane < first + k + SUB)
            for g in range(groups):
                identity = jnp.where(lane - first == sublane + g * GROUP, 1.0, 0.0)
                block[g] = jnp.where(taken, identity, block[g])
        last = k - k % SUB + SUB
        home, sub = k // GROUP, k % GROUP
        live = range(home, groups)
        u0, u1, u2, u3 = column[k : k + 4]

        def entry(i, j):
            return row_of(column[k + j][home], sub + i)

        a, b, c = entry(0, 0), entry(1, 0), entry(1, 1)
        p20, p21, p30, p31 = entry(2, 0), entry(2, 1), entry(3, 0), entry(3, 1)
        p22, p32, p33 = entry(2, 2), entry(3, 2), entry(3, 3)
        det1 = a * c - b * b
        m20, m21 = c * p20 - b * p21, a * p21 - b * p20
        m30, m31 = c * p30 - b * p31, a * p31 - b * p30
        s22 = det1 * p22 - (m20 * p20 + m21 * p21)
        s32 = det1 * p32 - (m30 * p20 + m31 * p21)
        s33 = det1 * p33 - (m30 * p30 + m31 * p31)
        det2 = s22 * s33 - s32 * s32
        guess1, correction1 = reciprocal(det1)
        guess2, correction2 = reciprocal(det2)
        r1 = guess1 * correction1
        n0 = {g: c * u0[g] - b * u1[g] for g in live}
        n1 = {g: a * u1[g] - b * u0[g] for g in live}
        v2 = {g: det1 * u2[g] - (n0[g] * p20 + n1[g] * p21) for g in live}
        v3 = {g: det1 * u3[g] - (n0[g] * p30 + n1[g] * p31) for g in live}
        n2 = {g: s33 * v2[g] - s32 * v3[g] for g in live}
        n3 = {g: s22 * v3[g] - s32 * v2[g] for g in live}
        w0 = {g: n0[g] * r1 for g in live}
        w1 = {g: n1[g] * r1 for g in live}
        y2 = {g: n2[g] * r1 for g in live}
        y3 = {g: n3[g] * r1 for g in live}
        w2 = {g: (y2[g] * guess2) * correction2 for g in live}
        w3 = {g: (y3[g] * guess2) * correction2 for g in live}
        for j in range(k + 4, last):
            at, row = j // GROUP, j % GROUP
            e0, e1, e2, e3 = (row_of(vector[at], row) for vector in (u0, u1, v2, v3))
            for g in range(at, groups):
                early = column[j][g] - (w0[g] * e0 + w1[g] * e1)
                if j < k + 8:
                    column[j][g] = early - ((y2[g] * e2 + y3[g] * e3) * guess2) * correction2
                else:
                    column[j][g] = early - (w2[g] * e2 + w3[g] * e3)
        schur, det_schur = s22 * r1, (det2 * r1) * r1
        root0, root1 = lax.rsqrt(a), lax.rsqrt(a * det1)
        root2, root3 = lax.rsqrt(schur) * r1, (lax.rsqrt(schur * det_schur) * r1) * r1
        for g in live:
            for i, value in enumerate((u0[g] * root0, n1[g] * root1, v2[g] * root2, n3[g] * root3)):
                lower[g] = jnp.where(lane == first + k + i, value, lower[g])
        t0, t1, t2, t3 = (row_of(block[home], sub + i) for i in range(4))
        t2 = det1 * t2 - (m20 * t0 + m21 * t1)
        t3 = det1 * t3 - (m30 * t0 + m31 * t1)
        for g in live:
            step = (w0[g] * t0 + w1[g] * t1) + (w2[g] * t2 + w3[g] * t3)
            if g == home:
                step = jnp.where(sublane > sub + 3, step, 0.0)
            block[g] = block[g] - step
        finals = (t0 * root0, (a * t1 - b * t0) * root1, t2 * root2, (s22 * t3 - s32 * t2) * root3)
        for i, value in enumerate(finals):
            block[home] = jnp.where(sublane == sub + i, value, block[home])
    for g in range(groups):
        keep = (lane <= first + sublane + g * GROUP) & inside
        lower[g] = jnp.where(keep, lower[g], 0.0)
    return jnp.concatenate(block, axis=0), jnp.concatenate(lower, axis=0)


def matmul(left, right):
    return jnp.dot(left, right, preferred_element_type=jnp.float32)


def stacked(value):
    high, low = split(value)
    return jnp.concatenate([high, high, low, jnp.zeros_like(high)], axis=0)


def rows_at(block):
    return pl.ds(pl.multiple_of(block * LANES, LANES), LANES)


def square_iota(axis):
    return lax.broadcasted_iota(jnp.int32, (LANES, LANES), axis)


def beyond_strip():
    return square_iota(1) // STRIP > square_iota(0) // STRIP


def eliminate_block(rows, lower_ref):
    lane = square_iota(1)
    done = [[] for _ in rows]
    for first in range(0, LANES, STRIP):
        last = first + STRIP
        solved, diagonal = eliminate_strip(rows[0][:STRIP], first)
        lower_ref[first:last, :] = diagonal
        in_strip = (lane[:STRIP] >= first) & (lane[:STRIP] < last)
        high, low = split(jnp.where(in_strip, solved, 0.0))
        high, low = high.astype(jnp.float32), low.astype(jnp.float32)
        inverse = high if first == 0 else pltpu.roll(high, LANES - first, 1)
        inverse += pltpu.roll(low, (LANES + STRIP - first) % LANES, 1) if first != STRIP else low
        inverse += pltpu.roll(high, (LANES + 2 * STRIP - first) % LANES, 1) if first != 2 * STRIP else high
        inverse = inverse.astype(jnp.bfloat16)
        strips = [solved] + [matmul(inverse, stacked(part[:STRIP])) for part in rows[1:]]
        for part, strip in zip(done, strips):
            part.append(strip)
        if last == LANES:
            break
        high, low = split(solved)
        wide = jnp.concatenate([high, low, high, jnp.zeros_like(high)], axis=0).astype(jnp.float32)
        left = wide.T[last:, :].astype(jnp.bfloat16)
        under = [part[STRIP:] for part in rows]
        inside = (lane[last:] >= first) & (lane[last:] < last)
        under[0] = jnp.where(inside, 0.0, under[0])
        rows = [part - matmul(left, stacked(strip)) for part, strip in zip(under, strips)]
    return [jnp.concatenate(part, axis=0) for part in done]


def assemble(me, own, mate, far, far_mate, work):
    size = own.shape[0]
    half = size // 2
    near = ((own, me), (mate, jnp.bitwise_xor(me, 1)))
    other = ((far, jnp.bitwise_xor(me, 2)), (far_mate, jnp.bitwise_xor(me, 3)))

    @pl.when(me < 2)
    def _():
        for part, column in near:
            work[column, :half, :] = part[:half, :].astype(jnp.float32)
            for block in range(half // LANES, size // LANES):
                flipped = part[block * LANES : (block + 1) * LANES, :].astype(jnp.float32).T
                work[block, rows_at(column), :] = flipped
        for part, column in other:
            work[column, half:size, :] = part[...].astype(jnp.float32)

    @pl.when(me >= 2)
    def _():
        for part, column in near:
            work[column, :size, :] = part[...].astype(jnp.float32)
        for part, column in other:
            work[column, :half, :] = part[...].astype(jnp.float32)


def first_kernel(axis, own, mate, far, far_mate, done_ref, lower_ref, work):
    count = lax.axis_size(axis)
    assemble(lax.axis_index(axis), own, mate, far, far_mate, work)
    done = eliminate_block([work[d, :LANES, :] for d in range(count)], lower_ref)
    for d in range(count):
        done_ref[d] = done[d]


def rest_kernel(
    axis, own, mate, far, far_mate, done_ref, first_lower, own_ref, high_ref, low_ref, work, lower
):
    count = lax.axis_size(axis)
    me = lax.axis_index(axis)
    lane, row = square_iota(1), square_iota(0)
    beyond = beyond_strip()
    assemble(me, own, mate, far, far_mate, work)
    work[:count, :LANES, :] = done_ref[...]
    lower[0] = first_lower[...]

    def block_step(q, carry):
        before = q - 1
        places = [lax.rem(before + d, count) for d in range(count)]
        rights = [work[place, rows_at(before), :] for place in places]
        rights[0] = jnp.where(beyond, 0.0, rights[0])
        rights = [split(right) for right in rights]

        def update(target):
            high, low = split(work[target, rows_at(before), :].T)
            both = jnp.concatenate([high, low], axis=1)
            new = []
            for d, (place, (right_high, right_low)) in enumerate(zip(places, rights)):
                product = matmul(both, jnp.concatenate([right_high, right_high], axis=0)) + matmul(high, right_low)
                new.append(-product if d == 0 else work[place, rows_at(target), :] - product)
            return new

        rows = update(q)
        for target in (q + 1, q + 2):
            for place, new in zip(places, update(target)):
                work[place, rows_at(target), :] = new
        done = eliminate_block(rows[1:] + rows[:1], lower.at[q])
        for place, part in zip(places[1:] + places[:1], done):
            work[place, rows_at(q), :] = part
        return carry

    lax.fori_loop(1, count, block_step, 0)

    for i in range(count):
        block = work[i, rows_at(me), :]
        upper = jnp.where((i > me) | ((i == me) & beyond), block, 0.0)
        own_ref[i * LANES : (i + 1) * LANES, :] = upper.T + jnp.where(i == me, lower[i], 0.0)
        for c in range(count):
            block = work[c, i * LANES : (i + 1) * LANES, :]
            if c > i:
                block = jnp.zeros_like(block)
            elif c == i:
                block = jnp.where(lane <= row, block, 0.0)
            high, low = split(block)
            high_ref[i * LANES : (i + 1) * LANES, c * LANES : (c + 1) * LANES] = high
            low_ref[i * LANES : (i + 1) * LANES, c * LANES : (c + 1) * LANES] = low


def solve_kernel(row_axis, col_axis, order, group_count, *refs):
    high_ref, low_ref = refs[:2]
    inputs = refs[2 : 3 + group_count]
    trailing_ref, own_ref, schur_ref, group, side = refs[3 + group_count :]
    size = high_ref.shape[0]
    half = size // 2
    share = own_ref.shape[1]
    count = side.shape[0] // share
    my_row, my_col = lax.axis_index(row_axis), lax.axis_index(col_axis)
    for i, ref in enumerate(inputs[:-1]):
        if order is None:
            group[...] = ref[...]
        else:
            for p in range(count):
                at = jnp.bitwise_xor(my_col, i * count + p) * share
                group[pl.ds(pl.multiple_of(at, share), share), :] = ref[p * share : (p + 1) * share, :]
    for p in range(count):
        place = jnp.bitwise_xor(my_row, p) if order else lax.rem(my_row + count - p, count)
        side[pl.ds(pl.multiple_of(place * share, share), share), :] = inputs[-1][p * share : (p + 1) * share, :]
    contract = (((1,), (1,)), ((), ()))

    def product(left, right):
        return lax.dot_general(left, right, contract, preferred_element_type=jnp.float32)

    def solve(rows):
        first = product(rows[:, :half], high_ref[:half, :half]) + product(rows[:, :half], low_ref[:half, :half])
        second = product(rows, high_ref[half:, :]) + product(rows, low_ref[half:, :])
        return jnp.concatenate([first, second], axis=1).astype(jnp.bfloat16)

    side[...] = solve(side[...])
    rows = group.shape[0]
    chunk = min(rows, 256)

    def step(i, carry):
        here = pl.ds(pl.multiple_of(i * chunk, chunk), chunk)
        solved = solve(group[here, :])
        group[here, :] = solved
        update = product(solved, side[...])
        schur_ref[here, :] = (trailing_ref[here, :].astype(jnp.float32) - update).astype(jnp.bfloat16)
        return carry

    if rows == chunk:
        step(0, 0)
    else:
        lax.fori_loop(0, rows // chunk, step, 0)
    own_ref[0] = group[pl.ds(pl.multiple_of(my_col * share, share), share), :]


def body(pivot_block, panel, lead, trailing):
    pivot_size, local_width = pivot_block.shape
    rows, cols = lax.axis_size("row"), lax.axis_size("col")
    share = panel.shape[1]
    col_index = lax.axis_index("col")
    vmem = pl.BlockSpec(memory_space=pltpu.VMEM)

    half = pivot_size // 2
    row_index = lax.axis_index("row")
    wide = pivot_block.astype(jnp.float32)
    diagonal_half = lax.dynamic_slice_in_dim(pivot_block, row_index // 2 * half, half, 0)
    far = lax.ppermute(diagonal_half, "row", [(d ^ 2, d) for d in range(rows)])
    far_mate = lax.ppermute(diagonal_half, "row", [(d ^ 3, d) for d in range(rows)])
    mate = lax.ppermute(pivot_block, "row", [(d ^ 1, d) for d in range(rows)])
    pivots = [wide, mate, far, far_mate]

    done, first_lower = pl.pallas_call(
        functools.partial(first_kernel, "row"),
        out_shape=(
            jax.ShapeDtypeStruct((rows, LANES, LANES), jnp.float32),
            jax.ShapeDtypeStruct((LANES, LANES), jnp.float32),
        ),
        in_specs=[vmem] * len(pivots),
        out_specs=(vmem,) * 2,
        scratch_shapes=[pltpu.VMEM((rows, pivot_size, LANES), jnp.float32)],
        compiler_params=pltpu.CompilerParams(vmem_limit_bytes=32 * 1024 * 1024),
        cost_estimate=pl.CostEstimate(flops=3 * 10**8, bytes_accessed=10**6, transcendentals=10**5),
        name="first",
    )(*pivots)

    def live(shards, rows_of):
        block = jnp.concatenate([(shard * share + jnp.arange(share)) // BLOCK for shard in shards])
        matches = block[:, None] == jnp.arange(lead.shape[1])[None, :]
        row_lead = jnp.sum(jnp.where(matches, lead, 0), axis=1)
        keep = (jnp.arange(pivot_size) // BLOCK)[None, :] >= row_lead[:, None]
        return jnp.where(keep, rows_of, jnp.zeros_like(rows_of))

    ratio = cols // rows
    paired = cols == 2 * rows and rows & (rows - 1) == 0

    def to_side(array, shift):
        pairs = []
        for r in range(rows):
            for c in range(cols):
                to_row, to_col = (c % rows + shift) % rows, r * ratio + c // rows
                pairs.append((c * rows + r, to_col * rows + to_row))
        return lax.ppermute(array, ("col", "row"), pairs)

    if paired:
        quad, _ = lax.optimization_barrier((panel[0], diagonal_half))
        step = 1
        while step < rows:
            pieces = (quad, lax.ppermute(quad, "col", [(d ^ step, d) for d in range(cols)]))
            step *= 2
            if step == rows:
                pieces, _ = lax.optimization_barrier((pieces, first_lower))
            quad = jnp.concatenate(pieces, axis=0)
        quad = live([col_index ^ p for p in range(rows)], quad)
        group = [quad, lax.ppermute(quad, "col", [(d ^ rows, d) for d in range(cols)])]
        side = to_side(quad, 0)
    else:
        masked = live([col_index], panel[0])
        group = [lax.all_gather(masked, "col", axis=0, tiled=True)]
        side = jnp.concatenate([to_side(masked, s) for s in range(rows)], axis=0)

    own, high, low = pl.pallas_call(
        functools.partial(rest_kernel, "row"),
        out_shape=(
            jax.ShapeDtypeStruct((pivot_size, local_width), jnp.float32),
            jax.ShapeDtypeStruct((pivot_size, pivot_size), jnp.bfloat16),
            jax.ShapeDtypeStruct((pivot_size, pivot_size), jnp.bfloat16),
        ),
        in_specs=[vmem] * (len(pivots) + 2),
        out_specs=(vmem,) * 3,
        scratch_shapes=[
            pltpu.VMEM((rows + 2, pivot_size + 2 * LANES, LANES), jnp.float32),
            pltpu.VMEM((rows, LANES, LANES), jnp.float32),
        ],
        compiler_params=pltpu.CompilerParams(vmem_limit_bytes=32 * 1024 * 1024),
        cost_estimate=pl.CostEstimate(flops=10**9, bytes_accessed=2 * 10**6, transcendentals=10**5),
        name="rest",
    )(*pivots, done, first_lower)

    group_rows = share * cols
    panel_factor, schur = pl.pallas_call(
        functools.partial(solve_kernel, "row", "col", True if paired else None, len(group)),
        out_shape=(
            jax.ShapeDtypeStruct(panel.shape, jnp.bfloat16),
            jax.ShapeDtypeStruct(trailing.shape, jnp.bfloat16),
        ),
        in_specs=[vmem] * (4 + len(group)),
        out_specs=(vmem,) * 2,
        scratch_shapes=[
            pltpu.VMEM((group_rows, pivot_size), jnp.bfloat16),
            pltpu.VMEM((share * rows, pivot_size), jnp.bfloat16),
        ],
        compiler_params=pltpu.CompilerParams(vmem_limit_bytes=48 * 1024 * 1024),
        cost_estimate=pl.CostEstimate(flops=4 * 10**8, bytes_accessed=2 * 10**6, transcendentals=0),
        name="solve",
    )(high, low, *group, side, trailing)
    return (own, panel_factor, schur)


def solution(mesh):
    return jax.shard_map(
        body,
        mesh=mesh,
        in_specs=(P(None, "row"), P("row", "col", None), P("row", None), P("row", "col")),
        out_specs=(P(None, "row"), P("row", "col", None), P("row", "col")),
        check_vma=False,
    )
```

```python
import functools

import jax
import jax.numpy as jnp
from jax import lax
from jax.experimental import pallas as pl
from jax.experimental.pallas import tpu as pltpu
from jax.sharding import PartitionSpec as P

BLOCK = 128
STRIP = 32
SUB = 16
GROUP = 8
LANES = 128


def split(value):
    high = value.astype(jnp.bfloat16)
    low = (value - high.astype(jnp.float32)).astype(jnp.bfloat16)
    return high, low


def row_of(value, row):
    return jnp.broadcast_to(value[row : row + 1, :], (GROUP, LANES))


def reciprocal(value):
    guess = pl.reciprocal(value, approx=True)
    return guess, 2.0 - value * guess


def eliminate_strip(strip, first):
    groups = STRIP // GROUP
    sublane = lax.broadcasted_iota(jnp.int32, (GROUP, LANES), 0)
    lane = lax.broadcasted_iota(jnp.int32, (GROUP, LANES), 1)
    zero = jnp.zeros((GROUP, LANES), jnp.float32)
    block = [strip[g * GROUP : (g + 1) * GROUP, :] for g in range(groups)]
    inside = (lane >= first) & (lane < first + STRIP)
    lower = [zero] * groups
    column = [None] * STRIP
    for k in range(0, STRIP, 2):
        if k % SUB == 0:
            for j in range(k, k + SUB):
                column[j] = [
                    jnp.broadcast_to(block[g][:, first + j : first + j + 1], (GROUP, LANES)) if g >= j // GROUP else None
                    for g in range(groups)
                ]
            taken = (lane >= first + k) & (lane < first + k + SUB)
            for g in range(groups):
                identity = jnp.where(lane - first == sublane + g * GROUP, 1.0, 0.0)
                block[g] = jnp.where(taken, identity, block[g])
        last = k - k % SUB + SUB
        home, sub = k // GROUP, k % GROUP
        u, v = column[k], column[k + 1]
        a = row_of(u[home], sub)
        b = row_of(u[home], sub + 1)
        c = row_of(v[home], sub + 1)
        det = a * c - b * b
        guess, correction = reciprocal(det)
        n1 = [None if g < home else c * u[g] - b * v[g] for g in range(groups)]
        n2 = [None if g < home else a * v[g] - b * u[g] for g in range(groups)]
        w1 = [None if g < home else (n1[g] * guess) * correction for g in range(groups)]
        w2 = [None if g < home else (n2[g] * guess) * correction for g in range(groups)]
        for j in range(k + 2, last):
            at, row = j // GROUP, j % GROUP
            uj, vj = row_of(u[at], row), row_of(v[at], row)
            for g in range(at, groups):
                if j < k + 4:
                    step = ((n1[g] * uj + n2[g] * vj) * guess) * correction
                else:
                    step = w1[g] * uj + w2[g] * vj
                column[j][g] = column[j][g] - step
        root_a = lax.rsqrt(a)
        root_d = lax.rsqrt(a * det)
        for g in range(home, groups):
            lower[g] = jnp.where(lane == first + k, u[g] * root_a, lower[g])
            lower[g] = jnp.where(lane == first + k + 1, n2[g] * root_d, lower[g])
        below = sublane > sub + 1
        w1[home] = jnp.where(below, w1[home], 0.0)
        w2[home] = jnp.where(below, w2[home], 0.0)
        t0, t1 = row_of(block[home], sub), row_of(block[home], sub + 1)
        for g in range(home, groups):
            block[g] = block[g] - (w1[g] * t0 + w2[g] * t1)
        block[home] = jnp.where(sublane == sub, t0 * root_a, block[home])
        block[home] = jnp.where(sublane == sub + 1, (a * t1 - b * t0) * root_d, block[home])
    for g in range(groups):
        keep = (lane <= first + sublane + g * GROUP) & inside
        lower[g] = jnp.where(keep, lower[g], 0.0)
    return jnp.concatenate(block, axis=0), jnp.concatenate(lower, axis=0)


def matmul(left, right):
    return jnp.dot(left, right, preferred_element_type=jnp.float32)


def stacked(value):
    high, low = split(value)
    return jnp.concatenate([high, high, low, jnp.zeros_like(high)], axis=0)


def rows_at(block):
    return pl.ds(pl.multiple_of(block * LANES, LANES), LANES)


def square_iota(axis):
    return lax.broadcasted_iota(jnp.int32, (LANES, LANES), axis)


def beyond_strip():
    return square_iota(1) // STRIP > square_iota(0) // STRIP


def eliminate_block(rows, lower_ref):
    lane = square_iota(1)
    done = [[] for _ in rows]
    for first in range(0, LANES, STRIP):
        last = first + STRIP
        solved, diagonal = eliminate_strip(rows[0][:STRIP], first)
        lower_ref[first:last, :] = diagonal
        in_strip = (lane[:STRIP] >= first) & (lane[:STRIP] < last)
        high, low = split(jnp.where(in_strip, solved, 0.0))
        high, low = high.astype(jnp.float32), low.astype(jnp.float32)
        inverse = high if first == 0 else pltpu.roll(high, LANES - first, 1)
        inverse += pltpu.roll(low, (LANES + STRIP - first) % LANES, 1) if first != STRIP else low
        inverse += pltpu.roll(high, (LANES + 2 * STRIP - first) % LANES, 1) if first != 2 * STRIP else high
        inverse = inverse.astype(jnp.bfloat16)
        strips = [solved] + [matmul(inverse, stacked(part[:STRIP])) for part in rows[1:]]
        for part, strip in zip(done, strips):
            part.append(strip)
        if last == LANES:
            break
        high, low = split(solved)
        wide = jnp.concatenate([high, low, high, jnp.zeros_like(high)], axis=0).astype(jnp.float32)
        left = wide.T[last:, :].astype(jnp.bfloat16)
        under = [part[STRIP:] for part in rows]
        inside = (lane[last:] >= first) & (lane[last:] < last)
        under[0] = jnp.where(inside, 0.0, under[0])
        rows = [part - matmul(left, stacked(strip)) for part, strip in zip(under, strips)]
    return [jnp.concatenate(part, axis=0) for part in done]


def assemble(me, own, mate, far, far_mate, work):
    size = own.shape[0]
    half = size // 2
    near = ((own, me), (mate, jnp.bitwise_xor(me, 1)))
    other = ((far, jnp.bitwise_xor(me, 2)), (far_mate, jnp.bitwise_xor(me, 3)))

    @pl.when(me < 2)
    def _():
        for part, column in near:
            work[column, :half, :] = part[:half, :].astype(jnp.float32)
            for block in range(half // LANES, size // LANES):
                flipped = part[block * LANES : (block + 1) * LANES, :].astype(jnp.float32).T
                work[block, rows_at(column), :] = flipped
        for part, column in other:
            work[column, half:size, :] = part[...].astype(jnp.float32)

    @pl.when(me >= 2)
    def _():
        for part, column in near:
            work[column, :size, :] = part[...].astype(jnp.float32)
        for part, column in other:
            work[column, :half, :] = part[...].astype(jnp.float32)


def first_kernel(axis, own, mate, far, far_mate, done_ref, lower_ref, work):
    count = lax.axis_size(axis)
    assemble(lax.axis_index(axis), own, mate, far, far_mate, work)
    done = eliminate_block([work[d, :LANES, :] for d in range(count)], lower_ref)
    for d in range(count):
        done_ref[d] = done[d]


def rest_kernel(
    axis, own, mate, far, far_mate, done_ref, first_lower, own_ref, high_ref, low_ref, work, lower
):
    count = lax.axis_size(axis)
    me = lax.axis_index(axis)
    lane, row = square_iota(1), square_iota(0)
    beyond = beyond_strip()
    assemble(me, own, mate, far, far_mate, work)
    work[:count, :LANES, :] = done_ref[...]
    lower[0] = first_lower[...]

    def block_step(q, carry):
        before = q - 1
        places = [lax.rem(before + d, count) for d in range(count)]
        rights = [work[place, rows_at(before), :] for place in places]
        rights[0] = jnp.where(beyond, 0.0, rights[0])
        rights = [split(right) for right in rights]

        def update(target):
            high, low = split(work[target, rows_at(before), :].T)
            both = jnp.concatenate([high, low], axis=1)
            new = []
            for d, (place, (right_high, right_low)) in enumerate(zip(places, rights)):
                product = matmul(both, jnp.concatenate([right_high, right_high], axis=0)) + matmul(high, right_low)
                new.append(-product if d == 0 else work[place, rows_at(target), :] - product)
            return new

        rows = update(q)
        for target in (q + 1, q + 2):
            for place, new in zip(places, update(target)):
                work[place, rows_at(target), :] = new
        done = eliminate_block(rows[1:] + rows[:1], lower.at[q])
        for place, part in zip(places[1:] + places[:1], done):
            work[place, rows_at(q), :] = part
        return carry

    lax.fori_loop(1, count, block_step, 0)

    for i in range(count):
        block = work[i, rows_at(me), :]
        upper = jnp.where((i > me) | ((i == me) & beyond), block, 0.0)
        own_ref[i * LANES : (i + 1) * LANES, :] = upper.T + jnp.where(i == me, lower[i], 0.0)
        for c in range(count):
            block = work[c, i * LANES : (i + 1) * LANES, :]
            if c > i:
                block = jnp.zeros_like(block)
            elif c == i:
                block = jnp.where(lane <= row, block, 0.0)
            high, low = split(block)
            high_ref[i * LANES : (i + 1) * LANES, c * LANES : (c + 1) * LANES] = high
            low_ref[i * LANES : (i + 1) * LANES, c * LANES : (c + 1) * LANES] = low


def solve_kernel(row_axis, col_axis, order, group_count, *refs):
    high_ref, low_ref = refs[:2]
    inputs = refs[2 : 3 + group_count]
    trailing_ref, own_ref, schur_ref, group, side = refs[3 + group_count :]
    size = high_ref.shape[0]
    half = size // 2
    share = own_ref.shape[1]
    count = side.shape[0] // share
    my_row, my_col = lax.axis_index(row_axis), lax.axis_index(col_axis)
    for i, ref in enumerate(inputs[:-1]):
        if order is None:
            group[...] = ref[...]
        else:
            for p in range(count):
                at = jnp.bitwise_xor(my_col, i * count + p) * share
                group[pl.ds(pl.multiple_of(at, share), share), :] = ref[p * share : (p + 1) * share, :]
    for p in range(count):
        place = jnp.bitwise_xor(my_row, p) if order else lax.rem(my_row + count - p, count)
        side[pl.ds(pl.multiple_of(place * share, share), share), :] = inputs[-1][p * share : (p + 1) * share, :]
    contract = (((1,), (1,)), ((), ()))

    def product(left, right):
        return lax.dot_general(left, right, contract, preferred_element_type=jnp.float32)

    def solve(rows):
        first = product(rows[:, :half], high_ref[:half, :half]) + product(rows[:, :half], low_ref[:half, :half])
        second = product(rows, high_ref[half:, :]) + product(rows, low_ref[half:, :])
        return jnp.concatenate([first, second], axis=1).astype(jnp.bfloat16)

    side[...] = solve(side[...])
    rows = group.shape[0]
    chunk = min(rows, 256)

    def step(i, carry):
        here = pl.ds(pl.multiple_of(i * chunk, chunk), chunk)
        solved = solve(group[here, :])
        group[here, :] = solved
        update = product(solved, side[...])
        schur_ref[here, :] = (trailing_ref[here, :].astype(jnp.float32) - update).astype(jnp.bfloat16)
        return carry

    if rows == chunk:
        step(0, 0)
    else:
        lax.fori_loop(0, rows // chunk, step, 0)
    own_ref[0] = group[pl.ds(pl.multiple_of(my_col * share, share), share), :]


def body(pivot_block, panel, lead, trailing):
    pivot_size, local_width = pivot_block.shape
    rows, cols = lax.axis_size("row"), lax.axis_size("col")
    share = panel.shape[1]
    col_index = lax.axis_index("col")
    vmem = pl.BlockSpec(memory_space=pltpu.VMEM)

    half = pivot_size // 2
    row_index = lax.axis_index("row")
    wide = pivot_block.astype(jnp.float32)
    diagonal_half = lax.dynamic_slice_in_dim(pivot_block, row_index // 2 * half, half, 0)
    far = lax.ppermute(diagonal_half, "row", [(d ^ 2, d) for d in range(rows)])
    far_mate = lax.ppermute(diagonal_half, "row", [(d ^ 3, d) for d in range(rows)])
    mate = lax.ppermute(pivot_block, "row", [(d ^ 1, d) for d in range(rows)])
    pivots = [wide, mate, far, far_mate]

    done, first_lower = pl.pallas_call(
        functools.partial(first_kernel, "row"),
        out_shape=(
            jax.ShapeDtypeStruct((rows, LANES, LANES), jnp.float32),
            jax.ShapeDtypeStruct((LANES, LANES), jnp.float32),
        ),
        in_specs=[vmem] * len(pivots),
        out_specs=(vmem,) * 2,
        scratch_shapes=[pltpu.VMEM((rows, pivot_size, LANES), jnp.float32)],
        compiler_params=pltpu.CompilerParams(vmem_limit_bytes=32 * 1024 * 1024),
        cost_estimate=pl.CostEstimate(flops=3 * 10**8, bytes_accessed=10**6, transcendentals=10**5),
        name="first",
    )(*pivots)

    def live(shards, rows_of):
        block = jnp.concatenate([(shard * share + jnp.arange(share)) // BLOCK for shard in shards])
        matches = block[:, None] == jnp.arange(lead.shape[1])[None, :]
        row_lead = jnp.sum(jnp.where(matches, lead, 0), axis=1)
        keep = (jnp.arange(pivot_size) // BLOCK)[None, :] >= row_lead[:, None]
        return jnp.where(keep, rows_of, jnp.zeros_like(rows_of))

    ratio = cols // rows
    paired = cols == 2 * rows and rows & (rows - 1) == 0

    def to_side(array, shift):
        pairs = []
        for r in range(rows):
            for c in range(cols):
                to_row, to_col = (c % rows + shift) % rows, r * ratio + c // rows
                pairs.append((c * rows + r, to_col * rows + to_row))
        return lax.ppermute(array, ("col", "row"), pairs)

    if paired:
        quad, _ = lax.optimization_barrier((panel[0], diagonal_half))
        step = 1
        while step < rows:
            pieces = (quad, lax.ppermute(quad, "col", [(d ^ step, d) for d in range(cols)]))
            step *= 2
            if step == rows:
                pieces, _ = lax.optimization_barrier((pieces, first_lower))
            quad = jnp.concatenate(pieces, axis=0)
        quad = live([col_index ^ p for p in range(rows)], quad)
        group = [quad, lax.ppermute(quad, "col", [(d ^ rows, d) for d in range(cols)])]
        side = to_side(quad, 0)
    else:
        masked = live([col_index], panel[0])
        group = [lax.all_gather(masked, "col", axis=0, tiled=True)]
        side = jnp.concatenate([to_side(masked, s) for s in range(rows)], axis=0)

    own, high, low = pl.pallas_call(
        functools.partial(rest_kernel, "row"),
        out_shape=(
            jax.ShapeDtypeStruct((pivot_size, local_width), jnp.float32),
            jax.ShapeDtypeStruct((pivot_size, pivot_size), jnp.bfloat16),
            jax.ShapeDtypeStruct((pivot_size, pivot_size), jnp.bfloat16),
        ),
        in_specs=[vmem] * (len(pivots) + 2),
        out_specs=(vmem,) * 3,
        scratch_shapes=[
            pltpu.VMEM((rows + 2, pivot_size + 2 * LANES, LANES), jnp.float32),
            pltpu.VMEM((rows, LANES, LANES), jnp.float32),
        ],
        compiler_params=pltpu.CompilerParams(vmem_limit_bytes=32 * 1024 * 1024),
        cost_estimate=pl.CostEstimate(flops=10**9, bytes_accessed=2 * 10**6, transcendentals=10**5),
        name="rest",
    )(*pivots, done, first_lower)

    group_rows = share * cols
    panel_factor, schur = pl.pallas_call(
        functools.partial(solve_kernel, "row", "col", True if paired else None, len(group)),
        out_shape=(
            jax.ShapeDtypeStruct(panel.shape, jnp.bfloat16),
            jax.ShapeDtypeStruct(trailing.shape, jnp.bfloat16),
        ),
        in_specs=[vmem] * (4 + len(group)),
        out_specs=(vmem,) * 2,
        scratch_shapes=[
            pltpu.VMEM((group_rows, pivot_size), jnp.bfloat16),
            pltpu.VMEM((share * rows, pivot_size), jnp.bfloat16),
        ],
        compiler_params=pltpu.CompilerParams(vmem_limit_bytes=48 * 1024 * 1024),
        cost_estimate=pl.CostEstimate(flops=4 * 10**8, bytes_accessed=2 * 10**6, transcendentals=0),
        name="solve",
    )(high, low, *group, side, trailing)
    return (own, panel_factor, schur)


def solution(mesh):
    return jax.shard_map(
        body,
        mesh=mesh,
        in_specs=(P(None, "row"), P("row", "col", None), P("row", None), P("row", "col")),
        out_specs=(P(None, "row"), P("row", "col", None), P("row", "col")),
        check_vma=False,
    )
```

```python
import functools

import jax
import jax.numpy as jnp
from jax import lax
from jax.experimental import pallas as pl
from jax.experimental.pallas import tpu as pltpu
from jax.sharding import PartitionSpec as P

BLOCK = 128
STRIP = 32
SUB = 8
GROUP = 8
LANES = 128


def split(value):
    high = value.astype(jnp.bfloat16)
    low = (value - high.astype(jnp.float32)).astype(jnp.bfloat16)
    return high, low


def row_of(value, row):
    return jnp.broadcast_to(value[row : row + 1, :], (GROUP, LANES))


def reciprocal(value):
    guess = pl.reciprocal(value, approx=True)
    return guess, 2.0 - value * guess


def eliminate_strip(strip, first):
    groups = STRIP // GROUP
    sublane = lax.broadcasted_iota(jnp.int32, (GROUP, LANES), 0)
    lane = lax.broadcasted_iota(jnp.int32, (GROUP, LANES), 1)
    block = [strip[g * GROUP : (g + 1) * GROUP, :] for g in range(groups)]
    column = [None] * STRIP
    for k in range(0, STRIP, 2):
        if k % SUB == 0:
            for j in range(k, k + SUB):
                column[j] = [
                    jnp.broadcast_to(block[g][:, first + j : first + j + 1], (GROUP, LANES)) if g >= j // GROUP else None
                    for g in range(groups)
                ]
            taken = (lane >= first + k) & (lane < first + k + SUB)
            for g in range(groups):
                identity = jnp.where(lane - first == sublane + g * GROUP, 1.0, 0.0)
                block[g] = jnp.where(taken, identity, block[g])
        last = k - k % SUB + SUB
        home, sub = k // GROUP, k % GROUP
        u, v = column[k], column[k + 1]
        a = row_of(u[home], sub)
        b = row_of(u[home], sub + 1)
        c = row_of(v[home], sub + 1)
        det = a * c - b * b
        guess, correction = reciprocal(det)
        n1 = [None if g < home else c * u[g] - b * v[g] for g in range(groups)]
        n2 = [None if g < home else a * v[g] - b * u[g] for g in range(groups)]
        inverse = guess * correction
        w1 = [None if g < home else n1[g] * inverse for g in range(groups)]
        w2 = [None if g < home else n2[g] * inverse for g in range(groups)]
        for j in range(k + 2, last):
            at, row = j // GROUP, j % GROUP
            uj, vj = row_of(u[at], row), row_of(v[at], row)
            for g in range(at, groups):
                if j < k + 4:
                    step = ((n1[g] * uj + n2[g] * vj) * guess) * correction
                else:
                    step = w1[g] * uj + w2[g] * vj
                column[j][g] = column[j][g] - step
        root_a = lax.rsqrt(a)
        root_d = lax.rsqrt(a * det)
        t0, t1 = row_of(block[home], sub), row_of(block[home], sub + 1)
        for g in range(home, groups):
            step = w1[g] * t0 + w2[g] * t1
            if g > home:
                block[g] = block[g] - step
            elif sub + 2 < GROUP:
                block[g] = block[g] - jnp.where(sublane > sub + 1, step, 0.0)
        block[home] = jnp.where(sublane == sub, t0 * root_a, block[home])
        block[home] = jnp.where(sublane == sub + 1, (a * t1 - b * t0) * root_d, block[home])
    return jnp.concatenate(block, axis=0)


def matmul(left, right):
    return jnp.dot(left, right, preferred_element_type=jnp.float32)


def matmul_nt(left, right):
    return lax.dot_general(left, right, (((1,), (1,)), ((), ())), preferred_element_type=jnp.float32)


def stacked(value):
    high, low = split(value)
    return jnp.concatenate([high, high, low, jnp.zeros_like(high)], axis=0)


def rows_at(block):
    return pl.ds(pl.multiple_of(block * LANES, LANES), LANES)


def square_iota(axis):
    return lax.broadcasted_iota(jnp.int32, (LANES, LANES), axis)


def beyond_strip():
    return square_iota(1) // STRIP > square_iota(0) // STRIP


def eliminate_block(rows, lower_ref):
    lane = square_iota(1)
    done = [[] for _ in rows]
    for first in range(0, LANES, STRIP):
        last = first + STRIP
        solved = eliminate_strip(rows[0][:STRIP], first)
        in_strip = (lane[:STRIP] >= first) & (lane[:STRIP] < last)
        high, low = split(jnp.where(in_strip, solved, 0.0))
        diagonal_high, diagonal_low = split(jnp.where(in_strip, rows[0][:STRIP], 0.0))
        spread = [
            jnp.concatenate([jnp.zeros_like(part)] * (first // STRIP) + [part] + [jnp.zeros_like(part)] * ((LANES - last) // STRIP))
            for part in (high, low)
        ]
        diagonal = matmul_nt(diagonal_high, spread[0]) + matmul_nt(diagonal_low, spread[0])
        diagonal += matmul_nt(diagonal_high, spread[1])
        at_or_below = lane[:STRIP] <= first + square_iota(0)[:STRIP]
        lower_ref[first:last, :] = jnp.where(at_or_below, diagonal, 0.0)
        high, low = high.astype(jnp.float32), low.astype(jnp.float32)
        inverse = high if first == 0 else pltpu.roll(high, LANES - first, 1)
        inverse += pltpu.roll(low, (LANES + STRIP - first) % LANES, 1) if first != STRIP else low
        inverse += pltpu.roll(high, (LANES + 2 * STRIP - first) % LANES, 1) if first != 2 * STRIP else high
        inverse = inverse.astype(jnp.bfloat16)
        strips = [solved] + [matmul(inverse, stacked(part[:STRIP])) for part in rows[1:]]
        for part, strip in zip(done, strips):
            part.append(strip)
        if last == LANES:
            break
        high, low = split(solved)
        wide = jnp.concatenate([high, low, high, jnp.zeros_like(high)], axis=0).astype(jnp.float32)
        left = wide.T[last:, :].astype(jnp.bfloat16)
        under = [part[STRIP:] for part in rows]
        inside = (lane[last:] >= first) & (lane[last:] < last)
        under[0] = jnp.where(inside, 0.0, under[0])
        rows = [part - matmul(left, stacked(strip)) for part, strip in zip(under, strips)]
    return [jnp.concatenate(part, axis=0) for part in done]


def assemble(me, own, mate, far, far_mate, work):
    size = own.shape[0]
    half = size // 2
    near = ((own, me), (mate, jnp.bitwise_xor(me, 1)))
    other = ((far, jnp.bitwise_xor(me, 2)), (far_mate, jnp.bitwise_xor(me, 3)))

    @pl.when(me < 2)
    def _():
        for part, column in near:
            work[column, :half, :] = part[:half, :].astype(jnp.float32)
            for block in range(half // LANES, size // LANES):
                flipped = part[block * LANES : (block + 1) * LANES, :].astype(jnp.float32).T
                work[block, rows_at(column), :] = flipped
        for part, column in other:
            work[column, half:size, :] = part[...].astype(jnp.float32)

    @pl.when(me >= 2)
    def _():
        for part, column in near:
            work[column, :size, :] = part[...].astype(jnp.float32)
        for part, column in other:
            work[column, :half, :] = part[...].astype(jnp.float32)


def first_kernel(axis, own, mate, far, far_mate, done_ref, lower_ref, work):
    count = lax.axis_size(axis)
    assemble(lax.axis_index(axis), own, mate, far, far_mate, work)
    done = eliminate_block([work[d, :LANES, :] for d in range(count)], lower_ref)
    for d in range(count):
        done_ref[d] = done[d]


def rest_kernel(
    axis, own, mate, far, far_mate, done_ref, first_lower, own_ref, high_ref, low_ref, work, lower
):
    count = lax.axis_size(axis)
    me = lax.axis_index(axis)
    lane, row = square_iota(1), square_iota(0)
    beyond = beyond_strip()
    assemble(me, own, mate, far, far_mate, work)
    work[:count, :LANES, :] = done_ref[...]
    lower[0] = first_lower[...]

    def block_step(q, carry):
        before = q - 1
        places = [lax.rem(before + d, count) for d in range(count)]
        rights = [work[place, rows_at(before), :] for place in places]
        rights[0] = jnp.where(beyond, 0.0, rights[0])
        rights = [split(right) for right in rights]

        def update(target):
            high, low = split(work[target, rows_at(before), :].T)
            both = jnp.concatenate([high, low], axis=1)
            new = []
            for d, (place, (right_high, right_low)) in enumerate(zip(places, rights)):
                product = matmul(both, jnp.concatenate([right_high, right_high], axis=0)) + matmul(high, right_low)
                new.append(-product if d == 0 else work[place, rows_at(target), :] - product)
            return new

        rows = update(q)
        for target in (q + 1, q + 2):
            for place, new in zip(places, update(target)):
                work[place, rows_at(target), :] = new
        done = eliminate_block(rows[1:] + rows[:1], lower.at[q])
        for place, part in zip(places[1:] + places[:1], done):
            work[place, rows_at(q), :] = part
        return carry

    lax.fori_loop(1, count, block_step, 0)

    for i in range(count):
        block = work[i, rows_at(me), :]
        upper = jnp.where((i > me) | ((i == me) & beyond), block, 0.0)
        own_ref[i * LANES : (i + 1) * LANES, :] = upper.T + jnp.where(i == me, lower[i], 0.0)
        for c in range(count):
            block = work[c, i * LANES : (i + 1) * LANES, :]
            if c > i:
                block = jnp.zeros_like(block)
            elif c == i:
                block = jnp.where(lane <= row, block, 0.0)
            high, low = split(block)
            high_ref[i * LANES : (i + 1) * LANES, c * LANES : (c + 1) * LANES] = high
            low_ref[i * LANES : (i + 1) * LANES, c * LANES : (c + 1) * LANES] = low


def solve_kernel(row_axis, col_axis, order, group_count, *refs):
    high_ref, low_ref = refs[:2]
    inputs = refs[2 : 3 + group_count]
    trailing_ref, own_ref, schur_ref, group, side = refs[3 + group_count :]
    size = high_ref.shape[0]
    half = size // 2
    share = own_ref.shape[1]
    count = side.shape[0] // share
    my_row, my_col = lax.axis_index(row_axis), lax.axis_index(col_axis)
    for i, ref in enumerate(inputs[:-1]):
        if order is None:
            group[...] = ref[...]
        else:
            for p in range(count):
                at = jnp.bitwise_xor(my_col, i * count + p) * share
                group[pl.ds(pl.multiple_of(at, share), share), :] = ref[p * share : (p + 1) * share, :]
    for p in range(count):
        place = jnp.bitwise_xor(my_row, p) if order else lax.rem(my_row + count - p, count)
        side[pl.ds(pl.multiple_of(place * share, share), share), :] = inputs[-1][p * share : (p + 1) * share, :]
    contract = (((1,), (1,)), ((), ()))

    def product(left, right):
        return lax.dot_general(left, right, contract, preferred_element_type=jnp.float32)

    def solve(rows):
        first = product(rows[:, :half], high_ref[:half, :half]) + product(rows[:, :half], low_ref[:half, :half])
        second = product(rows, high_ref[half:, :]) + product(rows, low_ref[half:, :])
        return jnp.concatenate([first, second], axis=1).astype(jnp.bfloat16)

    side[...] = solve(side[...])
    rows = group.shape[0]
    chunk = min(rows, 256)

    def step(i, carry):
        here = pl.ds(pl.multiple_of(i * chunk, chunk), chunk)
        solved = solve(group[here, :])
        group[here, :] = solved
        update = product(solved, side[...])
        schur_ref[here, :] = (trailing_ref[here, :].astype(jnp.float32) - update).astype(jnp.bfloat16)
        return carry

    if rows == chunk:
        step(0, 0)
    else:
        lax.fori_loop(0, rows // chunk, step, 0)
    own_ref[0] = group[pl.ds(pl.multiple_of(my_col * share, share), share), :]


def body(pivot_block, panel, lead, trailing):
    pivot_size, local_width = pivot_block.shape
    rows, cols = lax.axis_size("row"), lax.axis_size("col")
    share = panel.shape[1]
    col_index = lax.axis_index("col")
    vmem = pl.BlockSpec(memory_space=pltpu.VMEM)

    half = pivot_size // 2
    row_index = lax.axis_index("row")
    wide = pivot_block.astype(jnp.float32)
    diagonal_half = lax.dynamic_slice_in_dim(pivot_block, row_index // 2 * half, half, 0)
    far = lax.ppermute(diagonal_half, "row", [(d ^ 2, d) for d in range(rows)])
    far_mate = lax.ppermute(diagonal_half, "row", [(d ^ 3, d) for d in range(rows)])
    mate = lax.ppermute(pivot_block, "row", [(d ^ 1, d) for d in range(rows)])
    pivots = [wide, mate, far, far_mate]

    done, first_lower = pl.pallas_call(
        functools.partial(first_kernel, "row"),
        out_shape=(
            jax.ShapeDtypeStruct((rows, LANES, LANES), jnp.float32),
            jax.ShapeDtypeStruct((LANES, LANES), jnp.float32),
        ),
        in_specs=[vmem] * len(pivots),
        out_specs=(vmem,) * 2,
        scratch_shapes=[pltpu.VMEM((rows, pivot_size, LANES), jnp.float32)],
        compiler_params=pltpu.CompilerParams(vmem_limit_bytes=32 * 1024 * 1024),
        cost_estimate=pl.CostEstimate(flops=3 * 10**8, bytes_accessed=10**6, transcendentals=10**5),
        name="first",
    )(*pivots)

    def live(shards, rows_of):
        block = jnp.concatenate([(shard * share + jnp.arange(share)) // BLOCK for shard in shards])
        matches = block[:, None] == jnp.arange(lead.shape[1])[None, :]
        row_lead = jnp.sum(jnp.where(matches, lead, 0), axis=1)
        keep = (jnp.arange(pivot_size) // BLOCK)[None, :] >= row_lead[:, None]
        return jnp.where(keep, rows_of, jnp.zeros_like(rows_of))

    ratio = cols // rows
    paired = cols == 2 * rows and rows & (rows - 1) == 0

    def to_side(array, shift):
        pairs = []
        for r in range(rows):
            for c in range(cols):
                to_row, to_col = (c % rows + shift) % rows, r * ratio + c // rows
                pairs.append((c * rows + r, to_col * rows + to_row))
        return lax.ppermute(array, ("col", "row"), pairs)

    if paired:
        quad, _ = lax.optimization_barrier((panel[0], diagonal_half))
        step = 1
        while step < rows:
            pieces = (quad, lax.ppermute(quad, "col", [(d ^ step, d) for d in range(cols)]))
            step *= 2
            if step == rows:
                pieces, _ = lax.optimization_barrier((pieces, first_lower))
            quad = jnp.concatenate(pieces, axis=0)
        quad = live([col_index ^ p for p in range(rows)], quad)
        group = [quad, lax.ppermute(quad, "col", [(d ^ rows, d) for d in range(cols)])]
        side = to_side(quad, 0)
    else:
        masked = live([col_index], panel[0])
        group = [lax.all_gather(masked, "col", axis=0, tiled=True)]
        side = jnp.concatenate([to_side(masked, s) for s in range(rows)], axis=0)

    own, high, low = pl.pallas_call(
        functools.partial(rest_kernel, "row"),
        out_shape=(
            jax.ShapeDtypeStruct((pivot_size, local_width), jnp.float32),
            jax.ShapeDtypeStruct((pivot_size, pivot_size), jnp.bfloat16),
            jax.ShapeDtypeStruct((pivot_size, pivot_size), jnp.bfloat16),
        ),
        in_specs=[vmem] * (len(pivots) + 2),
        out_specs=(vmem,) * 3,
        scratch_shapes=[
            pltpu.VMEM((rows + 2, pivot_size + 2 * LANES, LANES), jnp.float32),
            pltpu.VMEM((rows, LANES, LANES), jnp.float32),
        ],
        compiler_params=pltpu.CompilerParams(vmem_limit_bytes=32 * 1024 * 1024),
        cost_estimate=pl.CostEstimate(flops=10**9, bytes_accessed=2 * 10**6, transcendentals=10**5),
        name="rest",
    )(*pivots, done, first_lower)

    group_rows = share * cols
    panel_factor, schur = pl.pallas_call(
        functools.partial(solve_kernel, "row", "col", True if paired else None, len(group)),
        out_shape=(
            jax.ShapeDtypeStruct(panel.shape, jnp.bfloat16),
            jax.ShapeDtypeStruct(trailing.shape, jnp.bfloat16),
        ),
        in_specs=[vmem] * (4 + len(group)),
        out_specs=(vmem,) * 2,
        scratch_shapes=[
            pltpu.VMEM((group_rows, pivot_size), jnp.bfloat16),
            pltpu.VMEM((share * rows, pivot_size), jnp.bfloat16),
        ],
        compiler_params=pltpu.CompilerParams(vmem_limit_bytes=48 * 1024 * 1024),
        cost_estimate=pl.CostEstimate(flops=4 * 10**8, bytes_accessed=2 * 10**6, transcendentals=0),
        name="solve",
    )(high, low, *group, side, trailing)
    return (own, panel_factor, schur)


def solution(mesh):
    return jax.shard_map(
        body,
        mesh=mesh,
        in_specs=(P(None, "row"), P("row", "col", None), P("row", None), P("row", "col")),
        out_specs=(P(None, "row"), P("row", "col", None), P("row", "col")),
        check_vma=False,
    )
```

```python
import functools

import jax
import jax.numpy as jnp
from jax import lax
from jax.experimental import pallas as pl
from jax.experimental.pallas import tpu as pltpu
from jax.sharding import PartitionSpec as P

BLOCK = 128
STRIP = 32
SUB = 16
GROUP = 8
LANES = 128


def split(value):
    high = value.astype(jnp.bfloat16)
    low = (value - high.astype(jnp.float32)).astype(jnp.bfloat16)
    return high, low


def row_of(value, row):
    return jnp.broadcast_to(value[row : row + 1, :], (GROUP, LANES))


def reciprocal(value):
    guess = pl.reciprocal(value, approx=True)
    return guess, 2.0 - value * guess


def eliminate_strip(strip, first):
    groups = STRIP // GROUP
    sublane = lax.broadcasted_iota(jnp.int32, (GROUP, LANES), 0)
    lane = lax.broadcasted_iota(jnp.int32, (GROUP, LANES), 1)
    zero = jnp.zeros((GROUP, LANES), jnp.float32)
    block = [strip[g * GROUP : (g + 1) * GROUP, :] for g in range(groups)]
    inside = (lane >= first) & (lane < first + STRIP)
    lower = [zero] * groups
    column = [None] * STRIP
    for k in range(0, STRIP, 2):
        if k % SUB == 0:
            for j in range(k, k + SUB):
                column[j] = [
                    jnp.broadcast_to(block[g][:, first + j : first + j + 1], (GROUP, LANES)) if g >= j // GROUP else None
                    for g in range(groups)
                ]
            taken = (lane >= first + k) & (lane < first + k + SUB)
            for g in range(groups):
                identity = jnp.where(lane - first == sublane + g * GROUP, 1.0, 0.0)
                block[g] = jnp.where(taken, identity, block[g])
        last = k - k % SUB + SUB
        home, sub = k // GROUP, k % GROUP
        u, v = column[k], column[k + 1]
        a = row_of(u[home], sub)
        b = row_of(u[home], sub + 1)
        c = row_of(v[home], sub + 1)
        det = a * c - b * b
        guess, correction = reciprocal(det)
        n1 = [None if g < home else c * u[g] - b * v[g] for g in range(groups)]
        n2 = [None if g < home else a * v[g] - b * u[g] for g in range(groups)]
        inverse = guess * correction
        w1 = [None if g < home else n1[g] * inverse for g in range(groups)]
        w2 = [None if g < home else n2[g] * inverse for g in range(groups)]
        for j in range(k + 2, last):
            at, row = j // GROUP, j % GROUP
            uj, vj = row_of(u[at], row), row_of(v[at], row)
            for g in range(at, groups):
                if j < k + 4:
                    step = ((n1[g] * uj + n2[g] * vj) * guess) * correction
                else:
                    step = w1[g] * uj + w2[g] * vj
                column[j][g] = column[j][g] - step
        root_a = lax.rsqrt(a)
        root_d = lax.rsqrt(a * det)
        for g in range(home, groups):
            lower[g] = jnp.where(lane == first + k, u[g] * root_a, lower[g])
            lower[g] = jnp.where(lane == first + k + 1, n2[g] * root_d, lower[g])
        t0, t1 = row_of(block[home], sub), row_of(block[home], sub + 1)
        for g in range(home, groups):
            step = w1[g] * t0 + w2[g] * t1
            if g > home:
                block[g] = block[g] - step
            elif sub + 2 < GROUP:
                block[g] = block[g] - jnp.where(sublane > sub + 1, step, 0.0)
        block[home] = jnp.where(sublane == sub, t0 * root_a, block[home])
        block[home] = jnp.where(sublane == sub + 1, (a * t1 - b * t0) * root_d, block[home])
    for g in range(groups):
        keep = (lane <= first + sublane + g * GROUP) & inside
        lower[g] = jnp.where(keep, lower[g], 0.0)
    return jnp.concatenate(block, axis=0), jnp.concatenate(lower, axis=0)


def matmul(left, right):
    return jnp.dot(left, right, preferred_element_type=jnp.float32)


def stacked(value):
    high, low = split(value)
    return jnp.concatenate([high, high, low, jnp.zeros_like(high)], axis=0)


def rows_at(block):
    return pl.ds(pl.multiple_of(block * LANES, LANES), LANES)


def square_iota(axis):
    return lax.broadcasted_iota(jnp.int32, (LANES, LANES), axis)


def beyond_strip():
    return square_iota(1) // STRIP > square_iota(0) // STRIP


def eliminate_block(rows, lower_ref):
    lane = square_iota(1)
    done = [[] for _ in rows]
    for first in range(0, LANES, STRIP):
        last = first + STRIP
        solved, diagonal = eliminate_strip(rows[0][:STRIP], first)
        lower_ref[first:last, :] = diagonal
        in_strip = (lane[:STRIP] >= first) & (lane[:STRIP] < last)
        high, low = split(jnp.where(in_strip, solved, 0.0))
        high, low = high.astype(jnp.float32), low.astype(jnp.float32)
        inverse = high if first == 0 else pltpu.roll(high, LANES - first, 1)
        inverse += pltpu.roll(low, (LANES + STRIP - first) % LANES, 1) if first != STRIP else low
        inverse += pltpu.roll(high, (LANES + 2 * STRIP - first) % LANES, 1) if first != 2 * STRIP else high
        inverse = inverse.astype(jnp.bfloat16)
        strips = [solved] + [matmul(inverse, stacked(part[:STRIP])) for part in rows[1:]]
        for part, strip in zip(done, strips):
            part.append(strip)
        if last == LANES:
            break
        high, low = split(solved)
        wide = jnp.concatenate([high, low, high, jnp.zeros_like(high)], axis=0).astype(jnp.float32)
        left = wide.T[last:, :].astype(jnp.bfloat16)
        under = [part[STRIP:] for part in rows]
        inside = (lane[last:] >= first) & (lane[last:] < last)
        under[0] = jnp.where(inside, 0.0, under[0])
        rows = [part - matmul(left, stacked(strip)) for part, strip in zip(under, strips)]
    return [jnp.concatenate(part, axis=0) for part in done]


def assemble(me, own, mate, far, far_mate, work, start, stop):
    size = own.shape[0]
    half = size // 2
    near = ((own, me), (mate, jnp.bitwise_xor(me, 1)))
    other = ((far, jnp.bitwise_xor(me, 2)), (far_mate, jnp.bitwise_xor(me, 3)))

    def place(parts, low, high, offset):
        low, high = max(low, start), min(high, stop)
        for part, column in parts:
            if low < high:
                work[column, low:high, :] = part[low - offset : high - offset, :].astype(jnp.float32)

    @pl.when(me < 2)
    def _():
        place(near, 0, half, 0)
        place(other, half, size, half)
        for row_block in range(start // LANES, min(half, stop) // LANES):
            for block in range(half // LANES, size // LANES):
                here = slice(block * LANES, (block + 1) * LANES)
                flipped = jnp.where(me == row_block, own[here, :], mate[here, :].astype(jnp.float32)).T
                work[block, row_block * LANES : (row_block + 1) * LANES, :] = flipped

    @pl.when(me >= 2)
    def _():
        place(near, 0, size, 0)
        place(other, 0, half, 0)


def first_kernel(axis, own, mate, far, far_mate, done_ref, lower_ref, work):
    count = lax.axis_size(axis)
    assemble(lax.axis_index(axis), own, mate, far, far_mate, work, 0, LANES)
    done = eliminate_block([work[d, :LANES, :] for d in range(count)], lower_ref)
    for d in range(count):
        done_ref[d] = done[d]


def rest_kernel(
    axis, own, mate, far, far_mate, done_ref, first_lower, own_ref, high_ref, low_ref, work, lower
):
    count = lax.axis_size(axis)
    me = lax.axis_index(axis)
    lane, row = square_iota(1), square_iota(0)
    beyond = beyond_strip()
    assemble(me, own, mate, far, far_mate, work, LANES, count * LANES)
    work[:count, :LANES, :] = done_ref[...]
    lower[0] = first_lower[...]

    def block_step(q, carry):
        before = q - 1
        places = [lax.rem(before + d, count) for d in range(count)]
        rights = [work[place, rows_at(before), :] for place in places]
        rights[0] = jnp.where(beyond, 0.0, rights[0])
        rights = [split(right) for right in rights]

        def update(target):
            high, low = split(work[target, rows_at(before), :].T)
            both = jnp.concatenate([high, low], axis=1)
            new = []
            for d, (place, (right_high, right_low)) in enumerate(zip(places, rights)):
                product = matmul(both, jnp.concatenate([right_high, right_high], axis=0)) + matmul(high, right_low)
                new.append(-product if d == 0 else work[place, rows_at(target), :] - product)
            return new

        rows = update(q)
        for target in (q + 1, q + 2):
            for place, new in zip(places, update(target)):
                work[place, rows_at(target), :] = new
        done = eliminate_block(rows[1:] + rows[:1], lower.at[q])
        for place, part in zip(places[1:] + places[:1], done):
            work[place, rows_at(q), :] = part
        return carry

    lax.fori_loop(1, count, block_step, 0)

    for i in range(count):
        block = work[i, rows_at(me), :]
        upper = jnp.where((i > me) | ((i == me) & beyond), block, 0.0)
        own_ref[i * LANES : (i + 1) * LANES, :] = upper.T + jnp.where(i == me, lower[i], 0.0)
        for c in range(count):
            block = work[c, i * LANES : (i + 1) * LANES, :]
            if c > i:
                block = jnp.zeros_like(block)
            elif c == i:
                block = jnp.where(lane <= row, block, 0.0)
            high, low = split(block)
            high_ref[i * LANES : (i + 1) * LANES, c * LANES : (c + 1) * LANES] = high
            low_ref[i * LANES : (i + 1) * LANES, c * LANES : (c + 1) * LANES] = low


def solve_kernel(row_axis, col_axis, order, group_count, *refs):
    high_ref, low_ref = refs[:2]
    inputs = refs[2 : 3 + group_count]
    trailing_ref, own_ref, schur_ref, group, side = refs[3 + group_count :]
    size = high_ref.shape[0]
    half = size // 2
    share = own_ref.shape[1]
    count = side.shape[0] // share
    my_row, my_col = lax.axis_index(row_axis), lax.axis_index(col_axis)
    for i, ref in enumerate(inputs[:-1]):
        if order is None:
            group[...] = ref[...]
        else:
            for p in range(count):
                at = jnp.bitwise_xor(my_col, i * count + p) * share
                group[pl.ds(pl.multiple_of(at, share), share), :] = ref[p * share : (p + 1) * share, :]
    for p in range(count):
        place = jnp.bitwise_xor(my_row, p) if order else lax.rem(my_row + count - p, count)
        side[pl.ds(pl.multiple_of(place * share, share), share), :] = inputs[-1][p * share : (p + 1) * share, :]
    contract = (((1,), (1,)), ((), ()))

    def product(left, right):
        return lax.dot_general(left, right, contract, preferred_element_type=jnp.float32)

    def solve(rows):
        first = product(rows[:, :half], high_ref[:half, :half]) + product(rows[:, :half], low_ref[:half, :half])
        second = product(rows, high_ref[half:, :]) + product(rows, low_ref[half:, :])
        return jnp.concatenate([first, second], axis=1).astype(jnp.bfloat16)

    side[...] = solve(side[...])
    rows = group.shape[0]
    chunk = min(rows, 256)

    def step(i, carry):
        here = pl.ds(pl.multiple_of(i * chunk, chunk), chunk)
        solved = solve(group[here, :])
        group[here, :] = solved
        update = product(solved, side[...])
        schur_ref[here, :] = (trailing_ref[here, :].astype(jnp.float32) - update).astype(jnp.bfloat16)
        return carry

    if rows == chunk:
        step(0, 0)
    else:
        lax.fori_loop(0, rows // chunk, step, 0)
    own_ref[0] = group[pl.ds(pl.multiple_of(my_col * share, share), share), :]


def body(pivot_block, panel, lead, trailing):
    pivot_size, local_width = pivot_block.shape
    rows, cols = lax.axis_size("row"), lax.axis_size("col")
    share = panel.shape[1]
    col_index = lax.axis_index("col")
    vmem = pl.BlockSpec(memory_space=pltpu.VMEM)

    half = pivot_size // 2
    row_index = lax.axis_index("row")
    wide = pivot_block.astype(jnp.float32)
    diagonal_half = lax.dynamic_slice_in_dim(pivot_block, row_index // 2 * half, half, 0)
    far = lax.ppermute(diagonal_half, "row", [(d ^ 2, d) for d in range(rows)])
    far_mate = lax.ppermute(diagonal_half, "row", [(d ^ 3, d) for d in range(rows)])
    whole, _ = lax.optimization_barrier((pivot_block, diagonal_half))
    mate = lax.ppermute(whole, "row", [(d ^ 1, d) for d in range(rows)])
    pivots = [wide, mate, far, far_mate]

    done, first_lower = pl.pallas_call(
        functools.partial(first_kernel, "row"),
        out_shape=(
            jax.ShapeDtypeStruct((rows, LANES, LANES), jnp.float32),
            jax.ShapeDtypeStruct((LANES, LANES), jnp.float32),
        ),
        in_specs=[vmem] * len(pivots),
        out_specs=(vmem,) * 2,
        scratch_shapes=[pltpu.VMEM((rows, LANES, LANES), jnp.float32)],
        compiler_params=pltpu.CompilerParams(vmem_limit_bytes=32 * 1024 * 1024),
        cost_estimate=pl.CostEstimate(flops=3 * 10**8, bytes_accessed=10**6, transcendentals=10**5),
        name="first",
    )(*pivots)

    def live(shards, rows_of):
        block = jnp.concatenate([(shard * share + jnp.arange(share)) // BLOCK for shard in shards])
        matches = block[:, None] == jnp.arange(lead.shape[1])[None, :]
        row_lead = jnp.sum(jnp.where(matches, lead, 0), axis=1)
        keep = (jnp.arange(pivot_size) // BLOCK)[None, :] >= row_lead[:, None]
        return jnp.where(keep, rows_of, jnp.zeros_like(rows_of))

    ratio = cols // rows
    paired = cols == 2 * rows and rows & (rows - 1) == 0

    def to_side(array, shift):
        pairs = []
        for r in range(rows):
            for c in range(cols):
                to_row, to_col = (c % rows + shift) % rows, r * ratio + c // rows
                pairs.append((c * rows + r, to_col * rows + to_row))
        return lax.ppermute(array, ("col", "row"), pairs)

    if paired:
        quad, _ = lax.optimization_barrier((panel[0], diagonal_half))
        step = 1
        while step < rows:
            pieces = (quad, lax.ppermute(quad, "col", [(d ^ step, d) for d in range(cols)]))
            step *= 2
            if step == rows:
                pieces, _ = lax.optimization_barrier((pieces, first_lower))
            quad = jnp.concatenate(pieces, axis=0)
        quad = live([col_index ^ p for p in range(rows)], quad)
        group = [quad, lax.ppermute(quad, "col", [(d ^ rows, d) for d in range(cols)])]
        side = to_side(quad, 0)
    else:
        masked = live([col_index], panel[0])
        group = [lax.all_gather(masked, "col", axis=0, tiled=True)]
        side = jnp.concatenate([to_side(masked, s) for s in range(rows)], axis=0)

    own, high, low = pl.pallas_call(
        functools.partial(rest_kernel, "row"),
        out_shape=(
            jax.ShapeDtypeStruct((pivot_size, local_width), jnp.float32),
            jax.ShapeDtypeStruct((pivot_size, pivot_size), jnp.bfloat16),
            jax.ShapeDtypeStruct((pivot_size, pivot_size), jnp.bfloat16),
        ),
        in_specs=[vmem] * (len(pivots) + 2),
        out_specs=(vmem,) * 3,
        scratch_shapes=[
            pltpu.VMEM((rows + 2, pivot_size + 2 * LANES, LANES), jnp.float32),
            pltpu.VMEM((rows, LANES, LANES), jnp.float32),
        ],
        compiler_params=pltpu.CompilerParams(vmem_limit_bytes=32 * 1024 * 1024),
        cost_estimate=pl.CostEstimate(flops=10**9, bytes_accessed=2 * 10**6, transcendentals=10**5),
        name="rest",
    )(*pivots, done, first_lower)

    group_rows = share * cols
    panel_factor, schur = pl.pallas_call(
        functools.partial(solve_kernel, "row", "col", True if paired else None, len(group)),
        out_shape=(
            jax.ShapeDtypeStruct(panel.shape, jnp.bfloat16),
            jax.ShapeDtypeStruct(trailing.shape, jnp.bfloat16),
        ),
        in_specs=[vmem] * (4 + len(group)),
        out_specs=(vmem,) * 2,
        scratch_shapes=[
            pltpu.VMEM((group_rows, pivot_size), jnp.bfloat16),
            pltpu.VMEM((share * rows, pivot_size), jnp.bfloat16),
        ],
        compiler_params=pltpu.CompilerParams(vmem_limit_bytes=48 * 1024 * 1024),
        cost_estimate=pl.CostEstimate(flops=4 * 10**8, bytes_accessed=2 * 10**6, transcendentals=0),
        name="solve",
    )(high, low, *group, side, trailing)
    return (own, panel_factor, schur)


def solution(mesh):
    return jax.shard_map(
        body,
        mesh=mesh,
        in_specs=(P(None, "row"), P("row", "col", None), P("row", None), P("row", "col")),
        out_specs=(P(None, "row"), P("row", "col", None), P("row", "col")),
        check_vma=False,
    )
```

```python
import functools

import jax
import jax.numpy as jnp
from jax import lax
from jax.experimental import pallas as pl
from jax.experimental.pallas import tpu as pltpu
from jax.sharding import PartitionSpec as P

BLOCK = 128
STRIP = 32
SUB = 16
GROUP = 8
LANES = 128


def split(value):
    high = value.astype(jnp.bfloat16)
    low = (value - high.astype(jnp.float32)).astype(jnp.bfloat16)
    return high, low


def row_of(value, row):
    return jnp.broadcast_to(value[row : row + 1, :], (GROUP, LANES))


def reciprocal(value):
    guess = pl.reciprocal(value, approx=True)
    return guess, 2.0 - value * guess


def eliminate_strip(strip, first):
    groups = STRIP // GROUP
    sublane = lax.broadcasted_iota(jnp.int32, (GROUP, LANES), 0)
    lane = lax.broadcasted_iota(jnp.int32, (GROUP, LANES), 1)
    zero = jnp.zeros((GROUP, LANES), jnp.float32)
    block = [strip[g * GROUP : (g + 1) * GROUP, :] for g in range(groups)]
    inside = (lane >= first) & (lane < first + STRIP)
    lower = [zero] * groups
    column = [None] * STRIP
    for k in range(0, STRIP, 2):
        if k % SUB == 0:
            for j in range(k, k + SUB):
                column[j] = [
                    jnp.broadcast_to(block[g][:, first + j : first + j + 1], (GROUP, LANES)) if g >= j // GROUP else None
                    for g in range(groups)
                ]
            taken = (lane >= first + k) & (lane < first + k + SUB)
            for g in range(groups):
                identity = jnp.where(lane - first == sublane + g * GROUP, 1.0, 0.0)
                block[g] = jnp.where(taken, identity, block[g])
        last = k - k % SUB + SUB
        home, sub = k // GROUP, k % GROUP
        u, v = column[k], column[k + 1]
        a = row_of(u[home], sub)
        b = row_of(u[home], sub + 1)
        c = row_of(v[home], sub + 1)
        det = a * c - b * b
        guess, correction = reciprocal(det)
        n1 = [None if g < home else c * u[g] - b * v[g] for g in range(groups)]
        n2 = [None if g < home else a * v[g] - b * u[g] for g in range(groups)]
        inverse = guess * correction
        w1 = [None if g < home else n1[g] * inverse for g in range(groups)]
        w2 = [None if g < home else n2[g] * inverse for g in range(groups)]
        for j in range(k + 2, last):
            at, row = j // GROUP, j % GROUP
            uj, vj = row_of(u[at], row), row_of(v[at], row)
            for g in range(at, groups):
                if j < k + 4:
                    step = ((n1[g] * uj + n2[g] * vj) * guess) * correction
                else:
                    step = w1[g] * uj + w2[g] * vj
                column[j][g] = column[j][g] - step
        root_a = lax.rsqrt(a)
        root_d = lax.rsqrt(a * det)
        for g in range(home, groups):
            lower[g] = jnp.where(lane == first + k, u[g] * root_a, lower[g])
            lower[g] = jnp.where(lane == first + k + 1, n2[g] * root_d, lower[g])
        t0, t1 = row_of(block[home], sub), row_of(block[home], sub + 1)
        for g in range(home, groups):
            step = w1[g] * t0 + w2[g] * t1
            if g > home:
                block[g] = block[g] - step
            elif sub + 2 < GROUP:
                block[g] = block[g] - jnp.where(sublane > sub + 1, step, 0.0)
        block[home] = jnp.where(sublane == sub, t0 * root_a, block[home])
        block[home] = jnp.where(sublane == sub + 1, (a * t1 - b * t0) * root_d, block[home])
    for g in range(groups):
        keep = (lane <= first + sublane + g * GROUP) & inside
        lower[g] = jnp.where(keep, lower[g], 0.0)
    return jnp.concatenate(block, axis=0), jnp.concatenate(lower, axis=0)


def matmul(left, right):
    return jnp.dot(left, right, preferred_element_type=jnp.float32)


def stacked(value):
    high, low = split(value)
    return jnp.concatenate([high, high, low, jnp.zeros_like(high)], axis=0)


def rows_at(block):
    return pl.ds(pl.multiple_of(block * LANES, LANES), LANES)


def square_iota(axis):
    return lax.broadcasted_iota(jnp.int32, (LANES, LANES), axis)


def beyond_strip():
    return square_iota(1) // STRIP > square_iota(0) // STRIP


def eliminate_block(rows, lower_ref):
    lane = square_iota(1)
    done = [[] for _ in rows]
    for first in range(0, LANES, STRIP):
        last = first + STRIP
        solved, diagonal = eliminate_strip(rows[0][:STRIP], first)
        lower_ref[first:last, :] = diagonal
        in_strip = (lane[:STRIP] >= first) & (lane[:STRIP] < last)
        high, low = split(jnp.where(in_strip, solved, 0.0))
        high, low = high.astype(jnp.float32), low.astype(jnp.float32)
        inverse = high if first == 0 else pltpu.roll(high, LANES - first, 1)
        inverse += pltpu.roll(low, (LANES + STRIP - first) % LANES, 1) if first != STRIP else low
        inverse += pltpu.roll(high, (LANES + 2 * STRIP - first) % LANES, 1) if first != 2 * STRIP else high
        inverse = inverse.astype(jnp.bfloat16)
        strips = [solved] + [matmul(inverse, stacked(part[:STRIP])) for part in rows[1:]]
        for part, strip in zip(done, strips):
            part.append(strip)
        if last == LANES:
            break
        high, low = split(solved)
        wide = jnp.concatenate([high, low, high, jnp.zeros_like(high)], axis=0).astype(jnp.float32)
        left = wide.T[last:, :].astype(jnp.bfloat16)
        under = [part[STRIP:] for part in rows]
        inside = (lane[last:] >= first) & (lane[last:] < last)
        under[0] = jnp.where(inside, 0.0, under[0])
        rows = [part - matmul(left, stacked(strip)) for part, strip in zip(under, strips)]
    return [jnp.concatenate(part, axis=0) for part in done]


def assemble(me, own, mate, far, far_mate, work, start, stop):
    size = own.shape[0]
    half = size // 2
    near = ((own, me), (mate, jnp.bitwise_xor(me, 1)))
    other = ((far, jnp.bitwise_xor(me, 2)), (far_mate, jnp.bitwise_xor(me, 3)))

    def place(parts, low, high, offset):
        low, high = max(low, start), min(high, stop)
        for part, column in parts:
            if low < high:
                work[column, low:high, :] = part[low - offset : high - offset, :].astype(jnp.float32)

    @pl.when(me < 2)
    def _():
        place(near, 0, half, 0)
        place(other, half, size, half)
        for row_block in range(start // LANES, min(half, stop) // LANES):
            for block in range(half // LANES, size // LANES):
                here = slice(block * LANES, (block + 1) * LANES)
                flipped = jnp.where(me == row_block, own[here, :], mate[here, :].astype(jnp.float32)).T
                work[block, row_block * LANES : (row_block + 1) * LANES, :] = flipped

    @pl.when(me >= 2)
    def _():
        place(near, 0, size, 0)
        place(other, 0, half, 0)


def first_kernel(axis, own, mate, far, far_mate, done_ref, lower_ref, work):
    count = lax.axis_size(axis)
    assemble(lax.axis_index(axis), own, mate, far, far_mate, work, 0, LANES)
    done = eliminate_block([work[d, :LANES, :] for d in range(count)], lower_ref)
    for d in range(count):
        done_ref[d] = done[d]


def eliminate_next(q, count, work, lower_ref):
    beyond = beyond_strip()
    before = q - 1
    places = [lax.rem(before + d, count) for d in range(count)]
    rights = [work[place, rows_at(before), :] for place in places]
    rights[0] = jnp.where(beyond, 0.0, rights[0])
    rights = [split(right) for right in rights]

    def update(target):
        high, low = split(work[target, rows_at(before), :].T)
        both = jnp.concatenate([high, low], axis=1)
        new = []
        for d, (place, (right_high, right_low)) in enumerate(zip(places, rights)):
            product = matmul(both, jnp.concatenate([right_high, right_high], axis=0)) + matmul(high, right_low)
            new.append(-product if d == 0 else work[place, rows_at(target), :] - product)
        return new

    rows = update(q)
    for target in (q + 1, q + 2):
        for place, new in zip(places, update(target)):
            work[place, rows_at(target), :] = new
    done = eliminate_block(rows[1:] + rows[:1], lower_ref)
    for place, part in zip(places[1:] + places[:1], done):
        work[place, rows_at(q), :] = part


def second_kernel(axis, own, mate, far, far_mate, done_ref, work, lower_ref):
    count = lax.axis_size(axis)
    assemble(lax.axis_index(axis), own, mate, far, far_mate, work, LANES, count * LANES)
    work[:, :LANES, :] = done_ref[...]
    eliminate_next(1, count, work, lower_ref)


def last_kernel(axis, before_ref, lower0, lower1, own_ref, high_ref, low_ref, work, lower):
    count = lax.axis_size(axis)
    me = lax.axis_index(axis)
    lane, row = square_iota(1), square_iota(0)
    beyond = beyond_strip()
    work[:count, : count * LANES, :] = before_ref[...]
    lower[0] = lower0[...]
    lower[1] = lower1[...]

    def block_step(q, carry):
        eliminate_next(q, count, work, lower.at[q])
        return carry

    lax.fori_loop(2, count, block_step, 0)

    for i in range(count):
        block = work[i, rows_at(me), :]
        upper = jnp.where((i > me) | ((i == me) & beyond), block, 0.0)
        own_ref[i * LANES : (i + 1) * LANES, :] = upper.T + jnp.where(i == me, lower[i], 0.0)
        for c in range(count):
            block = work[c, i * LANES : (i + 1) * LANES, :]
            if c > i:
                block = jnp.zeros_like(block)
            elif c == i:
                block = jnp.where(lane <= row, block, 0.0)
            high, low = split(block)
            high_ref[i * LANES : (i + 1) * LANES, c * LANES : (c + 1) * LANES] = high
            low_ref[i * LANES : (i + 1) * LANES, c * LANES : (c + 1) * LANES] = low


def solve_kernel(row_axis, col_axis, order, group_count, *refs):
    high_ref, low_ref = refs[:2]
    inputs = refs[2 : 3 + group_count]
    trailing_ref, own_ref, schur_ref, group, side = refs[3 + group_count :]
    size = high_ref.shape[0]
    half = size // 2
    share = own_ref.shape[1]
    count = side.shape[0] // share
    my_row, my_col = lax.axis_index(row_axis), lax.axis_index(col_axis)
    for i, ref in enumerate(inputs[:-1]):
        if order is None:
            group[...] = ref[...]
        else:
            for p in range(count):
                at = jnp.bitwise_xor(my_col, i * count + p) * share
                group[pl.ds(pl.multiple_of(at, share), share), :] = ref[p * share : (p + 1) * share, :]
    for p in range(count):
        place = jnp.bitwise_xor(my_row, p) if order else lax.rem(my_row + count - p, count)
        side[pl.ds(pl.multiple_of(place * share, share), share), :] = inputs[-1][p * share : (p + 1) * share, :]
    contract = (((1,), (1,)), ((), ()))

    def product(left, right):
        return lax.dot_general(left, right, contract, preferred_element_type=jnp.float32)

    def solve(rows):
        first = product(rows[:, :half], high_ref[:half, :half]) + product(rows[:, :half], low_ref[:half, :half])
        second = product(rows, high_ref[half:, :]) + product(rows, low_ref[half:, :])
        return jnp.concatenate([first, second], axis=1).astype(jnp.bfloat16)

    side[...] = solve(side[...])
    rows = group.shape[0]
    chunk = min(rows, 256)

    def step(i, carry):
        here = pl.ds(pl.multiple_of(i * chunk, chunk), chunk)
        solved = solve(group[here, :])
        group[here, :] = solved
        update = product(solved, side[...])
        schur_ref[here, :] = (trailing_ref[here, :].astype(jnp.float32) - update).astype(jnp.bfloat16)
        return carry

    if rows == chunk:
        step(0, 0)
    else:
        lax.fori_loop(0, rows // chunk, step, 0)
    own_ref[0] = group[pl.ds(pl.multiple_of(my_col * share, share), share), :]


def body(pivot_block, panel, lead, trailing):
    pivot_size, local_width = pivot_block.shape
    rows, cols = lax.axis_size("row"), lax.axis_size("col")
    share = panel.shape[1]
    col_index = lax.axis_index("col")
    vmem = pl.BlockSpec(memory_space=pltpu.VMEM)

    half = pivot_size // 2
    row_index = lax.axis_index("row")
    wide = pivot_block.astype(jnp.float32)
    diagonal_half = lax.dynamic_slice_in_dim(pivot_block, row_index // 2 * half, half, 0)
    far = lax.ppermute(diagonal_half, "row", [(d ^ 2, d) for d in range(rows)])
    far_mate = lax.ppermute(diagonal_half, "row", [(d ^ 3, d) for d in range(rows)])
    whole, _ = lax.optimization_barrier((pivot_block, diagonal_half))
    mate = lax.ppermute(whole, "row", [(d ^ 1, d) for d in range(rows)])
    pivots = [wide, mate, far, far_mate]

    done, first_lower = pl.pallas_call(
        functools.partial(first_kernel, "row"),
        out_shape=(
            jax.ShapeDtypeStruct((rows, LANES, LANES), jnp.float32),
            jax.ShapeDtypeStruct((LANES, LANES), jnp.float32),
        ),
        in_specs=[vmem] * len(pivots),
        out_specs=(vmem,) * 2,
        scratch_shapes=[pltpu.VMEM((rows, LANES, LANES), jnp.float32)],
        compiler_params=pltpu.CompilerParams(vmem_limit_bytes=32 * 1024 * 1024),
        cost_estimate=pl.CostEstimate(flops=3 * 10**8, bytes_accessed=10**6, transcendentals=10**5),
        name="first",
    )(*pivots)

    partly, second_lower = pl.pallas_call(
        functools.partial(second_kernel, "row"),
        out_shape=(
            jax.ShapeDtypeStruct((rows, pivot_size, LANES), jnp.float32),
            jax.ShapeDtypeStruct((LANES, LANES), jnp.float32),
        ),
        in_specs=[vmem] * (len(pivots) + 1),
        out_specs=(vmem,) * 2,
        compiler_params=pltpu.CompilerParams(vmem_limit_bytes=32 * 1024 * 1024),
        cost_estimate=pl.CostEstimate(flops=10**10, bytes_accessed=2 * 10**7, transcendentals=10**5),
        name="second",
    )(*pivots, done)

    def live(shards, rows_of):
        block = jnp.concatenate([(shard * share + jnp.arange(share)) // BLOCK for shard in shards])
        matches = block[:, None] == jnp.arange(lead.shape[1])[None, :]
        row_lead = jnp.sum(jnp.where(matches, lead, 0), axis=1)
        keep = (jnp.arange(pivot_size) // BLOCK)[None, :] >= row_lead[:, None]
        return jnp.where(keep, rows_of, jnp.zeros_like(rows_of))

    ratio = cols // rows
    paired = cols == 2 * rows and rows & (rows - 1) == 0

    def to_side(array, shift):
        pairs = []
        for r in range(rows):
            for c in range(cols):
                to_row, to_col = (c % rows + shift) % rows, r * ratio + c // rows
                pairs.append((c * rows + r, to_col * rows + to_row))
        return lax.ppermute(array, ("col", "row"), pairs)

    if paired:
        quad, _ = lax.optimization_barrier((panel[0], diagonal_half))
        step = 1
        while step < rows:
            pieces = (quad, lax.ppermute(quad, "col", [(d ^ step, d) for d in range(cols)]))
            step *= 2
            if step == rows:
                pieces, _ = lax.optimization_barrier((pieces, first_lower))
            quad = jnp.concatenate(pieces, axis=0)
        quad = live([col_index ^ p for p in range(rows)], quad)
        side = to_side(quad, 0)
        late, _ = lax.optimization_barrier((quad, (side, second_lower)))
        group = [quad, lax.ppermute(late, "col", [(d ^ rows, d) for d in range(cols)])]
    else:
        masked = live([col_index], panel[0])
        group = [lax.all_gather(masked, "col", axis=0, tiled=True)]
        side = jnp.concatenate([to_side(masked, s) for s in range(rows)], axis=0)

    own, high, low = pl.pallas_call(
        functools.partial(last_kernel, "row"),
        out_shape=(
            jax.ShapeDtypeStruct((pivot_size, local_width), jnp.float32),
            jax.ShapeDtypeStruct((pivot_size, pivot_size), jnp.bfloat16),
            jax.ShapeDtypeStruct((pivot_size, pivot_size), jnp.bfloat16),
        ),
        in_specs=[vmem] * 3,
        out_specs=(vmem,) * 3,
        scratch_shapes=[
            pltpu.VMEM((rows + 2, pivot_size + 2 * LANES, LANES), jnp.float32),
            pltpu.VMEM((rows, LANES, LANES), jnp.float32),
        ],
        compiler_params=pltpu.CompilerParams(vmem_limit_bytes=32 * 1024 * 1024),
        cost_estimate=pl.CostEstimate(flops=10**6, bytes_accessed=10**4, transcendentals=0),
        name="last",
    )(partly, first_lower, second_lower)

    group_rows = share * cols
    panel_factor, schur = pl.pallas_call(
        functools.partial(solve_kernel, "row", "col", True if paired else None, len(group)),
        out_shape=(
            jax.ShapeDtypeStruct(panel.shape, jnp.bfloat16),
            jax.ShapeDtypeStruct(trailing.shape, jnp.bfloat16),
        ),
        in_specs=[vmem] * (4 + len(group)),
        out_specs=(vmem,) * 2,
        scratch_shapes=[
            pltpu.VMEM((group_rows, pivot_size), jnp.bfloat16),
            pltpu.VMEM((share * rows, pivot_size), jnp.bfloat16),
        ],
        compiler_params=pltpu.CompilerParams(vmem_limit_bytes=48 * 1024 * 1024),
        cost_estimate=pl.CostEstimate(flops=4 * 10**8, bytes_accessed=2 * 10**6, transcendentals=0),
        name="solve",
    )(high, low, *group, side, trailing)
    return (own, panel_factor, schur)


def solution(mesh):
    return jax.shard_map(
        body,
        mesh=mesh,
        in_specs=(P(None, "row"), P("row", "col", None), P("row", None), P("row", "col")),
        out_specs=(P(None, "row"), P("row", "col", None), P("row", "col")),
        check_vma=False,
    )
```

```python
import functools

import jax
import jax.numpy as jnp
from jax import lax
from jax.experimental import pallas as pl
from jax.experimental.pallas import tpu as pltpu
from jax.sharding import PartitionSpec as P

BLOCK = 128
STRIP = 32
SUB = 16
GROUP = 8
LANES = 128


def split(value):
    high = value.astype(jnp.bfloat16)
    low = (value - high.astype(jnp.float32)).astype(jnp.bfloat16)
    return high, low


def row_of(value, row):
    return jnp.broadcast_to(value[row : row + 1, :], (GROUP, LANES))


def reciprocal(value):
    guess = pl.reciprocal(value, approx=True)
    return guess, 2.0 - value * guess


def eliminate_strip(strip, first):
    groups = STRIP // GROUP
    sublane = lax.broadcasted_iota(jnp.int32, (GROUP, LANES), 0)
    lane = lax.broadcasted_iota(jnp.int32, (GROUP, LANES), 1)
    zero = jnp.zeros((GROUP, LANES), jnp.float32)
    block = [strip[g * GROUP : (g + 1) * GROUP, :] for g in range(groups)]
    inside = (lane >= first) & (lane < first + STRIP)
    lower = [zero] * groups
    column = [None] * STRIP
    for k in range(0, STRIP, 2):
        if k % SUB == 0:
            for j in range(k, k + SUB):
                column[j] = [
                    jnp.broadcast_to(block[g][:, first + j : first + j + 1], (GROUP, LANES)) if g >= j // GROUP else None
                    for g in range(groups)
                ]
            taken = (lane >= first + k) & (lane < first + k + SUB)
            for g in range(groups):
                identity = jnp.where(lane - first == sublane + g * GROUP, 1.0, 0.0)
                block[g] = jnp.where(taken, identity, block[g])
        last = k - k % SUB + SUB
        home, sub = k // GROUP, k % GROUP
        u, v = column[k], column[k + 1]
        a = row_of(u[home], sub)
        b = row_of(u[home], sub + 1)
        c = row_of(v[home], sub + 1)
        det = a * c - b * b
        guess, correction = reciprocal(det)
        n1 = [None if g < home else c * u[g] - b * v[g] for g in range(groups)]
        n2 = [None if g < home else a * v[g] - b * u[g] for g in range(groups)]
        inverse = guess * correction
        w1 = [None if g < home else n1[g] * inverse for g in range(groups)]
        w2 = [None if g < home else n2[g] * inverse for g in range(groups)]
        for j in range(k + 2, last):
            at, row = j // GROUP, j % GROUP
            uj, vj = row_of(u[at], row), row_of(v[at], row)
            for g in range(at, groups):
                if j < k + 4:
                    step = ((n1[g] * uj + n2[g] * vj) * guess) * correction
                else:
                    step = w1[g] * uj + w2[g] * vj
                column[j][g] = column[j][g] - step
        root_a = lax.rsqrt(a)
        root_d = lax.rsqrt(a * det)
        for g in range(home, groups):
            lower[g] = jnp.where(lane == first + k, u[g] * root_a, lower[g])
            lower[g] = jnp.where(lane == first + k + 1, n2[g] * root_d, lower[g])
        t0, t1 = row_of(block[home], sub), row_of(block[home], sub + 1)
        for g in range(home, groups):
            step = w1[g] * t0 + w2[g] * t1
            if g > home:
                block[g] = block[g] - step
            elif sub + 2 < GROUP:
                block[g] = block[g] - jnp.where(sublane > sub + 1, step, 0.0)
        block[home] = jnp.where(sublane == sub, t0 * root_a, block[home])
        block[home] = jnp.where(sublane == sub + 1, (a * t1 - b * t0) * root_d, block[home])
    for g in range(groups):
        keep = (lane <= first + sublane + g * GROUP) & inside
        lower[g] = jnp.where(keep, lower[g], 0.0)
    return jnp.concatenate(block, axis=0), jnp.concatenate(lower, axis=0)


def matmul(left, right):
    return jnp.dot(left, right, preferred_element_type=jnp.float32)


def stacked(value):
    high, low = split(value)
    return jnp.concatenate([high, high, low, jnp.zeros_like(high)], axis=0)


def rows_at(block):
    return pl.ds(pl.multiple_of(block * LANES, LANES), LANES)


def square_iota(axis):
    return lax.broadcasted_iota(jnp.int32, (LANES, LANES), axis)


def beyond_strip():
    return square_iota(1) // STRIP > square_iota(0) // STRIP


def eliminate_block(rows, lower_ref):
    lane = square_iota(1)
    done = [[] for _ in rows]
    for first in range(0, LANES, STRIP):
        last = first + STRIP
        solved, diagonal = eliminate_strip(rows[0][:STRIP], first)
        lower_ref[first:last, :] = diagonal
        in_strip = (lane[:STRIP] >= first) & (lane[:STRIP] < last)
        high, low = split(jnp.where(in_strip, solved, 0.0))
        high, low = high.astype(jnp.float32), low.astype(jnp.float32)
        inverse = high if first == 0 else pltpu.roll(high, LANES - first, 1)
        inverse += pltpu.roll(low, (LANES + STRIP - first) % LANES, 1) if first != STRIP else low
        inverse += pltpu.roll(high, (LANES + 2 * STRIP - first) % LANES, 1) if first != 2 * STRIP else high
        inverse = inverse.astype(jnp.bfloat16)
        strips = [solved] + [matmul(inverse, stacked(part[:STRIP])) for part in rows[1:]]
        for part, strip in zip(done, strips):
            part.append(strip)
        if last == LANES:
            break
        high, low = split(solved)
        wide = jnp.concatenate([high, low, high, jnp.zeros_like(high)], axis=0).astype(jnp.float32)
        left = wide.T[last:, :].astype(jnp.bfloat16)
        under = [part[STRIP:] for part in rows]
        inside = (lane[last:] >= first) & (lane[last:] < last)
        under[0] = jnp.where(inside, 0.0, under[0])
        rows = [part - matmul(left, stacked(strip)) for part, strip in zip(under, strips)]
    return [jnp.concatenate(part, axis=0) for part in done]


def assemble(me, own, mate, far, far_mate, work, start, stop):
    size = own.shape[0]
    half = size // 2
    near = ((own, me), (mate, jnp.bitwise_xor(me, 1)))
    other = ((far, jnp.bitwise_xor(me, 2)), (far_mate, jnp.bitwise_xor(me, 3)))

    def place(parts, low, high, offset):
        low, high = max(low, start), min(high, stop)
        for part, column in parts:
            if low < high:
                work[column, low:high, :] = part[low - offset : high - offset, :].astype(jnp.float32)

    @pl.when(me < 2)
    def _():
        place(near, 0, half, 0)
        place(other, half, size, half)
        for row_block in range(start // LANES, min(half, stop) // LANES):
            for block in range(half // LANES, size // LANES):
                here = slice(block * LANES, (block + 1) * LANES)
                flipped = jnp.where(me == row_block, own[here, :], mate[here, :].astype(jnp.float32)).T
                work[block, row_block * LANES : (row_block + 1) * LANES, :] = flipped

    @pl.when(me >= 2)
    def _():
        place(near, 0, size, 0)
        place(other, 0, half, 0)


def first_kernel(axis, own, mate, far, far_mate, done_ref, lower_ref, work):
    count = lax.axis_size(axis)
    assemble(lax.axis_index(axis), own, mate, far, far_mate, work, 0, LANES)
    done = eliminate_block([work[d, :LANES, :] for d in range(count)], lower_ref)
    for d in range(count):
        done_ref[d] = done[d]


def rest_kernel(
    axis, own, mate, far, far_mate, done_ref, first_lower, own_ref, high_ref, low_ref, work, lower
):
    count = lax.axis_size(axis)
    me = lax.axis_index(axis)
    lane, row = square_iota(1), square_iota(0)
    beyond = beyond_strip()
    assemble(me, own, mate, far, far_mate, work, LANES, count * LANES)
    work[:count, :LANES, :] = done_ref[...]
    lower[0] = first_lower[...]

    def block_step(q, carry):
        before = q - 1
        places = [lax.rem(before + d, count) for d in range(count)]
        rights = [work[place, rows_at(before), :] for place in places]
        rights[0] = jnp.where(beyond, 0.0, rights[0])
        rights = [split(right) for right in rights]

        def update(target):
            high, low = split(work[target, rows_at(before), :].T)
            both = jnp.concatenate([high, low], axis=1)
            new = []
            for d, (place, (right_high, right_low)) in enumerate(zip(places, rights)):
                product = matmul(both, jnp.concatenate([right_high, right_high], axis=0)) + matmul(high, right_low)
                new.append(-product if d == 0 else work[place, rows_at(target), :] - product)
            return new

        rows = update(q)
        for target in (q + 1, q + 2):
            for place, new in zip(places, update(target)):
                work[place, rows_at(target), :] = new
        done = eliminate_block(rows[1:] + rows[:1], lower.at[q])
        for place, part in zip(places[1:] + places[:1], done):
            work[place, rows_at(q), :] = part
        return carry

    lax.fori_loop(1, count, block_step, 0)

    for i in range(count):
        block = work[i, rows_at(me), :]
        upper = jnp.where((i > me) | ((i == me) & beyond), block, 0.0)
        own_ref[i * LANES : (i + 1) * LANES, :] = upper.T + jnp.where(i == me, lower[i], 0.0)
        for c in range(count):
            block = work[c, i * LANES : (i + 1) * LANES, :]
            if c > i:
                block = jnp.zeros_like(block)
            elif c == i:
                block = jnp.where(lane <= row, block, 0.0)
            high, low = split(block)
            high_ref[i * LANES : (i + 1) * LANES, c * LANES : (c + 1) * LANES] = high
            low_ref[i * LANES : (i + 1) * LANES, c * LANES : (c + 1) * LANES] = low


def solve_kernel(row_axis, col_axis, orders, group_count, side_count, *refs):
    high_ref, low_ref = refs[:2]
    group_refs, side_refs = refs[2 : 2 + group_count], refs[2 + group_count : 2 + group_count + side_count]
    trailing_ref, own_ref, schur_ref, group, side = refs[2 + group_count + side_count :]
    size = high_ref.shape[0]
    half = size // 2
    share = own_ref.shape[1]
    my_row, my_col = lax.axis_index(row_axis), lax.axis_index(col_axis)

    def gather(parts, target, place):
        shard = 0
        for ref in parts:
            for first in range(0, ref.shape[0], share):
                at = pl.multiple_of(place(shard) * share, share)
                target[pl.ds(at, share), :] = ref[first : first + share, :]
                shard += 1

    if orders is None:
        count = len(side_refs)
        group[...] = group_refs[0][...]
        gather(side_refs, side, lambda i: lax.rem(my_row + count - i, count))
    else:
        gather(group_refs, group, lambda i: jnp.bitwise_xor(my_col, orders[0][i]))
        gather(side_refs, side, lambda i: jnp.bitwise_xor(my_row, orders[1][i]))
    contract = (((1,), (1,)), ((), ()))

    def product(left, right):
        return lax.dot_general(left, right, contract, preferred_element_type=jnp.float32)

    def solve(rows):
        first = product(rows[:, :half], high_ref[:half, :half]) + product(rows[:, :half], low_ref[:half, :half])
        second = product(rows, high_ref[half:, :]) + product(rows, low_ref[half:, :])
        return jnp.concatenate([first, second], axis=1).astype(jnp.bfloat16)

    side[...] = solve(side[...])
    rows = group.shape[0]
    chunk = min(rows, 256)

    def step(i, carry):
        here = pl.ds(pl.multiple_of(i * chunk, chunk), chunk)
        solved = solve(group[here, :])
        group[here, :] = solved
        update = product(solved, side[...])
        schur_ref[here, :] = (trailing_ref[here, :].astype(jnp.float32) - update).astype(jnp.bfloat16)
        return carry

    if rows == chunk:
        step(0, 0)
    else:
        lax.fori_loop(0, rows // chunk, step, 0)
    own_ref[0] = group[pl.ds(pl.multiple_of(my_col * share, share), share), :]


def body(pivot_block, panel, lead, trailing):
    pivot_size, local_width = pivot_block.shape
    rows, cols = lax.axis_size("row"), lax.axis_size("col")
    share = panel.shape[1]
    col_index = lax.axis_index("col")
    vmem = pl.BlockSpec(memory_space=pltpu.VMEM)

    half = pivot_size // 2
    row_index = lax.axis_index("row")
    wide = pivot_block.astype(jnp.float32)
    diagonal_half = lax.dynamic_slice_in_dim(pivot_block, row_index // 2 * half, half, 0)
    far = lax.ppermute(diagonal_half, "row", [(d ^ 2, d) for d in range(rows)])
    far_mate = lax.ppermute(diagonal_half, "row", [(d ^ 3, d) for d in range(rows)])
    whole, _ = lax.optimization_barrier((pivot_block, diagonal_half))
    mate = lax.ppermute(whole, "row", [(d ^ 1, d) for d in range(rows)])
    pivots = [wide, mate, far, far_mate]

    done, first_lower = pl.pallas_call(
        functools.partial(first_kernel, "row"),
        out_shape=(
            jax.ShapeDtypeStruct((rows, LANES, LANES), jnp.float32),
            jax.ShapeDtypeStruct((LANES, LANES), jnp.float32),
        ),
        in_specs=[vmem] * len(pivots),
        out_specs=(vmem,) * 2,
        scratch_shapes=[pltpu.VMEM((rows, LANES, LANES), jnp.float32)],
        compiler_params=pltpu.CompilerParams(vmem_limit_bytes=32 * 1024 * 1024),
        cost_estimate=pl.CostEstimate(flops=3 * 10**8, bytes_accessed=10**6, transcendentals=10**5),
        name="first",
    )(*pivots)

    def live(shards, rows_of):
        block = jnp.concatenate([(shard * share + jnp.arange(share)) // BLOCK for shard in shards])
        matches = block[:, None] == jnp.arange(lead.shape[1])[None, :]
        row_lead = jnp.sum(jnp.where(matches, lead, 0), axis=1)
        keep = (jnp.arange(pivot_size) // BLOCK)[None, :] >= row_lead[:, None]
        return jnp.where(keep, rows_of, jnp.zeros_like(rows_of))

    ratio = cols // rows
    paired = cols == 2 * rows and rows & (rows - 1) == 0

    def to_side(array, shift):
        pairs = []
        for r in range(rows):
            for c in range(cols):
                to_row, to_col = (c % rows + shift) % rows, r * ratio + c // rows
                pairs.append((c * rows + r, to_col * rows + to_row))
        return lax.ppermute(array, ("col", "row"), pairs)

    masked = live([col_index], panel[0])
    if paired:
        ready, _ = lax.optimization_barrier((masked, diagonal_half))
        group, group_order = ready, [0]
        side = to_side(ready, 0)
        col_steps = [rows >> i for i in range(rows.bit_length())]
        for i, step in enumerate(col_steps):
            pieces = [group, lax.ppermute(group, "col", [(d ^ step, d) for d in range(cols)])]
            group_order = group_order + [shard ^ step for shard in group_order]
            if i + 1 < len(col_steps):
                if i == 0:
                    pieces, side = lax.optimization_barrier((pieces, side))
                if i + 2 == len(col_steps):
                    pieces, _ = lax.optimization_barrier((pieces, first_lower))
                group = jnp.concatenate(pieces, axis=0)
        group = pieces
        side, _ = lax.optimization_barrier((side, first_lower))
        side_order = list(range(rows))
        side = [side] + [lax.ppermute(side, "row", [(d ^ p, d) for d in range(rows)]) for p in side_order[1:]]
        orders = (group_order, side_order)
    else:
        group = [lax.all_gather(masked, "col", axis=0, tiled=True)]
        side = [to_side(masked, s) for s in range(rows)]
        orders = None

    own, high, low = pl.pallas_call(
        functools.partial(rest_kernel, "row"),
        out_shape=(
            jax.ShapeDtypeStruct((pivot_size, local_width), jnp.float32),
            jax.ShapeDtypeStruct((pivot_size, pivot_size), jnp.bfloat16),
            jax.ShapeDtypeStruct((pivot_size, pivot_size), jnp.bfloat16),
        ),
        in_specs=[vmem] * (len(pivots) + 2),
        out_specs=(vmem,) * 3,
        scratch_shapes=[
            pltpu.VMEM((rows + 2, pivot_size + 2 * LANES, LANES), jnp.float32),
            pltpu.VMEM((rows, LANES, LANES), jnp.float32),
        ],
        compiler_params=pltpu.CompilerParams(vmem_limit_bytes=32 * 1024 * 1024),
        cost_estimate=pl.CostEstimate(flops=10**9, bytes_accessed=2 * 10**6, transcendentals=10**5),
        name="rest",
    )(*pivots, done, first_lower)

    group_rows = share * cols
    panel_factor, schur = pl.pallas_call(
        functools.partial(solve_kernel, "row", "col", orders, len(group), len(side)),
        out_shape=(
            jax.ShapeDtypeStruct(panel.shape, jnp.bfloat16),
            jax.ShapeDtypeStruct(trailing.shape, jnp.bfloat16),
        ),
        in_specs=[vmem] * (3 + len(group) + len(side)),
        out_specs=(vmem,) * 2,
        scratch_shapes=[
            pltpu.VMEM((group_rows, pivot_size), jnp.bfloat16),
            pltpu.VMEM((share * rows, pivot_size), jnp.bfloat16),
        ],
        compiler_params=pltpu.CompilerParams(vmem_limit_bytes=48 * 1024 * 1024),
        cost_estimate=pl.CostEstimate(flops=4 * 10**8, bytes_accessed=2 * 10**6, transcendentals=0),
        name="solve",
    )(high, low, *group, *side, trailing)
    return (own, panel_factor, schur)


def solution(mesh):
    return jax.shard_map(
        body,
        mesh=mesh,
        in_specs=(P(None, "row"), P("row", "col", None), P("row", None), P("row", "col")),
        out_specs=(P(None, "row"), P("row", "col", None), P("row", "col")),
        check_vma=False,
    )
```

```python
import functools

import jax
import jax.numpy as jnp
from jax import lax
from jax.experimental import pallas as pl
from jax.experimental.pallas import tpu as pltpu
from jax.sharding import PartitionSpec as P

BLOCK = 128
STRIP = 32
SUB = 16
GROUP = 8
LANES = 128


def split(value):
    high = value.astype(jnp.bfloat16)
    low = (value - high.astype(jnp.float32)).astype(jnp.bfloat16)
    return high, low


def row_of(value, row):
    return jnp.broadcast_to(value[row : row + 1, :], (GROUP, LANES))


def reciprocal(value):
    guess = pl.reciprocal(value, approx=True)
    return guess, 2.0 - value * guess


def eliminate_strip(strip, first):
    groups = STRIP // GROUP
    sublane = lax.broadcasted_iota(jnp.int32, (GROUP, LANES), 0)
    lane = lax.broadcasted_iota(jnp.int32, (GROUP, LANES), 1)
    zero = jnp.zeros((GROUP, LANES), jnp.float32)
    block = [strip[g * GROUP : (g + 1) * GROUP, :] for g in range(groups)]
    inside = (lane >= first) & (lane < first + STRIP)
    lower = [zero] * groups
    column = [None] * STRIP
    for k in range(0, STRIP, 2):
        if k % SUB == 0:
            for j in range(k, k + SUB):
                column[j] = [
                    jnp.broadcast_to(block[g][:, first + j : first + j + 1], (GROUP, LANES)) if g >= j // GROUP else None
                    for g in range(groups)
                ]
            taken = (lane >= first + k) & (lane < first + k + SUB)
            for g in range(groups):
                identity = jnp.where(lane - first == sublane + g * GROUP, 1.0, 0.0)
                block[g] = jnp.where(taken, identity, block[g])
        last = k - k % SUB + SUB
        home, sub = k // GROUP, k % GROUP
        u, v = column[k], column[k + 1]
        a = row_of(u[home], sub)
        b = row_of(u[home], sub + 1)
        c = row_of(v[home], sub + 1)
        det = a * c - b * b
        guess, correction = reciprocal(det)
        n1 = [None if g < home else c * u[g] - b * v[g] for g in range(groups)]
        n2 = [None if g < home else a * v[g] - b * u[g] for g in range(groups)]
        inverse = guess * correction
        w1 = [None if g < home else n1[g] * inverse for g in range(groups)]
        w2 = [None if g < home else n2[g] * inverse for g in range(groups)]
        for j in range(k + 2, last):
            at, row = j // GROUP, j % GROUP
            uj, vj = row_of(u[at], row), row_of(v[at], row)
            for g in range(at, groups):
                if j < k + 4:
                    step = ((n1[g] * uj + n2[g] * vj) * guess) * correction
                else:
                    step = w1[g] * uj + w2[g] * vj
                column[j][g] = column[j][g] - step
        root_a = lax.rsqrt(a)
        root_d = lax.rsqrt(a * det)
        for g in range(home, groups):
            lower[g] = jnp.where(lane == first + k, u[g] * root_a, lower[g])
            lower[g] = jnp.where(lane == first + k + 1, n2[g] * root_d, lower[g])
        t0, t1 = row_of(block[home], sub), row_of(block[home], sub + 1)
        for g in range(home, groups):
            step = w1[g] * t0 + w2[g] * t1
            if g > home:
                block[g] = block[g] - step
            elif sub + 2 < GROUP:
                block[g] = block[g] - jnp.where(sublane > sub + 1, step, 0.0)
        block[home] = jnp.where(sublane == sub, t0 * root_a, block[home])
        block[home] = jnp.where(sublane == sub + 1, (a * t1 - b * t0) * root_d, block[home])
    for g in range(groups):
        keep = (lane <= first + sublane + g * GROUP) & inside
        lower[g] = jnp.where(keep, lower[g], 0.0)
    return jnp.concatenate(block, axis=0), jnp.concatenate(lower, axis=0)


def matmul(left, right):
    return jnp.dot(left, right, preferred_element_type=jnp.float32)


def stacked(value):
    high, low = split(value)
    return jnp.concatenate([high, high, low, jnp.zeros_like(high)], axis=0)


def rows_at(block):
    return pl.ds(pl.multiple_of(block * LANES, LANES), LANES)


def square_iota(axis):
    return lax.broadcasted_iota(jnp.int32, (LANES, LANES), axis)


def beyond_strip():
    return square_iota(1) // STRIP > square_iota(0) // STRIP


def eliminate_block(rows, lower_ref):
    lane = square_iota(1)
    done = [[] for _ in rows]
    for first in range(0, LANES, STRIP):
        last = first + STRIP
        solved, diagonal = eliminate_strip(rows[0][:STRIP], first)
        lower_ref[first:last, :] = diagonal
        in_strip = (lane[:STRIP] >= first) & (lane[:STRIP] < last)
        high, low = split(jnp.where(in_strip, solved, 0.0))
        high, low = high.astype(jnp.float32), low.astype(jnp.float32)
        inverse = high if first == 0 else pltpu.roll(high, LANES - first, 1)
        inverse += pltpu.roll(low, (LANES + STRIP - first) % LANES, 1) if first != STRIP else low
        inverse += pltpu.roll(high, (LANES + 2 * STRIP - first) % LANES, 1) if first != 2 * STRIP else high
        inverse = inverse.astype(jnp.bfloat16)
        strips = [solved] + [matmul(inverse, stacked(part[:STRIP])) for part in rows[1:]]
        for part, strip in zip(done, strips):
            part.append(strip)
        if last == LANES:
            break
        high, low = split(solved)
        wide = jnp.concatenate([high, low, high, jnp.zeros_like(high)], axis=0).astype(jnp.float32)
        left = wide.T[last:, :].astype(jnp.bfloat16)
        under = [part[STRIP:] for part in rows]
        inside = (lane[last:] >= first) & (lane[last:] < last)
        under[0] = jnp.where(inside, 0.0, under[0])
        rows = [part - matmul(left, stacked(strip)) for part, strip in zip(under, strips)]
    return [jnp.concatenate(part, axis=0) for part in done]


def assemble(me, own, mate, far, far_mate, work, start, stop):
    size = own.shape[0]
    half = size // 2
    near = ((own, me), (mate, jnp.bitwise_xor(me, 1)))
    other = ((far, jnp.bitwise_xor(me, 2)), (far_mate, jnp.bitwise_xor(me, 3)))

    def place(parts, low, high, offset):
        low, high = max(low, start), min(high, stop)
        for part, column in parts:
            if low < high:
                work[column, low:high, :] = part[low - offset : high - offset, :].astype(jnp.float32)

    @pl.when(me < 2)
    def _():
        place(near, 0, half, 0)
        place(other, half, size, half)
        for row_block in range(start // LANES, min(half, stop) // LANES):
            for block in range(half // LANES, size // LANES):
                here = slice(block * LANES, (block + 1) * LANES)
                flipped = jnp.where(me == row_block, own[here, :], mate[here, :].astype(jnp.float32)).T
                work[block, row_block * LANES : (row_block + 1) * LANES, :] = flipped

    @pl.when(me >= 2)
    def _():
        place(near, 0, size, 0)
        place(other, 0, half, 0)


def first_kernel(axis, own, mate, far, far_mate, done_ref, lower_ref, work):
    count = lax.axis_size(axis)
    assemble(lax.axis_index(axis), own, mate, far, far_mate, work, 0, LANES)
    done = eliminate_block([work[d, :LANES, :] for d in range(count)], lower_ref)
    for d in range(count):
        done_ref[d] = done[d]


def rest_kernel(
    axis, own, mate, far, far_mate, done_ref, first_lower, own_ref, high_ref, low_ref, work, lower
):
    count = lax.axis_size(axis)
    me = lax.axis_index(axis)
    lane, row = square_iota(1), square_iota(0)
    beyond = beyond_strip()
    assemble(me, own, mate, far, far_mate, work, LANES, count * LANES)
    work[:count, :LANES, :] = done_ref[...]
    lower[0] = first_lower[...]

    def block_step(q, carry):
        before = q - 1
        places = [lax.rem(before + d, count) for d in range(count)]
        rights = [work[place, rows_at(before), :] for place in places]
        rights[0] = jnp.where(beyond, 0.0, rights[0])
        rights = [split(right) for right in rights]

        def update(target):
            high, low = split(work[target, rows_at(before), :].T)
            both = jnp.concatenate([high, low], axis=1)
            new = []
            for d, (place, (right_high, right_low)) in enumerate(zip(places, rights)):
                product = matmul(both, jnp.concatenate([right_high, right_high], axis=0)) + matmul(high, right_low)
                new.append(-product if d == 0 else work[place, rows_at(target), :] - product)
            return new

        rows = update(q)
        for target in (q + 1, q + 2):
            for place, new in zip(places, update(target)):
                work[place, rows_at(target), :] = new
        done = eliminate_block(rows[1:] + rows[:1], lower.at[q])
        for place, part in zip(places[1:] + places[:1], done):
            work[place, rows_at(q), :] = part
        return carry

    lax.fori_loop(1, count, block_step, 0)

    for i in range(count):
        block = work[i, rows_at(me), :]
        upper = jnp.where((i > me) | ((i == me) & beyond), block, 0.0)
        own_ref[i * LANES : (i + 1) * LANES, :] = upper.T + jnp.where(i == me, lower[i], 0.0)
        for c in range(count):
            block = work[c, i * LANES : (i + 1) * LANES, :]
            if c > i:
                block = jnp.zeros_like(block)
            elif c == i:
                block = jnp.where(lane <= row, block, 0.0)
            high, low = split(block)
            high_ref[i * LANES : (i + 1) * LANES, c * LANES : (c + 1) * LANES] = high
            low_ref[i * LANES : (i + 1) * LANES, c * LANES : (c + 1) * LANES] = low


def solve_kernel(row_axis, col_axis, order, group_count, *refs):
    high_ref, low_ref = refs[:2]
    inputs = refs[2 : 3 + group_count]
    trailing_ref, own_ref, schur_ref, group, side = refs[3 + group_count :]
    size = high_ref.shape[0]
    half = size // 2
    share = own_ref.shape[1]
    count = side.shape[0] // share
    my_row, my_col = lax.axis_index(row_axis), lax.axis_index(col_axis)
    for i, ref in enumerate(inputs[:-1]):
        if order is None:
            group[...] = ref[...]
        else:
            for p in range(count):
                at = jnp.bitwise_xor(my_col, i * count + p) * share
                group[pl.ds(pl.multiple_of(at, share), share), :] = ref[p * share : (p + 1) * share, :]
    for p in range(count):
        place = jnp.bitwise_xor(my_row, p) if order else lax.rem(my_row + count - p, count)
        side[pl.ds(pl.multiple_of(place * share, share), share), :] = inputs[-1][p * share : (p + 1) * share, :]
    contract = (((1,), (1,)), ((), ()))

    def product(left, right):
        return lax.dot_general(left, right, contract, preferred_element_type=jnp.float32)

    def solve(rows):
        first = product(rows[:, :half], high_ref[:half, :half]) + product(rows[:, :half], low_ref[:half, :half])
        second = product(rows, high_ref[half:, :]) + product(rows, low_ref[half:, :])
        return jnp.concatenate([first, second], axis=1).astype(jnp.bfloat16)

    side[...] = solve(side[...])
    rows = group.shape[0]
    chunk = min(rows, 256)

    def step(i, carry):
        here = pl.ds(pl.multiple_of(i * chunk, chunk), chunk)
        solved = solve(group[here, :])
        group[here, :] = solved
        update = product(solved, side[...])
        schur_ref[here, :] = (trailing_ref[here, :].astype(jnp.float32) - update).astype(jnp.bfloat16)
        return carry

    if rows == chunk:
        step(0, 0)
    else:
        lax.fori_loop(0, rows // chunk, step, 0)
    own_ref[0] = group[pl.ds(pl.multiple_of(my_col * share, share), share), :]


def body(pivot_block, panel, lead, trailing):
    pivot_size, local_width = pivot_block.shape
    rows, cols = lax.axis_size("row"), lax.axis_size("col")
    share = panel.shape[1]
    col_index = lax.axis_index("col")
    vmem = pl.BlockSpec(memory_space=pltpu.VMEM)

    half = pivot_size // 2
    row_index = lax.axis_index("row")
    wide = pivot_block.astype(jnp.float32)
    diagonal_half = lax.dynamic_slice_in_dim(pivot_block, row_index // 2 * half, half, 0)
    far = lax.ppermute(diagonal_half, "row", [(d ^ 2, d) for d in range(rows)])
    far_mate = lax.ppermute(diagonal_half, "row", [(d ^ 3, d) for d in range(rows)])
    mate = lax.ppermute(pivot_block, "row", [(d ^ 1, d) for d in range(rows)])
    pivots = [wide, mate, far, far_mate]

    done, first_lower = pl.pallas_call(
        functools.partial(first_kernel, "row"),
        out_shape=(
            jax.ShapeDtypeStruct((rows, LANES, LANES), jnp.float32),
            jax.ShapeDtypeStruct((LANES, LANES), jnp.float32),
        ),
        in_specs=[vmem] * len(pivots),
        out_specs=(vmem,) * 2,
        scratch_shapes=[pltpu.VMEM((rows, LANES, LANES), jnp.float32)],
        compiler_params=pltpu.CompilerParams(vmem_limit_bytes=32 * 1024 * 1024),
        cost_estimate=pl.CostEstimate(flops=3 * 10**8, bytes_accessed=10**6, transcendentals=10**5),
        name="first",
    )(*pivots)

    def live(shards, rows_of):
        block = jnp.concatenate([(shard * share + jnp.arange(share)) // BLOCK for shard in shards])
        matches = block[:, None] == jnp.arange(lead.shape[1])[None, :]
        row_lead = jnp.sum(jnp.where(matches, lead, 0), axis=1)
        keep = (jnp.arange(pivot_size) // BLOCK)[None, :] >= row_lead[:, None]
        return jnp.where(keep, rows_of, jnp.zeros_like(rows_of))

    ratio = cols // rows
    paired = cols == 2 * rows and rows & (rows - 1) == 0

    def to_side(array, shift):
        pairs = []
        for r in range(rows):
            for c in range(cols):
                to_row, to_col = (c % rows + shift) % rows, r * ratio + c // rows
                pairs.append((c * rows + r, to_col * rows + to_row))
        return lax.ppermute(array, ("col", "row"), pairs)

    if paired:
        quad, _ = lax.optimization_barrier((panel[0], diagonal_half))
        step = 1
        while step < rows:
            pieces = (quad, lax.ppermute(quad, "col", [(d ^ step, d) for d in range(cols)]))
            step *= 2
            if step == rows:
                pieces, _ = lax.optimization_barrier((pieces, first_lower))
            quad = jnp.concatenate(pieces, axis=0)
        quad = live([col_index ^ p for p in range(rows)], quad)
        group = [quad, lax.ppermute(quad, "col", [(d ^ rows, d) for d in range(cols)])]
        side = to_side(quad, 0)
    else:
        masked = live([col_index], panel[0])
        group = [lax.all_gather(masked, "col", axis=0, tiled=True)]
        side = jnp.concatenate([to_side(masked, s) for s in range(rows)], axis=0)

    own, high, low = pl.pallas_call(
        functools.partial(rest_kernel, "row"),
        out_shape=(
            jax.ShapeDtypeStruct((pivot_size, local_width), jnp.float32),
            jax.ShapeDtypeStruct((pivot_size, pivot_size), jnp.bfloat16),
            jax.ShapeDtypeStruct((pivot_size, pivot_size), jnp.bfloat16),
        ),
        in_specs=[vmem] * (len(pivots) + 2),
        out_specs=(vmem,) * 3,
        scratch_shapes=[
            pltpu.VMEM((rows + 2, pivot_size + 2 * LANES, LANES), jnp.float32),
            pltpu.VMEM((rows, LANES, LANES), jnp.float32),
        ],
        compiler_params=pltpu.CompilerParams(vmem_limit_bytes=32 * 1024 * 1024),
        cost_estimate=pl.CostEstimate(flops=10**9, bytes_accessed=2 * 10**6, transcendentals=10**5),
        name="rest",
    )(*pivots, done, first_lower)

    group_rows = share * cols
    panel_factor, schur = pl.pallas_call(
        functools.partial(solve_kernel, "row", "col", True if paired else None, len(group)),
        out_shape=(
            jax.ShapeDtypeStruct(panel.shape, jnp.bfloat16),
            jax.ShapeDtypeStruct(trailing.shape, jnp.bfloat16),
        ),
        in_specs=[vmem] * (4 + len(group)),
        out_specs=(vmem,) * 2,
        scratch_shapes=[
            pltpu.VMEM((group_rows, pivot_size), jnp.bfloat16),
            pltpu.VMEM((share * rows, pivot_size), jnp.bfloat16),
        ],
        compiler_params=pltpu.CompilerParams(vmem_limit_bytes=48 * 1024 * 1024),
        cost_estimate=pl.CostEstimate(flops=4 * 10**8, bytes_accessed=2 * 10**6, transcendentals=0),
        name="solve",
    )(high, low, *group, side, trailing)
    return (own, panel_factor, schur)


def solution(mesh):
    return jax.shard_map(
        body,
        mesh=mesh,
        in_specs=(P(None, "row"), P("row", "col", None), P("row", None), P("row", "col")),
        out_specs=(P(None, "row"), P("row", "col", None), P("row", "col")),
        check_vma=False,
    )
```

```python
import functools

import jax
import jax.numpy as jnp
from jax import lax
from jax.experimental import pallas as pl
from jax.experimental.pallas import tpu as pltpu
from jax.sharding import PartitionSpec as P

BLOCK = 128
STRIP = 32
SUB = 16
GROUP = 8
LANES = 128


def split(value):
    high = value.astype(jnp.bfloat16)
    low = (value - high.astype(jnp.float32)).astype(jnp.bfloat16)
    return high, low


def row_of(value, row):
    return jnp.broadcast_to(value[row : row + 1, :], (GROUP, LANES))


def reciprocal(value):
    guess = pl.reciprocal(value, approx=True)
    return guess, 2.0 - value * guess


def eliminate_strip(strip, first):
    groups = STRIP // GROUP
    sublane = lax.broadcasted_iota(jnp.int32, (GROUP, LANES), 0)
    lane = lax.broadcasted_iota(jnp.int32, (GROUP, LANES), 1)
    zero = jnp.zeros((GROUP, LANES), jnp.float32)
    block = [strip[g * GROUP : (g + 1) * GROUP, :] for g in range(groups)]
    inside = (lane >= first) & (lane < first + STRIP)
    lower = [zero] * groups
    column = [None] * STRIP
    for k in range(0, STRIP, 2):
        if k % SUB == 0:
            for j in range(k, k + SUB):
                column[j] = [
                    jnp.broadcast_to(block[g][:, first + j : first + j + 1], (GROUP, LANES)) if g >= j // GROUP else None
                    for g in range(groups)
                ]
            taken = (lane >= first + k) & (lane < first + k + SUB)
            for g in range(groups):
                identity = jnp.where(lane - first == sublane + g * GROUP, 1.0, 0.0)
                block[g] = jnp.where(taken, identity, block[g])
        last = k - k % SUB + SUB
        home, sub = k // GROUP, k % GROUP
        u, v = column[k], column[k + 1]
        a = row_of(u[home], sub)
        b = row_of(u[home], sub + 1)
        c = row_of(v[home], sub + 1)
        det = a * c - b * b
        guess, correction = reciprocal(det)
        n1 = [None if g < home else c * u[g] - b * v[g] for g in range(groups)]
        n2 = [None if g < home else a * v[g] - b * u[g] for g in range(groups)]
        inverse = guess * correction
        w1 = [None if g < home else n1[g] * inverse for g in range(groups)]
        w2 = [None if g < home else n2[g] * inverse for g in range(groups)]
        for j in range(k + 2, last):
            at, row = j // GROUP, j % GROUP
            uj, vj = row_of(u[at], row), row_of(v[at], row)
            for g in range(at, groups):
                if j < k + 4:
                    step = (n1[g] * uj + n2[g] * vj) * inverse
                else:
                    step = w1[g] * uj + w2[g] * vj
                column[j][g] = column[j][g] - step
        root_a = lax.rsqrt(a)
        root_d = lax.rsqrt(a * det)
        for g in range(home, groups):
            lower[g] = jnp.where(lane == first + k, u[g] * root_a, lower[g])
            lower[g] = jnp.where(lane == first + k + 1, n2[g] * root_d, lower[g])
        t0, t1 = row_of(block[home], sub), row_of(block[home], sub + 1)
        for g in range(home, groups):
            step = w1[g] * t0 + w2[g] * t1
            if g > home:
                block[g] = block[g] - step
            elif sub + 2 < GROUP:
                block[g] = block[g] - jnp.where(sublane > sub + 1, step, 0.0)
        block[home] = jnp.where(sublane == sub, t0 * root_a, block[home])
        block[home] = jnp.where(sublane == sub + 1, (a * t1 - b * t0) * root_d, block[home])
    for g in range(groups):
        keep = (lane <= first + sublane + g * GROUP) & inside
        lower[g] = jnp.where(keep, lower[g], 0.0)
    return jnp.concatenate(block, axis=0), jnp.concatenate(lower, axis=0)


def matmul(left, right):
    return jnp.dot(left, right, preferred_element_type=jnp.float32)


def stacked(value):
    high, low = split(value)
    return jnp.concatenate([high, high, low, jnp.zeros_like(high)], axis=0)


def rows_at(block):
    return pl.ds(pl.multiple_of(block * LANES, LANES), LANES)


def square_iota(axis):
    return lax.broadcasted_iota(jnp.int32, (LANES, LANES), axis)


def beyond_strip():
    return square_iota(1) // STRIP > square_iota(0) // STRIP


def eliminate_block(rows, lower_ref):
    lane = square_iota(1)
    done = [[] for _ in rows]
    for first in range(0, LANES, STRIP):
        last = first + STRIP
        solved, diagonal = eliminate_strip(rows[0][:STRIP], first)
        lower_ref[first:last, :] = diagonal
        in_strip = (lane[:STRIP] >= first) & (lane[:STRIP] < last)
        high, low = split(jnp.where(in_strip, solved, 0.0))
        high, low = high.astype(jnp.float32), low.astype(jnp.float32)
        inverse = high if first == 0 else pltpu.roll(high, LANES - first, 1)
        inverse += pltpu.roll(low, (LANES + STRIP - first) % LANES, 1) if first != STRIP else low
        inverse += pltpu.roll(high, (LANES + 2 * STRIP - first) % LANES, 1) if first != 2 * STRIP else high
        inverse = inverse.astype(jnp.bfloat16)
        strips = [solved] + [matmul(inverse, stacked(part[:STRIP])) for part in rows[1:]]
        for part, strip in zip(done, strips):
            part.append(strip)
        if last == LANES:
            break
        high, low = split(solved)
        wide = jnp.concatenate([high, low, high, jnp.zeros_like(high)], axis=0).astype(jnp.float32)
        left = wide.T[last:, :].astype(jnp.bfloat16)
        under = [part[STRIP:] for part in rows]
        inside = (lane[last:] >= first) & (lane[last:] < last)
        under[0] = jnp.where(inside, 0.0, under[0])
        rows = [part - matmul(left, stacked(strip)) for part, strip in zip(under, strips)]
    return [jnp.concatenate(part, axis=0) for part in done]


def assemble(me, own, mate, far, far_mate, work, start, stop):
    size = own.shape[0]
    half = size // 2
    near = ((own, me), (mate, jnp.bitwise_xor(me, 1)))
    other = ((far, jnp.bitwise_xor(me, 2)), (far_mate, jnp.bitwise_xor(me, 3)))

    def place(parts, low, high, offset):
        low, high = max(low, start), min(high, stop)
        for part, column in parts:
            if low < high:
                work[column, low:high, :] = part[low - offset : high - offset, :].astype(jnp.float32)

    @pl.when(me < 2)
    def _():
        place(near, 0, half, 0)
        place(other, half, size, half)
        for row_block in range(start // LANES, min(half, stop) // LANES):
            for block in range(half // LANES, size // LANES):
                here = slice(block * LANES, (block + 1) * LANES)
                flipped = jnp.where(me == row_block, own[here, :], mate[here, :].astype(jnp.float32)).T
                work[block, row_block * LANES : (row_block + 1) * LANES, :] = flipped

    @pl.when(me >= 2)
    def _():
        place(near, 0, size, 0)
        place(other, 0, half, 0)


def first_kernel(axis, own, mate, far, far_mate, done_ref, lower_ref, work):
    count = lax.axis_size(axis)
    assemble(lax.axis_index(axis), own, mate, far, far_mate, work, 0, LANES)
    done = eliminate_block([work[d, :LANES, :] for d in range(count)], lower_ref)
    for d in range(count):
        done_ref[d] = done[d]


def rest_kernel(
    axis, own, mate, far, far_mate, done_ref, first_lower, own_ref, high_ref, low_ref, work, lower
):
    count = lax.axis_size(axis)
    me = lax.axis_index(axis)
    lane, row = square_iota(1), square_iota(0)
    beyond = beyond_strip()
    assemble(me, own, mate, far, far_mate, work, LANES, count * LANES)
    work[:count, :LANES, :] = done_ref[...]
    lower[0] = first_lower[...]

    def block_step(q, carry):
        before = q - 1
        places = [lax.rem(before + d, count) for d in range(count)]
        rights = [work[place, rows_at(before), :] for place in places]
        rights[0] = jnp.where(beyond, 0.0, rights[0])
        rights = [split(right) for right in rights]

        def update(target):
            high, low = split(work[target, rows_at(before), :].T)
            both = jnp.concatenate([high, low], axis=1)
            new = []
            for d, (place, (right_high, right_low)) in enumerate(zip(places, rights)):
                product = matmul(both, jnp.concatenate([right_high, right_high], axis=0)) + matmul(high, right_low)
                new.append(-product if d == 0 else work[place, rows_at(target), :] - product)
            return new

        rows = update(q)
        for target in (q + 1, q + 2):
            for place, new in zip(places, update(target)):
                work[place, rows_at(target), :] = new
        done = eliminate_block(rows[1:] + rows[:1], lower.at[q])
        for place, part in zip(places[1:] + places[:1], done):
            work[place, rows_at(q), :] = part
        return carry

    lax.fori_loop(1, count, block_step, 0)

    for i in range(count):
        block = work[i, rows_at(me), :]
        upper = jnp.where((i > me) | ((i == me) & beyond), block, 0.0)
        own_ref[i * LANES : (i + 1) * LANES, :] = upper.T + jnp.where(i == me, lower[i], 0.0)
        for c in range(count):
            block = work[c, i * LANES : (i + 1) * LANES, :]
            if c > i:
                block = jnp.zeros_like(block)
            elif c == i:
                block = jnp.where(lane <= row, block, 0.0)
            high, low = split(block)
            high_ref[i * LANES : (i + 1) * LANES, c * LANES : (c + 1) * LANES] = high
            low_ref[i * LANES : (i + 1) * LANES, c * LANES : (c + 1) * LANES] = low


def solve_kernel(row_axis, col_axis, order, group_count, *refs):
    high_ref, low_ref = refs[:2]
    inputs = refs[2 : 3 + group_count]
    trailing_ref, own_ref, schur_ref, group, side = refs[3 + group_count :]
    size = high_ref.shape[0]
    half = size // 2
    share = own_ref.shape[1]
    count = side.shape[0] // share
    my_row, my_col = lax.axis_index(row_axis), lax.axis_index(col_axis)
    for i, ref in enumerate(inputs[:-1]):
        if order is None:
            group[...] = ref[...]
        else:
            for p in range(count):
                at = jnp.bitwise_xor(my_col, i * count + p) * share
                group[pl.ds(pl.multiple_of(at, share), share), :] = ref[p * share : (p + 1) * share, :]
    for p in range(count):
        place = jnp.bitwise_xor(my_row, p) if order else lax.rem(my_row + count - p, count)
        side[pl.ds(pl.multiple_of(place * share, share), share), :] = inputs[-1][p * share : (p + 1) * share, :]
    contract = (((1,), (1,)), ((), ()))

    def product(left, right):
        return lax.dot_general(left, right, contract, preferred_element_type=jnp.float32)

    def solve(rows):
        first = product(rows[:, :half], high_ref[:half, :half]) + product(rows[:, :half], low_ref[:half, :half])
        second = product(rows, high_ref[half:, :]) + product(rows, low_ref[half:, :])
        return jnp.concatenate([first, second], axis=1).astype(jnp.bfloat16)

    side[...] = solve(side[...])
    rows = group.shape[0]
    chunk = min(rows, 256)

    def step(i, carry):
        here = pl.ds(pl.multiple_of(i * chunk, chunk), chunk)
        solved = solve(group[here, :])
        group[here, :] = solved
        update = product(solved, side[...])
        schur_ref[here, :] = (trailing_ref[here, :].astype(jnp.float32) - update).astype(jnp.bfloat16)
        return carry

    if rows == chunk:
        step(0, 0)
    else:
        lax.fori_loop(0, rows // chunk, step, 0)
    own_ref[0] = group[pl.ds(pl.multiple_of(my_col * share, share), share), :]


def body(pivot_block, panel, lead, trailing):
    pivot_size, local_width = pivot_block.shape
    rows, cols = lax.axis_size("row"), lax.axis_size("col")
    share = panel.shape[1]
    col_index = lax.axis_index("col")
    vmem = pl.BlockSpec(memory_space=pltpu.VMEM)

    half = pivot_size // 2
    row_index = lax.axis_index("row")
    wide = pivot_block.astype(jnp.float32)
    diagonal_half = lax.dynamic_slice_in_dim(pivot_block, row_index // 2 * half, half, 0)
    far = lax.ppermute(diagonal_half, "row", [(d ^ 2, d) for d in range(rows)])
    far_mate = lax.ppermute(diagonal_half, "row", [(d ^ 3, d) for d in range(rows)])
    mate = lax.ppermute(pivot_block, "row", [(d ^ 1, d) for d in range(rows)])
    pivots = [wide, mate, far, far_mate]

    done, first_lower = pl.pallas_call(
        functools.partial(first_kernel, "row"),
        out_shape=(
            jax.ShapeDtypeStruct((rows, LANES, LANES), jnp.float32),
            jax.ShapeDtypeStruct((LANES, LANES), jnp.float32),
        ),
        in_specs=[vmem] * len(pivots),
        out_specs=(vmem,) * 2,
        scratch_shapes=[pltpu.VMEM((rows, LANES, LANES), jnp.float32)],
        compiler_params=pltpu.CompilerParams(vmem_limit_bytes=32 * 1024 * 1024),
        cost_estimate=pl.CostEstimate(flops=3 * 10**8, bytes_accessed=10**6, transcendentals=10**5),
        name="first",
    )(*pivots)

    def live(shards, rows_of):
        block = jnp.concatenate([(shard * share + jnp.arange(share)) // BLOCK for shard in shards])
        matches = block[:, None] == jnp.arange(lead.shape[1])[None, :]
        row_lead = jnp.sum(jnp.where(matches, lead, 0), axis=1)
        keep = (jnp.arange(pivot_size) // BLOCK)[None, :] >= row_lead[:, None]
        return jnp.where(keep, rows_of, jnp.zeros_like(rows_of))

    ratio = cols // rows
    paired = cols == 2 * rows and rows & (rows - 1) == 0

    def to_side(array, shift):
        pairs = []
        for r in range(rows):
            for c in range(cols):
                to_row, to_col = (c % rows + shift) % rows, r * ratio + c // rows
                pairs.append((c * rows + r, to_col * rows + to_row))
        return lax.ppermute(array, ("col", "row"), pairs)

    if paired:
        quad, _ = lax.optimization_barrier((panel[0], diagonal_half))
        step = 1
        while step < rows:
            pieces = (quad, lax.ppermute(quad, "col", [(d ^ step, d) for d in range(cols)]))
            step *= 2
            if step == rows:
                pieces, _ = lax.optimization_barrier((pieces, first_lower))
            quad = jnp.concatenate(pieces, axis=0)
        quad = live([col_index ^ p for p in range(rows)], quad)
        group = [quad, lax.ppermute(quad, "col", [(d ^ rows, d) for d in range(cols)])]
        side = to_side(quad, 0)
    else:
        masked = live([col_index], panel[0])
        group = [lax.all_gather(masked, "col", axis=0, tiled=True)]
        side = jnp.concatenate([to_side(masked, s) for s in range(rows)], axis=0)

    own, high, low = pl.pallas_call(
        functools.partial(rest_kernel, "row"),
        out_shape=(
            jax.ShapeDtypeStruct((pivot_size, local_width), jnp.float32),
            jax.ShapeDtypeStruct((pivot_size, pivot_size), jnp.bfloat16),
            jax.ShapeDtypeStruct((pivot_size, pivot_size), jnp.bfloat16),
        ),
        in_specs=[vmem] * (len(pivots) + 2),
        out_specs=(vmem,) * 3,
        scratch_shapes=[
            pltpu.VMEM((rows + 2, pivot_size + 2 * LANES, LANES), jnp.float32),
            pltpu.VMEM((rows, LANES, LANES), jnp.float32),
        ],
        compiler_params=pltpu.CompilerParams(vmem_limit_bytes=32 * 1024 * 1024),
        cost_estimate=pl.CostEstimate(flops=10**9, bytes_accessed=2 * 10**6, transcendentals=10**5),
        name="rest",
    )(*pivots, done, first_lower)

    group_rows = share * cols
    panel_factor, schur = pl.pallas_call(
        functools.partial(solve_kernel, "row", "col", True if paired else None, len(group)),
        out_shape=(
            jax.ShapeDtypeStruct(panel.shape, jnp.bfloat16),
            jax.ShapeDtypeStruct(trailing.shape, jnp.bfloat16),
        ),
        in_specs=[vmem] * (4 + len(group)),
        out_specs=(vmem,) * 2,
        scratch_shapes=[
            pltpu.VMEM((group_rows, pivot_size), jnp.bfloat16),
            pltpu.VMEM((share * rows, pivot_size), jnp.bfloat16),
        ],
        compiler_params=pltpu.CompilerParams(vmem_limit_bytes=48 * 1024 * 1024),
        cost_estimate=pl.CostEstimate(flops=4 * 10**8, bytes_accessed=2 * 10**6, transcendentals=0),
        name="solve",
    )(high, low, *group, side, trailing)
    return (own, panel_factor, schur)


def solution(mesh):
    return jax.shard_map(
        body,
        mesh=mesh,
        in_specs=(P(None, "row"), P("row", "col", None), P("row", None), P("row", "col")),
        out_specs=(P(None, "row"), P("row", "col", None), P("row", "col")),
        check_vma=False,
    )
```
